32 devices in a mesh: shard: 4 (over z), ctx: 4 (over x, core), tp: 2 (over y).
Axes of the slice: x: 2, y: 2, z: 4, core: 2. Of those that a mesh axis runs over, the one named last changes fastest.
Arguments:
- tokens: bfloat16 [2048, 768], P(('shard', 'ctx')), may hold values from -6 to 6
- timesteps: int32 [4, 9], P('shard'), may hold values from 0 to 999
- cont_lengths: int32 [4, 8], P('shard'), may hold values from 1 to 128, 256 in all within a row
- table: bfloat16 [1000, 768], P(None, ('shard', 'ctx')), may hold values from -3 to 3
- w_qkv: bfloat16 [2, 768, 3, 768], P(None, ('shard', 'ctx'), None, 'tp'), may hold values from -0.21875 to 0.21875
- w_out: bfloat16 [2, 768, 768], P(None, ('shard', 'ctx'), 'tp'), may hold values from -2.5 to 2.5
- w_up: bfloat16 [2, 768, 3072], P(None, ('shard', 'ctx'), 'tp'), may hold values from -0.21875 to 0.21875
- w_down: bfloat16 [2, 768, 3072], P(None, ('shard', 'ctx'), 'tp'), may hold values from -0.109375 to 0.109375
- norms: bfloat16 [2, 768, 2], P(None, ('shard', 'ctx')), may hold values from 0.099609375 to 1.8984375
- query_bias: bfloat16 [2, 768], P(None, 'tp'), may hold values from -3 to 3
- value_bias: bfloat16 [2, 768], P(None, 'tp'), may hold values from -0.1796875 to 0.1796875
- up_bias: bfloat16 [2, 3072], P(None, 'tp'), may hold values from -3 to 3
- out_biases: bfloat16 [2, 768, 2], P(None, ('shard', 'ctx')), may hold values from -3 to 3
- cotangent: bfloat16 [2048, 768], P(('shard', 'ctx')), may hold values from -6 to 6
Outputs:
- activations: bfloat16 [2048, 768], P(('shard', 'ctx'))
- grad_tokens: float32 [2048, 768], P(('shard', 'ctx'))
- grad_qkv: float32 [2, 768, 3, 768], P(None, ('shard', 'ctx'), None, 'tp')
- grad_out: float32 [2, 768, 768], P(None, ('shard', 'ctx'), 'tp')
- grad_up: float32 [2, 768, 3072], P(None, ('shard', 'ctx'), 'tp')
- grad_down: float32 [2, 768, 3072], P(None, ('shard', 'ctx'), 'tp')
- grad_norms: float32 [2, 768, 2], P(None, ('shard', 'ctx'))
- grad_table: float32 [1000, 768], P(None, ('shard', 'ctx'))
- grad_query_bias: float32 [2, 768], P(None, 'tp')
- grad_value_bias: float32 [2, 768], P(None, 'tp')
- grad_up_bias: float32 [2, 3072], P(None, 'tp')
- grad_out_biases: float32 [2, 768, 2], P(None, ('shard', 'ctx'))
The draws below stay inside these ranges and needn't reach their ends.
Inputs may be any that keep to these rules, and one draw needn't show every extreme that they name: `cont_lengths`: the lengths of each group sum to half of 512, and the largest of each group is exactly 128.
All inputs are finite; a program needn't handle non-finite values.
Results may differ from the reference program's by a relative error of at most 0.014.
Values may be sent and summed in bfloat16 or wider, within the bound.
No kernel may reach another device: no remote copies, remote signals or barrier semaphores. Data moves between devices by JAX's collectives and lax.ppermute only.
A program may use at most 192 MiB of HBM per device.

```python
import math
import jax
import jax.numpy as jnp
import numpy as np
from jax import lax

D = 768
HEADS = 12
HEAD_DIM = 64
FF = 3072
STEPS = 1000
LAYERS = 2
CONTS = 8
GROUPS = 4
GROUP_TOK = 512
PROMPT = 256
CONT_MAX = 128
SEQS = 9
TOKENS = 2048


def touch_ends(values, own_key, least, largest):
    longest = values.shape.index(max(values.shape))
    spots = []
    for shift in (0, 1):
        where = [jax.random.randint(jax.random.fold_in(own_key, axis), (), 0, length) for axis, length in enumerate(values.shape)]
        where[longest] = (where[longest] + shift) % values.shape[longest]
        spots.append(tuple(where))
    return values.at[spots[0]].set(least).at[spots[1]].set(largest)


def block_scale(stream_key, dims, split, low, largest):
    factor_of, own = 1.0, jax.random.fold_in(stream_key, 6)
    for dim, parts in split:
        draws = jnp.exp(jax.random.uniform(jax.random.fold_in(own, dim), (parts,), jnp.float32, low / len(split), largest / len(split)))
        factor_of = factor_of * jnp.repeat(draws, dims[dim] // parts).reshape([-1 if axis == dim else 1 for axis in range(len(dims))])
    return factor_of


def length_profile(number_of, total, limit, slope):
    portions = [(1 << 20) // math.isqrt(standing ** slope) + 1 for standing in range(2, number_of + 1)]
    spare, given = total - limit - (number_of - 1), [1] * (number_of - 1)
    while spare > 0:
        movable = [i for i in range(number_of - 1) if given[i] < limit]
        whole, remaining = sum([portions[i] for i in movable]), spare
        for i in movable:
            addition = min(limit - given[i], max(1, remaining * portions[i] // whole), spare)
            given[i] = given[i] + addition
            spare = spare - addition
    return np.array([limit] + given)


def ragged_sizes(rng, amount, total, most, slope):
    if amount == 2:
        one = jax.random.randint(rng, (), max(1, total - most), min(most, total - 1) + 1)
        return jnp.stack([one, total - one])
    sizes = jnp.asarray(length_profile(amount, total, most, slope), jnp.int32)
    couples = (amount - 1) // 2
    donor, sink = sizes[1:1 + 2 * couples:2], sizes[2:2 + 2 * couples:2]
    slack = jnp.minimum(donor - 1, most - sink)
    moved = jax.random.randint(jax.random.fold_in(rng, 1), (couples,), 0, 1 << 20) % (slack + 1)
    sizes = sizes.at[1:1 + 2 * couples:2].set(donor - moved).at[2:2 + 2 * couples:2].set(sink + moved)
    return sizes[jax.random.permutation(jax.random.fold_in(rng, 2), amount)]


def bell_draw(rng, extent, scale, bound, pieces=(), kind=jnp.bfloat16):
    gain = block_scale(rng, extent, pieces, -0.22, 0.18) if pieces else 1.0
    values = jax.random.normal(rng, extent, jnp.float32) * scale * gain
    return jnp.minimum(jnp.maximum(values, -bound), bound).astype(kind)


def setup_inputs(seed: int = 0) -> dict:
    key_list = jax.random.split(jax.random.key(seed), 15)
    tokens = bell_draw(key_list[0], (TOKENS, D), 1.0, 6.0, ((0, 16),))
    timesteps = touch_ends(jax.random.randint(key_list[1], (GROUPS, SEQS), 0, STEPS), jax.random.fold_in(key_list[1], 1), 0, STEPS - 1).astype(jnp.int32)
    cont_lengths = jax.vmap(lambda own: ragged_sizes(own, CONTS, GROUP_TOK // 2, CONT_MAX, 2))(jax.random.split(key_list[2], GROUPS)).reshape((GROUPS, CONTS)).astype(jnp.int32)
    table = bell_draw(key_list[3], (STEPS, D), 0.5, 3.0, ((1, 16),))
    w_qkv = bell_draw(key_list[4], (LAYERS, D, 3, D), D ** -0.5, 0.21875, ((1, 16), (3, 2)))
    w_out = bell_draw(key_list[5], (LAYERS, D, D), (max(1, D // (PROMPT // 2))) ** -0.5, 2.5, ((1, 16), (2, 2)))
    w_up = bell_draw(key_list[6], (LAYERS, D, FF), D ** -0.5, 0.21875, ((1, 16), (2, 2)))
    w_down = bell_draw(key_list[7], (LAYERS, D, FF), FF ** -0.5, 0.109375, ((1, 16), (2, 2)))
    norms = jnp.clip(1.0 + 0.18 * jax.random.normal(key_list[8], (LAYERS, D, 2), jnp.float32), 0.099609375, 1.8984375).astype(jnp.bfloat16)
    query_bias = bell_draw(key_list[9], (LAYERS, D), 0.5, 3.0, ((1, 2),))
    value_bias = bell_draw(key_list[10], (LAYERS, D), 0.03, 0.1796875, ((1, 2),))
    up_bias = bell_draw(key_list[11], (LAYERS, FF), 0.5, 3.0, ((1, 2),))
    out_biases = bell_draw(key_list[12], (LAYERS, D, 2), 0.5, 3.0, ((1, 16),))
    cotangent = bell_draw(key_list[13], (TOKENS, D), 1.0, 6.0, ((0, 16),))
    return dict(tokens=tokens, timesteps=timesteps, cont_lengths=cont_lengths, table=table, w_qkv=w_qkv, w_out=w_out, w_up=w_up, w_down=w_down, norms=norms, query_bias=query_bias, value_bias=value_bias, up_bias=up_bias, out_biases=out_biases, cotangent=cotangent)


EPSILON = 1e-05
PRECISE = lax.Precision.HIGHEST

@jax.custom_vjp
def low(v):
    return lax.optimization_barrier(v.astype(jnp.bfloat16)).astype(jnp.float32)

@jax.custom_vjp
def low_back(v):
    return v

def low_keep(v):
    return (low(v), None)

def low_pass(kept, grad):
    return (grad,)

def back_keep(v):
    return (v, None)

def back_low(kept, grad):
    return (low(grad),)
low.defvjp(low_keep, low_pass)
low_back.defvjp(back_keep, back_low)

def layer_norm(values, gain_vec):
    row_mean = lax.optimization_barrier(jnp.mean(values, axis=-1, keepdims=True))
    centered = values - row_mean
    row_var = lax.optimization_barrier(jnp.mean(centered * centered, axis=-1, keepdims=True))
    return centered * lax.rsqrt(row_var + EPSILON) * gain_vec

def group_segments(lengths):
    seq_ends = jnp.cumsum(lengths).astype(jnp.int32)
    position = jnp.arange(GROUP_TOK, dtype=jnp.int32) - PROMPT
    passed = (position[:, None] >= seq_ends[None, :]).astype(jnp.int32)
    seg_ids = 1 + lax.optimization_barrier(jnp.sum(passed, axis=1)).astype(jnp.int32)
    return jnp.where(position < 0, 0, seg_ids).astype(jnp.int32)

def attention(queries, keys, values, seg_ids):
    block_rows = math.gcd(GROUP_TOK, 512)
    query_blocks = queries.reshape(GROUP_TOK // block_rows, block_rows, HEADS, HEAD_DIM)
    seg_blocks = seg_ids.reshape(GROUP_TOK // block_rows, block_rows)
    key_heads = keys.reshape(GROUP_TOK, HEADS, HEAD_DIM)
    value_heads = values.reshape(GROUP_TOK, HEADS, HEAD_DIM)
    score_scale = 1.0 / math.sqrt(HEAD_DIM)

    def one_block(block_pair):
        query_part, seg_query = block_pair
        scores = jnp.einsum('qhd,khd->hqk', query_part, key_heads, precision=PRECISE) * score_scale
        scores = low_back(scores)
        allowed = (seg_ids[None, None, :] == 0) | (seg_ids[None, None, :] == seg_query[None, :, None])
        scores = jnp.where(allowed, scores, -1e+30)
        row_top = lax.optimization_barrier(jnp.max(scores, axis=-1, keepdims=True))
        weights_exp = jnp.exp(scores - row_top)
        attn_prob = low(weights_exp / lax.optimization_barrier(jnp.sum(weights_exp, axis=-1, keepdims=True)))
        return jnp.einsum('hqk,khd->qhd', attn_prob, value_heads, precision=PRECISE)
    result = lax.map(jax.checkpoint(one_block), (query_blocks, seg_blocks))
    return result.reshape(GROUP_TOK, D)

def layer(stream, seg_ids, qkv_w, out_w, up_w, down_w, gain_pair, q_bias, v_bias, u_bias, o_bias):
    normed = low(layer_norm(stream, gain_pair[:, 0]))
    bias_rows = jnp.stack([q_bias, jnp.zeros_like(q_bias), v_bias])
    qkv_raw = low(low_back(jnp.einsum('td,dcn->tcn', normed, qkv_w, precision=PRECISE) + bias_rows[None]))
    attended = low(low_back(attention(qkv_raw[:, 0], qkv_raw[:, 1], qkv_raw[:, 2], seg_ids)))
    stream = stream + low_back(jnp.dot(attended, out_w.T, precision=PRECISE, preferred_element_type=jnp.float32)) + o_bias[:, 0]
    second = low(layer_norm(stream, gain_pair[:, 1]))
    hidden = low_back(jnp.dot(second, up_w, precision=PRECISE, preferred_element_type=jnp.float32) + u_bias)
    gelu_out = low(jax.nn.gelu(hidden, approximate=False))
    return stream + low_back(jnp.dot(gelu_out, down_w.T, precision=PRECISE, preferred_element_type=jnp.float32)) + o_bias[:, 1]

def reference(tokens, timesteps, cont_lengths, table, w_qkv, w_out, w_up, w_down, norms, query_bias, value_bias, up_bias, out_biases, cotangent):
    floats = tuple((entry.astype(jnp.float32) for entry in (tokens, table, w_qkv, w_out, w_up, w_down, norms, query_bias, value_bias, up_bias, out_biases)))

    def forward(tokens_f, table_f, qkv_f, out_f, up_f, down_f, norms_f, qb_f, vb_f, ub_f, ob_f):

        def one_group(group_pack):
            group_tokens, steps_row, length_row = group_pack
            seg_ids = group_segments(length_row)
            stream = group_tokens + jnp.take(table_f, jnp.take(steps_row, seg_ids, axis=0), axis=0)
            for layer_index in range(LAYERS):
                stream = layer(stream, seg_ids, qkv_f[layer_index], out_f[layer_index], up_f[layer_index], down_f[layer_index], norms_f[layer_index], qb_f[layer_index], vb_f[layer_index], ub_f[layer_index], ob_f[layer_index])
            return stream
        result = lax.map(one_group, (tokens_f.reshape(GROUPS, GROUP_TOK, D), timesteps, cont_lengths))
        return result.reshape(TOKENS, D)
    result, pullback = jax.vjp(forward, *floats)
    gradients = pullback(cotangent.astype(jnp.float32))
    return (result.astype(jnp.bfloat16), gradients[0], gradients[2], gradients[3], gradients[4], gradients[5], gradients[6], gradients[1], gradients[7], gradients[8], gradients[9], gradients[10])
```

```python
import functools
import math

import jax
import jax.numpy as jnp
from jax import lax
from jax.experimental import pallas as pl
from jax.experimental.pallas import tpu as pltpu
from jax.sharding import PartitionSpec as P

HEAD_DIM = 64
EPSILON = 1e-05
NEGATIVE = -1e30
F32 = jnp.float32
BF16 = jnp.bfloat16
LANES = 128
CHUNK = 512
VMEM_LIMIT = 40 * 1024 * 1024
ORDER = (0, 2, 1, 3)


def nn(a, b):
    return lax.dot_general(a, b, (((1,), (0,)), ((), ())), preferred_element_type=F32)


def nt(a, b):
    return lax.dot_general(a, b, (((1,), (1,)), ((), ())), preferred_element_type=F32)


def tn(a, b):
    return lax.dot_general(a, b, (((0,), (0,)), ((), ())), preferred_element_type=F32)


def normed_rows(values):
    centered = values - jnp.mean(values, axis=-1, keepdims=True)
    scale = lax.rsqrt(jnp.mean(centered * centered, axis=-1, keepdims=True) + EPSILON)
    return centered * scale, scale


def norm_back(values, gain, grad):
    hat, scale = normed_rows(values)
    grad_gain = jnp.sum(grad * hat, axis=0, keepdims=True)
    inner = grad * gain
    along = jnp.mean(inner * hat, axis=-1, keepdims=True)
    centre = jnp.mean(inner, axis=-1, keepdims=True)
    return scale * (inner - centre - hat * along), grad_gain


def rows_of(parts, count, width):
    have = len(parts)
    if have < count:
        parts = list(parts) + [jnp.zeros((count - have, width), F32)]
    return jnp.concatenate(parts, axis=0)


class Plan:
    def __init__(self, rows, width, block, heads_width, hidden, shards, contexts, conts):
        self.rows, self.width, self.block = rows, width, block
        self.heads_width, self.hidden = heads_width, hidden
        self.shards, self.contexts, self.conts = shards, contexts, conts
        self.group = rows * contexts
        self.blocks = contexts == 4 and block % 16 == 0


def run(plan, body, name, meta, inputs, weights, outs, flops, scratch=(), direct=()):
    n_in, n_out = len(inputs), len(outs)
    counts = [len(arrays) for arrays, _, _ in weights]
    per_block = plan.shards * len(ORDER)
    copies = sum(1 if n == 1 else per_block for n in counts)

    def kernel(meta_ref, *refs):
        ins = refs[:n_in]
        at = n_in
        sources = []
        for n in counts:
            sources.append(refs[at : at + n])
            at += n
        results = refs[at : at + n_out]
        at += n_out
        held = refs[at : at + len(weights)]
        at += len(weights)
        sems = refs[at] if weights else None
        own = refs[at + 1 :] if weights else refs[at:]
        started, slot = [], 0
        for (_, column, width), refs_of, into in zip(weights, sources, held):
            group = []
            columns = pl.ds(column, width)
            if len(refs_of) == 1:
                group.append(pltpu.make_async_copy(refs_of[0].at[:, columns], into, sems.at[slot]))
                slot += 1
            else:
                for ref, offset in zip(refs_of, ORDER):
                    for shift in range(plan.shards):
                        z = lax.rem(meta_ref[0] + (plan.shards - shift), plan.shards)
                        index = z * plan.contexts + jnp.bitwise_xor(meta_ref[1], offset)
                        row = pl.multiple_of(index * plan.block, 16)
                        group.append(
                            pltpu.make_async_copy(
                                ref.at[shift, :, columns],
                                into.at[pl.ds(row, plan.block), :],
                                sems.at[slot],
                            )
                        )
                        slot += 1
            for copy in group:
                copy.start()
            started.append(group)

        def weight(i):
            for copy in started[i]:
                copy.wait()
            return held[i]

        body(meta_ref, ins, weight, results, own)

    vmem = pl.BlockSpec(memory_space=pltpu.VMEM)
    anywhere = pl.BlockSpec(memory_space=pl.ANY)
    scratch_shapes = [pltpu.VMEM((plan.width, width), BF16) for _, _, width in weights]
    if weights:
        scratch_shapes.append(pltpu.SemaphoreType.DMA((copies,)))
    moved = sum(x.size * x.dtype.itemsize for x in inputs)
    moved += sum(math.prod(o.shape) * o.dtype.itemsize for o in outs)
    moved += sum(plan.width * width * 2 for _, _, width in weights)
    return pl.pallas_call(
        kernel,
        name=name,
        out_shape=tuple(outs),
        in_specs=[pl.BlockSpec(memory_space=pltpu.SMEM)]
        + [vmem] * n_in
        + [anywhere] * sum(counts),
        out_specs=tuple(anywhere if i in direct else vmem for i in range(n_out)),
        scratch_shapes=scratch_shapes + list(scratch),
        compiler_params=pltpu.CompilerParams(vmem_limit_bytes=VMEM_LIMIT),
        cost_estimate=pl.CostEstimate(flops=flops, bytes_accessed=moved, transcendentals=0),
    )(meta, *inputs, *[array for arrays, _, _ in weights for array in arrays])


def shape(*dims, dtype=BF16):
    return jax.ShapeDtypeStruct(dims, dtype)


def segment(plan, meta, position):
    prompt = plan.group // 2
    seg = jnp.ones(position.shape, jnp.int32)
    for j in range(plan.conts):
        seg = seg + (position - prompt >= meta[2 + j]).astype(jnp.int32)
    return jnp.where(position < prompt, 0, seg)


def key_positions(plan, meta):
    if not plan.blocks:
        return lax.broadcasted_iota(jnp.int32, (plan.group, 1), 0)
    inside = lax.broadcasted_iota(jnp.int32, (plan.rows, 1), 0)
    return jnp.concatenate(
        [inside + jnp.bitwise_xor(meta[1], d) * plan.rows for d in ORDER], axis=0
    )


def allowed_keys(plan, meta):
    lane = lax.broadcasted_iota(jnp.int32, (1, 2 * plan.rows), 1)
    query = meta[1] * plan.rows + jnp.where(lane >= plan.rows, lane - plan.rows, lane)
    seg_query = segment(plan, meta, query)
    seg_key = segment(plan, meta, key_positions(plan, meta))
    return (seg_key == 0) | (seg_key == seg_query)


def pair_rows(values):
    first = lax.broadcasted_iota(jnp.int32, values.shape, 1) < HEAD_DIM
    none = jnp.zeros_like(values)
    return jnp.concatenate([jnp.where(first, values, none), jnp.where(first, none, values)], axis=0)


def pair_lanes(values):
    rows = values.shape[0] // 2
    first = lax.broadcasted_iota(jnp.int32, (rows, LANES), 1) < HEAD_DIM
    return jnp.where(first, values[:rows], values[rows:])


def write_qkv(plan, layer, x, gain, weight, q_bias, v_bias, a_ref, q_ref, kv_ref):
    n = plan.heads_width
    hat, _ = normed_rows(x)
    a = (hat * gain).astype(BF16)
    a_ref[...] = a
    bias_q = q_bias[...].astype(F32)[layer : layer + 1]
    bias_v = v_bias[...].astype(F32)[layer : layer + 1]
    kv_ref[:, :n] = nn(a, weight[:, n : 2 * n]).astype(BF16)
    kv_ref[:, n:] = (nn(a, weight[:, 2 * n :]) + bias_v).astype(BF16)
    q_ref[...] = (nn(a, weight[:, :n]) + bias_q).astype(BF16)


def embed_body(plan, meta, ins, weight, outs, own):
    tokens, q_bias, v_bias = ins
    x_ref, vec_ref, a_ref, q_ref, kv_ref = outs
    small = weight(1)[...].astype(F32).T
    vec_ref[...] = small[:8]
    lookup = small[8:24].astype(BF16)
    inside = lax.broadcasted_iota(jnp.int32, (plan.rows, 1), 0)
    seg = segment(plan, meta, meta[1] * plan.rows + inside)
    member = seg == lax.broadcasted_iota(jnp.int32, (plan.rows, 16), 1)
    x = tokens[...].astype(F32) + nn(member.astype(F32).astype(BF16), lookup)
    x_ref[...] = x
    write_qkv(plan, 0, x, small[:1], weight(0), q_bias, v_bias, a_ref, q_ref, kv_ref)


def next_body(plan, layer, meta, ins, weight, outs, own):
    x_mid, part, part_far, vec, q_bias, v_bias = ins
    x_ref, a_ref, q_ref, kv_ref = outs
    x = x_mid[...] + (part[...].astype(F32) + part_far[...].astype(F32))
    x = x + vec[2 * layer + 3 : 2 * layer + 4, :]
    x_ref[...] = x
    gain = vec[2 * layer : 2 * layer + 1, :]
    write_qkv(plan, layer, x, gain, weight(0), q_bias, v_bias, a_ref, q_ref, kv_ref)


def attend_body(plan, meta, ins, weight, outs, own):
    q_ref, kvs = ins[0], ins[1:]
    part_ref, o_ref, total_ref = outs
    n = plan.heads_width
    allowed = allowed_keys(plan, meta)
    totals = []
    for pair in range(n // LANES):
        lanes = slice(pair * LANES, (pair + 1) * LANES)
        late = slice(n + pair * LANES, n + (pair + 1) * LANES)
        q2 = pair_rows(q_ref[:, lanes])
        keys = jnp.concatenate([kv[:, lanes] for kv in kvs], axis=0)
        values = jnp.concatenate([kv[:, late] for kv in kvs], axis=0)
        scores = jnp.where(allowed, nt(keys, q2) * (1.0 / math.sqrt(HEAD_DIM)), NEGATIVE)
        top = jnp.max(scores, axis=0, keepdims=True)
        exps = jnp.exp(scores - top)
        total = jnp.sum(exps, axis=0, keepdims=True)
        prob = (exps * (1.0 / total)).astype(BF16)
        o_ref[:, lanes] = pair_lanes(tn(prob, values)).astype(BF16)
        totals.append(top + jnp.log(total))
    total_ref[...] = rows_of(totals, 8, 2 * plan.rows)
    part_ref[...] = nt(o_ref[...], weight(0)[...]).astype(BF16)


def feed_body(plan, layer, last, meta, ins, weight, outs, own):
    x, part, part_far, vec, bias = ins[:5]
    mid_ref, b_ref, gelu_ref, slope_ref, part_ref = outs[:5]
    x_mid = x[...] + (part[...].astype(F32) + part_far[...].astype(F32))
    x_mid = x_mid + vec[2 * layer + 4 : 2 * layer + 5, :]
    mid_ref[...] = x_mid
    hat, _ = normed_rows(x_mid)
    b = (hat * vec[2 * layer + 1 : 2 * layer + 2, :]).astype(BF16)
    b_ref[...] = b
    bias_f = bias[...].astype(F32)[layer : layer + 1]
    up = weight(0)
    chunks = [slice(i, min(i + CHUNK, plan.hidden)) for i in range(0, plan.hidden, CHUNK)]
    for columns in chunks:
        hidden = nn(b, up[:, columns]) + bias_f[:, columns]
        half = 0.5 * (1.0 + lax.erf(hidden * math.sqrt(0.5)))
        gelu_ref[:, columns] = (hidden * half).astype(BF16)
        bell = jnp.exp(hidden * hidden * -0.5) * (1.0 / math.sqrt(2.0 * math.pi))
        slope_ref[:, columns] = half + hidden * bell
    down = weight(1)
    if last:
        back_feed(plan, ins[5][...], slope_ref, up, down, outs[5], outs[6], outs[7], ins[5][...].astype(F32), None)
    part_ref[...] = nt(gelu_ref[...], down[...]).astype(BF16)


def back_feed(plan, dy, slope, up, down, dh_ref, db_ref, sum_ref, gradient, extra):
    sums = []
    total = None
    for i in range(0, plan.hidden, CHUNK):
        columns = slice(i, min(i + CHUNK, plan.hidden))
        dh = (nn(dy, down[:, columns]) * slope[:, columns]).astype(BF16)
        dh_ref[:, columns] = dh
        sums.append(jnp.sum(dh.astype(F32), axis=0, keepdims=True))
        term = nt(dh, up[:, columns])
        total = term if total is None else total + term
    db_ref[...] = total.astype(BF16)
    bias_sum = jnp.concatenate(sums, axis=1)
    parts = [jnp.sum(gradient, axis=0, keepdims=True)]
    for i in range(plan.hidden // plan.width):
        parts.append(bias_sum[:, i * plan.width : (i + 1) * plan.width])
    if extra is not None:
        parts.append(extra)
    sum_ref[...] = rows_of(parts, 8, plan.width)


def between_body(plan, layer, meta, ins, weight, outs, own):
    dx_mid, x_above, da, da_far, vec, slope = ins
    gy_ref, dy_ref, dh_ref, db_ref, sum_ref = outs
    grad = da[...].astype(F32) + da_far[...].astype(F32)
    back, gain_sum = norm_back(x_above[...], vec[2 * layer + 2 : 2 * layer + 3, :], grad)
    gy = dx_mid[...] + back
    gy_ref[...] = gy
    dy = gy.astype(BF16)
    dy_ref[...] = dy
    back_feed(plan, dy, slope, weight(0), weight(1), dh_ref, db_ref, sum_ref, gy, gain_sum)


def attend_back_body(plan, layer, meta, ins, weight, outs, own):
    gy, x_mid, db, db_far, vec, q_ref, total = ins[:7]
    kvs = ins[7:]
    mid_ref, dz_ref, dq_ref, sum_ref = outs[:4]
    dkv = outs[4:]
    n = plan.heads_width
    scale = 1.0 / math.sqrt(HEAD_DIM)
    grad = db[...].astype(F32) + db_far[...].astype(F32)
    back, gain_sum = norm_back(x_mid[...], vec[2 * layer + 1 : 2 * layer + 2, :], grad)
    dx_mid = gy[...].astype(F32) + back
    mid_ref[...] = dx_mid
    sum_ref[...] = rows_of([gain_sum, jnp.sum(dx_mid, axis=0, keepdims=True)], 8, plan.width)
    dz = dx_mid.astype(BF16)
    dz_ref[...] = dz
    do = nn(dz, weight(0)[...]).astype(BF16)
    allowed = allowed_keys(plan, meta)
    each = plan.group // len(dkv)
    for pair in range(n // LANES):
        lanes = slice(pair * LANES, (pair + 1) * LANES)
        late = slice(n + pair * LANES, n + (pair + 1) * LANES)
        q2 = pair_rows(q_ref[:, lanes])
        do2 = pair_rows(do[:, lanes])
        keys = jnp.concatenate([kv[:, lanes] for kv in kvs], axis=0)
        values = jnp.concatenate([kv[:, late] for kv in kvs], axis=0)
        prob = jnp.exp(nt(keys, q2) * scale - total[pair : pair + 1, :])
        prob = jnp.where(allowed, prob, 0.0)
        dprob = nt(values, do2)
        delta = jnp.sum(prob * dprob, axis=0, keepdims=True)
        dscore = (prob * (dprob - delta)).astype(BF16)
        dq_ref[:, lanes] = (pair_lanes(tn(dscore, keys)) * scale).astype(BF16)
        dk = (nn(dscore, q2) * scale).astype(BF16)
        dv = nn(prob.astype(BF16), do2).astype(BF16)
        for i, ref in enumerate(dkv):
            ref[:, lanes] = dk[i * each : (i + 1) * each]
            ref[:, late] = dv[i * each : (i + 1) * each]


def project_back_body(plan, meta, ins, weight, outs, own):
    dq = ins[0]
    dqkv_ref, da_ref, sum_ref = outs
    n = plan.heads_width
    dkv = ins[1][: plan.rows].astype(F32)
    for term in ins[2:]:
        dkv = dkv + term[: plan.rows].astype(F32)
    dkv = dkv.astype(BF16)
    dqkv_ref[:, :n] = dq[...]
    dqkv_ref[:, n:] = dkv
    da_ref[...] = nt(dqkv_ref[...], weight(0)[...]).astype(BF16)
    sums = [
        jnp.sum(dq[...].astype(F32), axis=0, keepdims=True),
        jnp.sum(dkv[:, n:].astype(F32), axis=0, keepdims=True),
    ]
    sum_ref[...] = rows_of([jnp.concatenate(sums, axis=1)], 8, 2 * n)


def weight_grad_body(plan, widths, meta, ins, weight, outs, own):
    packet, sems = own
    column = 0
    for i, width in enumerate(widths):
        left, right = ins[2 * i], ins[2 * i + 1]
        for j in range(0, width, CHUNK):
            size = min(CHUNK, width - j)
            value = tn(left[...], right[:, j : j + size])
            packet[:, column : column + size] = value.astype(BF16)
            column += size
    if not plan.blocks:
        copies = [pltpu.make_async_copy(packet, outs[0], sems.at[0])]
    else:
        copies = []
        for place, offset in enumerate(ORDER):
            for shift in range(plan.shards):
                z = lax.rem(meta[0] + shift, plan.shards)
                index = z * plan.contexts + jnp.bitwise_xor(meta[1], offset)
                row = pl.multiple_of(index * plan.block, 16)
                copies.append(
                    pltpu.make_async_copy(
                        packet.at[pl.ds(row, plan.block), :],
                        outs[place // 2].at[place % 2, shift],
                        sems.at[place * plan.shards + shift],
                    )
                )
    for copy in copies:
        copy.start()
    for copy in copies:
        copy.wait()


def end_body(plan, meta, ins, weight, outs, own):
    dx_mid, x, da, da_far, vec = ins[:5]
    feed0, attn0, proj0, feed1, attn1, proj1 = ins[5:]
    gy_ref, small_ref = outs
    grad = da[...].astype(F32) + da_far[...].astype(F32)
    back, gain_sum = norm_back(x[...], vec[:1, :], grad)
    gy = dx_mid[...] + back
    gy_ref[...] = gy
    lane = lax.broadcasted_iota(jnp.int32, (1, plan.rows), 1)
    seg = segment(plan, meta, meta[1] * plan.rows + lane)
    member = (seg == lax.broadcasted_iota(jnp.int32, (16, plan.rows), 0)).astype(F32)
    sums = lax.dot_general(
        member, gy, (((1,), (0,)), ((), ())), precision=lax.Precision.HIGHEST, preferred_element_type=F32
    )
    halves = plan.hidden // plan.width
    parts = [sums]
    for gain_row, feed, attn, proj in (
        (gain_sum, feed0, attn0, proj0),
        (feed0[1 + halves : 2 + halves, :], feed1, attn1, proj1),
    ):
        parts += [gain_row, attn[0:1, :], attn[1:2, :], feed[0:1, :]]
        parts += [feed[1 + i : 2 + i, :] for i in range(halves)]
        parts += [proj[0:1, :]]
    small_ref[...] = rows_of_total(parts, 32, plan.width).astype(BF16)


def rows_of_total(parts, count, width):
    have = sum(part.shape[0] for part in parts)
    return jnp.concatenate(parts + [jnp.zeros((count - have, width), F32)], axis=0)


def swap_core(array):
    return lax.ppermute(array, "ctx", [(i, i ^ 1) for i in range(4)])


def swap_chip(array):
    return lax.ppermute(array, "ctx", [(i, i ^ 2) for i in range(4)])


def swap_tp(array):
    return lax.ppermute(array, "tp", [(0, 1), (1, 0)])


def to_shard(plan, array, shift):
    n = plan.shards
    return lax.ppermute(array, "shard", [(i, (i + shift) % n) for i in range(n)])


def along_shard(plan, pieces):
    got = [pieces[0]] + [to_shard(plan, pieces[k], k) for k in range(1, plan.shards)]
    return jnp.stack(got)


def across_chip(stack):
    far = swap_chip(stack)
    return (stack, far, swap_core(stack), swap_core(far))


def gather_rows(plan, packet):
    if plan.blocks:
        return across_chip(along_shard(plan, [packet] * plan.shards))
    return (lax.all_gather(packet, ("shard", "ctx"), axis=0, tiled=True),)


def gather_keys(plan, kv):
    if plan.blocks:
        far = swap_chip(kv)
        return (kv, far, swap_core(kv), swap_core(far))
    return (lax.all_gather(kv, "ctx", axis=0, tiled=True),)


def add(*terms):
    total = terms[0].astype(F32)
    for term in terms[1:]:
        total = total + term.astype(F32)
    return total


def weight_grad(plan, meta, name, pairs):
    widths = tuple(right.shape[1] for _, right in pairs)
    width = sum(widths)
    if plan.blocks:
        part = shape(2, plan.shards, plan.block, width)
        outs, copies = [part, part], plan.shards * 4
    else:
        outs, copies = [shape(plan.width, width)], 1
    parts = run(
        plan,
        functools.partial(weight_grad_body, plan, widths),
        name,
        meta,
        [array for pair in pairs for array in pair],
        [],
        outs,
        2 * plan.rows * plan.width * width,
        scratch=[pltpu.VMEM((plan.width, width), BF16), pltpu.SemaphoreType.DMA((copies,))],
        direct=tuple(range(len(outs))),
    )
    if not plan.blocks:
        return lax.psum_scatter(parts[0], ("shard", "ctx"), scatter_dimension=0, tiled=True).astype(F32)
    keep, send = parts
    near = swap_core(send)
    far = swap_chip(add(keep[1], near[1]).astype(BF16))
    sums = [add(keep[0, k], near[0, k], far[k]) for k in range(plan.shards)]
    got = [to_shard(plan, sums[k].astype(BF16), k) for k in range(1, plan.shards)]
    return add(sums[0], *got)


def per_device(
    tokens,
    timesteps,
    cont_lengths,
    table,
    w_qkv,
    w_out,
    w_up,
    w_down,
    norms,
    query_bias,
    value_bias,
    up_bias,
    out_biases,
    cotangent,
):
    rows, width = tokens.shape
    layers, block = w_qkv.shape[:2]
    heads_width, hidden = w_qkv.shape[3], w_up.shape[2]
    shards, contexts = lax.axis_size("shard"), lax.axis_size("ctx")
    conts = cont_lengths.shape[1]
    plan = Plan(rows, width, block, heads_width, hidden, shards, contexts, conts)
    z, c = lax.axis_index("shard"), lax.axis_index("ctx")
    meta = jnp.concatenate([jnp.stack([z, c]).astype(jnp.int32), jnp.cumsum(cont_lengths[0])])

    vectors = jnp.concatenate(
        [norms[0], norms[1], out_biases[0], out_biases[1]], axis=1
    )
    seqs = conts + 1
    steps_all = lax.all_gather(timesteps, "shard", axis=0, tiled=True)
    steps_near = jnp.roll(steps_all, -z, axis=0).reshape(-1)
    one_hot = (steps_near[:, None] == jnp.arange(table.shape[0], dtype=jnp.int32)[None, :]).astype(BF16)
    looked = lax.dot_general(
        table, one_hot, (((0,), (1,)), ((), ())), preferred_element_type=F32
    ).astype(BF16)
    blank = jnp.zeros((block, LANES - vectors.shape[1] - seqs), BF16)
    if plan.blocks:
        small = along_shard(
            plan,
            [
                jnp.concatenate([vectors, looked[:, k * seqs : (k + 1) * seqs], blank], axis=1)
                for k in range(shards)
            ],
        )
        first = along_shard(plan, [w_qkv[0].reshape(block, -1)] * shards)
        first = across_chip(jnp.concatenate([first, small], axis=2))
        small_of = (first, 3 * heads_width, LANES)
    else:
        looked = jnp.roll(looked.reshape(block, shards, seqs), z, axis=1).reshape(block, -1)
        every = lax.all_gather(jnp.concatenate([vectors, looked], axis=1), ("shard", "ctx"), axis=0, tiled=True)
        mine = lax.dynamic_slice_in_dim(every, 8 + z * seqs, seqs, axis=1)
        blank = jnp.zeros((width, LANES - 8 - seqs), BF16)
        small_of = ((jnp.concatenate([every[:, :8], mine, blank], axis=1),), 0, LANES)
        first = gather_rows(plan, w_qkv[0].reshape(block, -1))
    n3 = 3 * heads_width
    second = gather_rows(plan, jnp.concatenate([w_out[0], w_up[0]], axis=1))
    third = gather_rows(plan, w_down[0])
    fourth = gather_rows(plan, jnp.concatenate([w_qkv[1].reshape(block, -1), w_out[1]], axis=1))
    fifth = gather_rows(plan, jnp.concatenate([w_up[1], w_down[1]], axis=1))
    of_qkv = [(first, 0, n3), (fourth, 0, n3)]
    of_out = [(second, 0, heads_width), (fourth, n3, heads_width)]
    of_up = [(second, heads_width, hidden), (fifth, 0, hidden)]
    of_down = [(third, 0, hidden), (fifth, hidden, hidden)]

    mm = 2 * rows * width
    full = shape(rows, width, dtype=F32)
    low = shape(rows, width)
    heads = shape(rows, heads_width)
    wide = shape(rows, hidden)
    sums = shape(8, width, dtype=F32)
    qkv_outs = [low, heads, shape(rows, 2 * heads_width)]
    attn_flops = 4 * rows * plan.group * heads_width

    saved = []
    x_mid = part = part_far = None
    for layer in range(layers):
        if layer == 0:
            x, vec, a, q, kv = run(
                plan,
                functools.partial(embed_body, plan),
                "embed",
                meta,
                [tokens, query_bias, value_bias],
                [of_qkv[0], small_of],
                [full, sums, *qkv_outs],
                mm * n3,
            )
        else:
            x, a, q, kv = run(
                plan,
                functools.partial(next_body, plan, layer),
                "project",
                meta,
                [x_mid, part, part_far, vec, query_bias, value_bias],
                [of_qkv[layer]],
                [full, *qkv_outs],
                mm * n3,
            )
        kvs = gather_keys(plan, kv)
        part, o, total = run(
            plan,
            functools.partial(attend_body, plan),
            "attend",
            meta,
            [q, *kvs],
            [of_out[layer]],
            [low, heads, shape(8, 2 * rows, dtype=F32)],
            mm * heads_width + attn_flops,
        )
        part_far = swap_tp(part)
        last = layer == layers - 1
        outs = [full, low, wide, shape(rows, hidden, dtype=F32), low]
        if last:
            outs += [wide, low, sums]
        got = run(
            plan,
            functools.partial(feed_body, plan, layer, last),
            "feed",
            meta,
            [x, part, part_far, vec, up_bias] + ([cotangent] if last else []),
            [of_up[layer], of_down[layer]],
            outs,
            mm * hidden * (4 if last else 2),
        )
        x_mid, b, gelu, slope, part = got[:5]
        part_far = swap_tp(part)
        saved.append((x, a, q, kvs, o, total, x_mid, b, gelu, slope))

    bias_last = vec[2 * layers + 3][None, :]
    activations = (x_mid + add(part, part_far) + bias_last).astype(BF16)

    gy = dy = cotangent
    dh, db, feed_sum = got[5:]
    grads, small_sums = [None] * layers, [None] * layers
    for layer in reversed(range(layers)):
        x, a, q, kvs, o, total, x_mid, b, gelu, slope = saved[layer]
        if layer < layers - 1:
            gy, dy, dh, db, feed_sum = run(
                plan,
                functools.partial(between_body, plan, layer),
                "feed_back",
                meta,
                [dx_mid, saved[layer + 1][0], da, da_far, vec, slope],
                [of_up[layer], of_down[layer]],
                [full, low, wide, low, sums],
                2 * mm * hidden,
            )
        db_far = swap_tp(db)
        feed_grad = weight_grad(plan, meta, "feed_grad", [(b, dh), (dy, gelu)])
        if plan.blocks:
            dkv_outs = [shape(2 * rows, 2 * heads_width)] * 2
        else:
            dkv_outs = [shape(plan.group, 2 * heads_width)]
        dx_mid, dz, dq, attn_sum, *dkv = run(
            plan,
            functools.partial(attend_back_body, plan, layer),
            "attend_back",
            meta,
            [gy, x_mid, db, db_far, vec, q, total, *kvs],
            [of_out[layer]],
            [full, low, heads, sums, *dkv_outs],
            mm * heads_width + 10 * rows * plan.group * heads_width,
        )
        if plan.blocks:
            keep, send = dkv
            near = swap_core(send)
            far = swap_chip(add(keep[rows:], near[rows:]).astype(BF16))
            terms = [keep, near, far]
        else:
            terms = [lax.psum_scatter(dkv[0], "ctx", scatter_dimension=0, tiled=True)]
        dqkv, da, proj_sum = run(
            plan,
            functools.partial(project_back_body, plan),
            "project_back",
            meta,
            [dq, *terms],
            [of_qkv[layer]],
            [shape(rows, n3), low, shape(8, 2 * heads_width, dtype=F32)],
            mm * n3,
        )
        da_far = swap_tp(da)
        attn_grad = weight_grad(plan, meta, "attn_grad", [(a, dqkv), (dz, o)])
        grads[layer] = (feed_grad, attn_grad)
        small_sums[layer] = [feed_sum, attn_sum, proj_sum]

    grad_tokens, packet = run(
        plan,
        functools.partial(end_body, plan),
        "end",
        meta,
        [dx_mid, saved[0][0], da, da_far, vec, *small_sums[0], *small_sums[1]],
        [],
        [full, shape(32, width)],
        mm * 32,
    )
    start = (z * contexts + c) * block
    if plan.blocks:
        packet = add(packet, swap_core(packet)).astype(BF16)
        packet = add(packet, swap_chip(packet)).astype(BF16)
        got = along_shard(plan, [packet] * shards)
        other = add(*[got[k] for k in range(0, shards, 2)]) + add(*[got[k] for k in range(1, shards, 2)])
        steps_back = jnp.roll(steps_all[::-1], z + 1, axis=0)
    else:
        packet = lax.psum(packet, "ctx")
        got = lax.all_gather(packet, "shard", axis=0)
        other = jnp.sum(got.astype(F32), axis=0)
        steps_back = steps_all
    mine = lax.dynamic_slice_in_dim(got[:, :seqs], start, block, axis=2).reshape(-1, block)
    one_hot = (jnp.arange(table.shape[0], dtype=jnp.int32)[:, None] == steps_back.reshape(-1)[None, :]).astype(BF16)
    grad_table = jnp.dot(one_hot, mine, preferred_element_type=F32)

    halves = hidden // width
    per_layer = 5 + halves
    by_layer = other[16 : 16 + layers * per_layer].reshape(layers, per_layer, width)
    local = lax.dynamic_slice_in_dim(by_layer[:, :4], start, block, axis=2)
    grad_norms = jnp.moveaxis(local[:, :2], 1, 2)
    grad_out_biases = jnp.moveaxis(local[:, 2:], 1, 2)
    grad_up_bias = by_layer[:, 4 : 4 + halves].reshape(layers, hidden)
    grad_query_bias = by_layer[:, 4 + halves, :heads_width]
    grad_value_bias = by_layer[:, 4 + halves, heads_width:]
    feeds = [grads[layer][0] for layer in range(layers)]
    attns = [grads[layer][1] for layer in range(layers)]
    return (
        activations,
        grad_tokens,
        jnp.stack([g[:, :n3].reshape(block, 3, heads_width) for g in attns]),
        jnp.stack([g[:, n3:] for g in attns]),
        jnp.stack([g[:, :hidden] for g in feeds]),
        jnp.stack([g[:, hidden:] for g in feeds]),
        grad_norms,
        grad_table,
        grad_query_bias,
        grad_value_bias,
        grad_up_bias,
        grad_out_biases,
    )


def solution(mesh):
    placed = (
        P(("shard", "ctx"), None),
        P("shard", None),
        P("shard", None),
        P(None, ("shard", "ctx")),
        P(None, ("shard", "ctx"), None, "tp"),
        P(None, ("shard", "ctx"), "tp"),
        P(None, ("shard", "ctx"), "tp"),
        P(None, ("shard", "ctx"), "tp"),
        P(None, ("shard", "ctx"), None),
        P(None, "tp"),
        P(None, "tp"),
        P(None, "tp"),
        P(None, ("shard", "ctx"), None),
        P(("shard", "ctx"), None),
    )
    return jax.shard_map(
        per_device,
        mesh=mesh,
        in_specs=placed,
        out_specs=(
            P(("shard", "ctx"), None),
            P(("shard", "ctx"), None),
            P(None, ("shard", "ctx"), None, "tp"),
            P(None, ("shard", "ctx"), "tp"),
            P(None, ("shard", "ctx"), "tp"),
            P(None, ("shard", "ctx"), "tp"),
            P(None, ("shard", "ctx"), None),
            P(None, ("shard", "ctx")),
            P(None, "tp"),
            P(None, "tp"),
            P(None, "tp"),
            P(None, ("shard", "ctx"), None),
        ),
        check_vma=False,
    )
```

```python
import functools
import math

import jax
import jax.numpy as jnp
from jax import lax
from jax.experimental import pallas as pl
from jax.experimental.pallas import tpu as pltpu
from jax.sharding import PartitionSpec as P

HEAD_DIM = 64
EPSILON = 1e-05
NEGATIVE = -1e30
F32 = jnp.float32
BF16 = jnp.bfloat16
LANES = 128
CHUNK = 512
SPLIT = 3
VMEM_LIMIT = 46 * 1024 * 1024
ORDER = (0, 2, 1, 3)


def nn(a, b):
    return lax.dot_general(a, b, (((1,), (0,)), ((), ())), preferred_element_type=F32)


def nt(a, b):
    return lax.dot_general(a, b, (((1,), (1,)), ((), ())), preferred_element_type=F32)


def tn(a, b):
    return lax.dot_general(a, b, (((0,), (0,)), ((), ())), preferred_element_type=F32)


def normed_rows(values):
    centered = values - jnp.mean(values, axis=-1, keepdims=True)
    scale = lax.rsqrt(jnp.mean(centered * centered, axis=-1, keepdims=True) + EPSILON)
    return centered * scale, scale


def norm_back(values, gain, grad):
    hat, scale = normed_rows(values)
    grad_gain = jnp.sum(grad * hat, axis=0, keepdims=True)
    inner = grad * gain
    along = jnp.mean(inner * hat, axis=-1, keepdims=True)
    centre = jnp.mean(inner, axis=-1, keepdims=True)
    return scale * (inner - centre - hat * along), grad_gain


def rows_of(parts, count, width):
    have = len(parts)
    if have < count:
        parts = list(parts) + [jnp.zeros((count - have, width), F32)]
    return jnp.concatenate(parts, axis=0)


class Plan:
    def __init__(self, rows, width, block, heads_width, hidden, shards, contexts, conts):
        self.rows, self.width, self.block = rows, width, block
        self.heads_width, self.hidden = heads_width, hidden
        self.shards, self.contexts, self.conts = shards, contexts, conts
        self.group = rows * contexts
        self.blocks = contexts == 4 and block % 16 == 0


def run(plan, body, name, meta, inputs, weights, outs, flops, scratch=(), direct=(), ties=(), kept=()):
    if ties:
        inputs = [after(inputs[0], *ties), *inputs[1:]]
    n_in, n_out = len(inputs), len(outs)
    counts = [len(entry[0]) for entry in weights]
    per_block = plan.shards * len(ORDER) * SPLIT
    copies = sum(1 if n == 1 else per_block for n in counts) + len(kept)

    def kernel(meta_ref, *refs):
        ins = refs[:n_in]
        at = n_in
        sources = []
        for n in counts:
            sources.append(refs[at : at + n])
            at += n
        lying = refs[at : at + len(kept)]
        at += len(kept)
        results = refs[at : at + n_out]
        at += n_out
        held = refs[at : at + len(weights)]
        at += len(weights)
        brought = refs[at : at + len(kept)]
        at += len(kept)
        sems = refs[at] if copies else None
        own = refs[at + 1 :] if copies else refs[at:]
        started, slot = [], 0
        bringing = []
        for ref, into in zip(lying, brought):
            bringing.append(pltpu.make_async_copy(ref, into, sems.at[slot]))
            slot += 1
        for copy in bringing:
            copy.start()
        for (_, column, width, *whole), refs_of, into in zip(weights, sources, held):
            group = []
            columns = pl.ds(column, width)
            split = math.gcd(width // LANES, SPLIT)
            if len(refs_of) == 1:
                group.append(pltpu.make_async_copy(refs_of[0].at[:, columns], into, sems.at[slot]))
                slot += 1
            else:
                for place, offset in enumerate(ORDER):
                    for shift in range(plan.shards):
                        ref = refs_of[place].at[shift]
                        z = shift if whole else lax.rem(meta_ref[0] + (plan.shards - shift), plan.shards)
                        index = z * plan.contexts + jnp.bitwise_xor(meta_ref[1], offset)
                        row = pl.multiple_of(index * plan.block, 16)
                        for part in range(0, width, width // split):
                            group.append(
                                pltpu.make_async_copy(
                                    ref.at[:, pl.ds(column + part, width // split)],
                                    into.at[pl.ds(row, plan.block), pl.ds(part, width // split)],
                                    sems.at[slot],
                                )
                            )
                            slot += 1
            for copy in group:
                copy.start()
            started.append(group)

        def weight(i):
            for copy in started[i]:
                copy.wait()
            return held[i]

        for copy in bringing:
            copy.wait()
        body(meta_ref, (*ins, *brought), weight, results, own)

    vmem = pl.BlockSpec(memory_space=pltpu.VMEM)
    anywhere = pl.BlockSpec(memory_space=pl.ANY)
    outside = pl.BlockSpec(memory_space=pltpu.HBM)
    scratch_shapes = [pltpu.VMEM((plan.width, entry[2]), BF16) for entry in weights]
    scratch_shapes += [pltpu.VMEM(array.shape, array.dtype) for array in kept]
    if copies:
        scratch_shapes.append(pltpu.SemaphoreType.DMA((copies,)))
    moved = sum(x.size * x.dtype.itemsize for x in inputs)
    moved += sum(math.prod(o.shape) * o.dtype.itemsize for o in outs)
    moved += sum(plan.width * entry[2] * 2 for entry in weights)
    call = pl.pallas_call(
        kernel,
        name=name,
        out_shape=tuple(outs),
        in_specs=[pl.BlockSpec(memory_space=pltpu.SMEM)]
        + [vmem] * n_in
        + [outside if n == 1 else anywhere for n in counts for _ in range(n)]
        + [anywhere] * len(kept),
        out_specs=tuple(outside if i in direct else vmem for i in range(n_out)),
        scratch_shapes=scratch_shapes + list(scratch),
        compiler_params=pltpu.CompilerParams(vmem_limit_bytes=VMEM_LIMIT),
        cost_estimate=pl.CostEstimate(flops=0, bytes_accessed=0, transcendentals=0),
    )
    return call(meta, *inputs, *[array for entry in weights for array in entry[0]], *kept)


def shape(*dims, dtype=BF16):
    return jax.ShapeDtypeStruct(dims, dtype)


def segment(plan, meta, position):
    prompt = plan.group // 2
    seg = jnp.ones(position.shape, jnp.int32)
    for j in range(plan.conts):
        seg = seg + (position - prompt >= meta[2 + j]).astype(jnp.int32)
    return jnp.where(position < prompt, 0, seg)


def key_positions(plan, meta):
    if not plan.blocks:
        return lax.broadcasted_iota(jnp.int32, (plan.group, 1), 0)
    inside = lax.broadcasted_iota(jnp.int32, (plan.rows, 1), 0)
    return jnp.concatenate(
        [inside + jnp.bitwise_xor(meta[1], d) * plan.rows for d in ORDER], axis=0
    )


def allowed_keys(plan, meta):
    lane = lax.broadcasted_iota(jnp.int32, (1, 2 * plan.rows), 1)
    query = meta[1] * plan.rows + jnp.where(lane >= plan.rows, lane - plan.rows, lane)
    seg_query = segment(plan, meta, query)
    seg_key = segment(plan, meta, key_positions(plan, meta))
    return (seg_key == 0) | (seg_key == seg_query)


def pair_rows(values):
    first = lax.broadcasted_iota(jnp.int32, values.shape, 1) < HEAD_DIM
    none = jnp.zeros_like(values)
    return jnp.concatenate([jnp.where(first, values, none), jnp.where(first, none, values)], axis=0)


def pair_lanes(values):
    rows = values.shape[0] // 2
    first = lax.broadcasted_iota(jnp.int32, (rows, LANES), 1) < HEAD_DIM
    return jnp.where(first, values[:rows], values[rows:])


def write_qkv(plan, layer, x, gain, weight, q_bias, v_bias, a_ref, q_ref, kv_ref):
    n = plan.heads_width
    hat, _ = normed_rows(x)
    a = (hat * gain).astype(BF16)
    a_ref[...] = a
    bias_q = q_bias[...].astype(F32)[layer : layer + 1]
    bias_v = v_bias[...].astype(F32)[layer : layer + 1]
    kv_ref[:, :n] = nn(a, weight[:, n : 2 * n]).astype(BF16)
    kv_ref[:, n:] = (nn(a, weight[:, 2 * n :]) + bias_v).astype(BF16)
    q_ref[...] = (nn(a, weight[:, :n]) + bias_q).astype(BF16)


def embed_body(plan, meta, ins, weight, outs, own):
    tokens, q_bias, v_bias = ins
    x_ref, vec_ref, a_ref, q_ref, kv_ref = outs
    small = weight(1)[...].astype(F32).T
    vec_ref[...] = small[:8]
    lookup = small[8:24].astype(BF16)
    inside = lax.broadcasted_iota(jnp.int32, (plan.rows, 1), 0)
    seg = segment(plan, meta, meta[1] * plan.rows + inside)
    member = seg == lax.broadcasted_iota(jnp.int32, (plan.rows, 16), 1)
    x = tokens[...].astype(F32) + nn(member.astype(F32).astype(BF16), lookup)
    x_ref[...] = x
    write_qkv(plan, 0, x, small[:1], weight(0), q_bias, v_bias, a_ref, q_ref, kv_ref)


def next_body(plan, layer, meta, ins, weight, outs, own):
    x_mid, part, part_far, vec, q_bias, v_bias = ins
    x_ref, a_ref, q_ref, kv_ref = outs
    x = x_mid[...] + (part[...].astype(F32) + part_far[...].astype(F32))
    x = x + vec[2 * layer + 3 : 2 * layer + 4, :]
    x_ref[...] = x
    gain = vec[2 * layer : 2 * layer + 1, :]
    write_qkv(plan, layer, x, gain, weight(0), q_bias, v_bias, a_ref, q_ref, kv_ref)


def attend_body(plan, meta, ins, weight, outs, own):
    q_ref, kvs = ins[0], ins[1:]
    part_ref, o_ref, total_ref, all_ref = outs
    n = plan.heads_width
    for i, kv in enumerate(kvs):
        all_ref[i * kv.shape[0] : (i + 1) * kv.shape[0], :] = kv[...]
    allowed = allowed_keys(plan, meta)
    totals = []
    for pair in range(n // LANES):
        lanes = slice(pair * LANES, (pair + 1) * LANES)
        late = slice(n + pair * LANES, n + (pair + 1) * LANES)
        q2 = pair_rows(q_ref[:, lanes])
        keys = jnp.concatenate([kv[:, lanes] for kv in kvs], axis=0)
        values = jnp.concatenate([kv[:, late] for kv in kvs], axis=0)
        scores = jnp.where(allowed, nt(keys, q2) * (1.0 / math.sqrt(HEAD_DIM)), NEGATIVE)
        top = jnp.max(scores, axis=0, keepdims=True)
        exps = jnp.exp(scores - top)
        total = jnp.sum(exps, axis=0, keepdims=True)
        prob = (exps * (1.0 / total)).astype(BF16)
        o_ref[:, lanes] = pair_lanes(tn(prob, values)).astype(BF16)
        totals.append(top + jnp.log(total))
    total_ref[...] = rows_of(totals, 8, 2 * plan.rows)
    part_ref[...] = nt(o_ref[...], weight(0)[...]).astype(BF16)


def feed_body(plan, layer, last, meta, ins, weight, outs, own):
    x, part, part_far, vec, bias = ins[:5]
    mid_ref, b_ref, gelu_ref, slope_ref, part_ref = outs[:5]
    x_mid = x[...] + (part[...].astype(F32) + part_far[...].astype(F32))
    x_mid = x_mid + vec[2 * layer + 4 : 2 * layer + 5, :]
    mid_ref[...] = x_mid
    hat, _ = normed_rows(x_mid)
    b = (hat * vec[2 * layer + 1 : 2 * layer + 2, :]).astype(BF16)
    b_ref[...] = b
    bias_f = bias[...].astype(F32)[layer : layer + 1]
    up = weight(0)
    chunks = [slice(i, min(i + CHUNK, plan.hidden)) for i in range(0, plan.hidden, CHUNK)]
    for columns in chunks:
        hidden = nn(b, up[:, columns]) + bias_f[:, columns]
        half = 0.5 * (1.0 + lax.erf(hidden * math.sqrt(0.5)))
        gelu_ref[:, columns] = (hidden * half).astype(BF16)
        bell = jnp.exp(hidden * hidden * -0.5) * (1.0 / math.sqrt(2.0 * math.pi))
        slope_ref[:, columns] = half + hidden * bell
    down = weight(1)
    if last:
        back_feed(plan, ins[5][...], slope_ref, up, down, outs[5], outs[6], outs[7], ins[5][...].astype(F32), None)
    part_ref[...] = nt(gelu_ref[...], down[...]).astype(BF16)


def back_feed(plan, dy, slope, up, down, dh_ref, db_ref, sum_ref, gradient, extra):
    sums = []
    total = None
    for i in range(0, plan.hidden, CHUNK):
        columns = slice(i, min(i + CHUNK, plan.hidden))
        dh = (nn(dy, down[:, columns]) * slope[:, columns]).astype(BF16)
        dh_ref[:, columns] = dh
        sums.append(jnp.sum(dh.astype(F32), axis=0, keepdims=True))
        term = nt(dh, up[:, columns])
        total = term if total is None else total + term
    db_ref[...] = total.astype(BF16)
    bias_sum = jnp.concatenate(sums, axis=1)
    parts = [jnp.sum(gradient, axis=0, keepdims=True)]
    for i in range(plan.hidden // plan.width):
        parts.append(bias_sum[:, i * plan.width : (i + 1) * plan.width])
    if extra is not None:
        parts.append(extra)
    sum_ref[...] = rows_of(parts, 8, plan.width)


def between_body(plan, layer, meta, ins, weight, outs, own):
    da, da_far, dx_mid, x_above, vec, slope = ins
    gy_ref, dy_ref, dh_ref, db_ref, sum_ref = outs
    grad = da[...].astype(F32) + da_far[...].astype(F32)
    back, gain_sum = norm_back(x_above[...], vec[2 * layer + 2 : 2 * layer + 3, :], grad)
    gy = dx_mid[...] + back
    gy_ref[...] = gy
    dy = gy.astype(BF16)
    dy_ref[...] = dy
    back_feed(plan, dy, slope, weight(0), weight(1), dh_ref, db_ref, sum_ref, gy, gain_sum)


def attend_back_body(plan, layer, meta, ins, weight, outs, own):
    gy, db, db_far, x_mid, vec, q_ref, total = ins[:7]
    kvs = ins[7:]
    mid_ref, dz_ref, dq_ref, sum_ref = outs[:4]
    dkv = outs[4:]
    n = plan.heads_width
    scale = 1.0 / math.sqrt(HEAD_DIM)
    grad = db[...].astype(F32) + db_far[...].astype(F32)
    back, gain_sum = norm_back(x_mid[...], vec[2 * layer + 1 : 2 * layer + 2, :], grad)
    dx_mid = gy[...].astype(F32) + back
    mid_ref[...] = dx_mid
    sum_ref[...] = rows_of([gain_sum, jnp.sum(dx_mid, axis=0, keepdims=True)], 8, plan.width)
    dz = dx_mid.astype(BF16)
    dz_ref[...] = dz
    do = nn(dz, weight(0)[...]).astype(BF16)
    allowed = allowed_keys(plan, meta)
    each = plan.group // len(dkv)
    for pair in range(n // LANES):
        lanes = slice(pair * LANES, (pair + 1) * LANES)
        late = slice(n + pair * LANES, n + (pair + 1) * LANES)
        q2 = pair_rows(q_ref[:, lanes])
        do2 = pair_rows(do[:, lanes])
        keys = jnp.concatenate([kv[:, lanes] for kv in kvs], axis=0)
        values = jnp.concatenate([kv[:, late] for kv in kvs], axis=0)
        prob = jnp.exp(nt(keys, q2) * scale - total[pair : pair + 1, :])
        prob = jnp.where(allowed, prob, 0.0)
        dprob = nt(values, do2)
        delta = jnp.sum(prob * dprob, axis=0, keepdims=True)
        dscore = (prob * (dprob - delta)).astype(BF16)
        dq_ref[:, lanes] = (pair_lanes(tn(dscore, keys)) * scale).astype(BF16)
        dk = (nn(dscore, q2) * scale).astype(BF16)
        dv = nn(prob.astype(BF16), do2).astype(BF16)
        for i, ref in enumerate(dkv):
            ref[:, lanes] = dk[i * each : (i + 1) * each]
            ref[:, late] = dv[i * each : (i + 1) * each]


def project_back_body(plan, meta, ins, weight, outs, own):
    dq = ins[0]
    dqkv_ref, da_ref, sum_ref = outs
    n = plan.heads_width
    dkv = ins[1][: plan.rows].astype(F32)
    for term in ins[2:]:
        dkv = dkv + term[: plan.rows].astype(F32)
    dkv = dkv.astype(BF16)
    dqkv_ref[:, :n] = dq[...]
    dqkv_ref[:, n:] = dkv
    da_ref[...] = nt(dqkv_ref[...], weight(0)[...]).astype(BF16)
    sums = [
        jnp.sum(dq[...].astype(F32), axis=0, keepdims=True),
        jnp.sum(dkv[:, n:].astype(F32), axis=0, keepdims=True),
    ]
    sum_ref[...] = rows_of([jnp.concatenate(sums, axis=1)], 8, 2 * n)


def weight_grad_body(plan, widths, relative, meta, ins, weight, outs, own):
    packet, sems = own
    column, copies = 0, []
    for i, width in enumerate(widths):
        left, right = ins[2 * i], ins[2 * i + 1]
        turned = left[...].T
        for j in range(0, width, CHUNK):
            size = min(CHUNK, width - j)
            window = pl.ds(column, size)
            packet[:, column : column + size] = nn(turned, right[:, j : j + size]).astype(BF16)
            column += size
            if len(outs) == 1:
                copy = pltpu.make_async_copy(packet.at[:, window], outs[0].at[:, window], sems.at[len(copies)])
                copy.start()
                copies.append(copy)
                continue
            for place, offset in enumerate(ORDER):
                for k in range(plan.shards):
                    z = lax.rem(meta[0] + k, plan.shards) if relative else k
                    index = z * plan.contexts + jnp.bitwise_xor(meta[1], offset)
                    row = pl.multiple_of(index * plan.block, 16)
                    copy = pltpu.make_async_copy(
                        packet.at[pl.ds(row, plan.block), window],
                        outs[place // 2].at[place % 2, k, :, window],
                        sems.at[len(copies)],
                    )
                    copy.start()
                    copies.append(copy)
    for copy in copies:
        copy.wait()


def end_body(plan, meta, ins, weight, outs, own):
    da, da_far, dx_mid, x, vec = ins[:5]
    feed0, attn0, proj0, feed1, attn1, proj1 = ins[5:]
    gy_ref, small_ref = outs
    grad = da[...].astype(F32) + da_far[...].astype(F32)
    back, gain_sum = norm_back(x[...], vec[:1, :], grad)
    gy = dx_mid[...] + back
    gy_ref[...] = gy
    lane = lax.broadcasted_iota(jnp.int32, (1, plan.rows), 1)
    seg = segment(plan, meta, meta[1] * plan.rows + lane)
    member = (seg == lax.broadcasted_iota(jnp.int32, (16, plan.rows), 0)).astype(F32)
    sums = lax.dot_general(
        member, gy, (((1,), (0,)), ((), ())), precision=lax.Precision.HIGHEST, preferred_element_type=F32
    )
    halves = plan.hidden // plan.width
    parts = [sums]
    for gain_row, feed, attn, proj in (
        (gain_sum, feed0, attn0, proj0),
        (feed0[1 + halves : 2 + halves, :], feed1, attn1, proj1),
    ):
        parts += [gain_row, attn[0:1, :], attn[1:2, :], feed[0:1, :]]
        parts += [feed[1 + i : 2 + i, :] for i in range(halves)]
        parts += [proj[0:1, :]]
    small_ref[...] = rows_of_total(parts, 32, plan.width).astype(BF16)


def rows_of_total(parts, count, width):
    have = sum(part.shape[0] for part in parts)
    return jnp.concatenate(parts + [jnp.zeros((count - have, width), F32)], axis=0)


def swap_core(array):
    return lax.ppermute(array, "ctx", [(i, i ^ 1) for i in range(4)])


def swap_chip(array):
    return lax.ppermute(array, "ctx", [(i, i ^ 2) for i in range(4)])


def swap_tp(array):
    return lax.ppermute(array, "tp", [(0, 1), (1, 0)])


def to_shard(plan, array, shift):
    n = plan.shards
    return lax.ppermute(array, "shard", [(i, (i + shift) % n) for i in range(n)])


def stage_of(plan, thing, *names):
    if not plan.blocks:
        return ()
    found = [getattr(thing, name) for name in names]
    return tuple(array for one in found for array in (one if isinstance(one, tuple) else (one,)))


class Gather:
    def __init__(self, plan, packets, *ties):
        self.plan = plan
        if plan.blocks:
            packets = after_all(packets, *ties) if ties else tuple(packets)
            got = [to_shard(plan, packets[k], k) for k in range(1, plan.shards)]
            self.got = tuple(got)
            self.blocks = (packets[0], *got)
        else:
            self.arrays = (lax.all_gather(packets[0], ("shard", "ctx"), axis=0, tiled=True),)

    @classmethod
    def at_once(cls, plan, packet, *ties):
        self = cls.__new__(cls)
        self.plan = plan
        if plan.blocks:
            copies = jnp.broadcast_to(after(packet, *ties), (plan.shards, *packet.shape))
            self.stack = lax.all_to_all(copies, "shard", 0, 0, tiled=True)
        else:
            self.arrays = (lax.all_gather(packet, ("shard", "ctx"), axis=0, tiled=True),)
        return self

    def along(self, *ties):
        if self.plan.blocks:
            self.stack = jnp.stack(after_all(self.blocks, *ties) if ties else self.blocks)
        return self

    def across(self, *ties):
        if self.plan.blocks:
            self.far = swap_chip(after(self.stack, *ties) if ties else self.stack)
        return self

    def cores(self, *ties):
        if self.plan.blocks:
            halves = (self.stack, self.far)
            sent = after_all(halves, *ties) if ties else halves
            self.arrays = (*halves, *[swap_core(half) for half in sent])
        return self


def gather_keys(plan, kv):
    if plan.blocks:
        far = swap_chip(kv)
        return (kv, far, swap_core(kv), swap_core(far))
    return (lax.all_gather(kv, "ctx", axis=0, tiled=True),)


def after(array, *others):
    return lax.optimization_barrier((array, *others))[0]


def after_all(arrays, *others):
    return lax.optimization_barrier((*arrays, *others))[: len(arrays)]


def add(*terms):
    total = terms[0].astype(F32)
    for term in terms[1:]:
        total = total + term.astype(F32)
    return total


def weight_grads(plan, meta, name, pairs, blocks, relative=False):
    widths = tuple(right.shape[1] for _, right in pairs)
    width = sum(widths)
    copies = sum(pl.cdiv(width, CHUNK) for width in widths)
    if blocks:
        outs = [shape(2, plan.shards, plan.block, width)] * 2
        copies *= plan.shards * 4
    else:
        outs = [shape(plan.width, width)]
    return run(
        plan,
        functools.partial(weight_grad_body, plan, widths, relative),
        name,
        meta,
        [],
        [],
        outs,
        2 * plan.rows * plan.width * width,
        kept=[array for pair in pairs for array in pair],
        scratch=[pltpu.VMEM((plan.width, width), BF16), pltpu.SemaphoreType.DMA((copies,))],
        direct=tuple(range(len(outs))),
    )


class Reduction:
    def __init__(self, plan, meta, name, pairs, blocks=True, relative=False):
        self.blocks = blocks and plan.blocks
        self.plan, self.relative = plan, relative
        parts = weight_grads(plan, meta, name, pairs, self.blocks, relative)
        if self.blocks:
            self.keep, self.send = parts
        else:
            self.send = parts[0]
            total = lax.psum_scatter(parts[0], ("shard", "ctx"), scatter_dimension=0, tiled=True)
            self.total = total

    def core(self, *ties):
        if self.blocks:
            self.near = swap_core(after(self.send, *ties))
        return self

    def pairs(self, *ties):
        if self.blocks:
            self.near = after(self.near, *ties)
            self.pair = add(self.keep[1], self.near[1]).astype(BF16)
            self.far = swap_chip(self.pair)
        return self

    def along(self, *ties):
        if self.blocks:
            far = after(self.far, *ties) if ties else self.far
            if self.relative:
                n = self.plan.shards
                self.sums = tuple(
                    add(self.keep[0, k], self.near[0, k], far[k]).astype(BF16) for k in range(n)
                )
                self.got = (self.sums[0], *[to_shard(self.plan, self.sums[k], k) for k in range(1, n)])
            else:
                self.sums = add(self.keep[0], self.near[0], far).astype(BF16)
                self.got = lax.all_to_all(self.sums, "shard", 0, 0, tiled=True)
        return self

    def end(self, *ties):
        if not self.blocks:
            return (after(self.total, *ties) if self.plan.blocks else self.total).astype(F32)
        if self.relative:
            return add(*after_all(self.got, *ties))
        return jnp.sum(after(self.got, *ties).astype(F32), axis=0)


def per_device(
    tokens,
    timesteps,
    cont_lengths,
    table,
    w_qkv,
    w_out,
    w_up,
    w_down,
    norms,
    query_bias,
    value_bias,
    up_bias,
    out_biases,
    cotangent,
):
    rows, width = tokens.shape
    layers, block = w_qkv.shape[:2]
    heads_width, hidden = w_qkv.shape[3], w_up.shape[2]
    shards, contexts = lax.axis_size("shard"), lax.axis_size("ctx")
    conts = cont_lengths.shape[1]
    plan = Plan(rows, width, block, heads_width, hidden, shards, contexts, conts)
    z, c = lax.axis_index("shard"), lax.axis_index("ctx")
    meta = jnp.concatenate([jnp.stack([z, c]).astype(jnp.int32), jnp.cumsum(cont_lengths[0])])

    n3 = 3 * heads_width

    def everywhere(packet):
        return (lax.all_gather(packet, ("shard", "ctx"), axis=0, tiled=True),)

    upper = jnp.concatenate([w_qkv[1].reshape(block, -1), w_out[1], w_up[1], w_down[1]], axis=1)
    first = jnp.concatenate([w_qkv[0].reshape(block, -1), w_out[0]], axis=1)
    steps = after(timesteps, first)
    first = Gather(plan, [first] * shards)

    vectors = jnp.concatenate(
        [norms[0], norms[1], out_biases[0], out_biases[1]], axis=1
    )
    seqs = conts + 1
    steps_back = jnp.concatenate([steps] + [to_shard(plan, steps, k) for k in range(1, shards)])
    steps_near = jnp.concatenate([steps_back[:1], steps_back[:0:-1]]).reshape(-1)
    one_hot = (steps_near[:, None] == jnp.arange(table.shape[0], dtype=jnp.int32)[None, :]).astype(BF16)
    looked = lax.dot_general(
        table, one_hot, (((0,), (1,)), ((), ())), preferred_element_type=F32
    ).astype(BF16)
    blank = jnp.zeros((block, LANES - vectors.shape[1] - seqs), BF16)
    if plan.blocks:
        small = [
            jnp.concatenate([vectors, looked[:, k * seqs : (k + 1) * seqs], blank], axis=1)
            for k in range(shards)
        ]
        small = Gather(plan, small)
        first.along(*small.got)
        ties = (first.stack,)
        small = small.along().across().cores().arrays
    else:
        looked = jnp.roll(looked.reshape(block, shards, seqs), z, axis=1).reshape(block, -1)
        every = lax.all_gather(jnp.concatenate([vectors, looked], axis=1), ("shard", "ctx"), axis=0, tiled=True)
        mine = lax.dynamic_slice_in_dim(every, 8 + z * seqs, seqs, axis=1)
        blank = jnp.zeros((width, LANES - 8 - seqs), BF16)
        small = [jnp.concatenate([every[:, :8], mine, blank], axis=1)]
        ties = ()
    second = Gather(plan, [w_up[0]] * shards, *ties)
    third = Gather.at_once(plan, w_down[0], *ties)
    first.across().cores(*stage_of(plan, second, "got"))
    upper = everywhere(after(upper, *ties))

    mm = 2 * rows * width
    full = shape(rows, width, dtype=F32)
    low = shape(rows, width)
    heads = shape(rows, heads_width)
    wide = shape(rows, hidden)
    sums = shape(8, width, dtype=F32)
    qkv_outs = [low, heads, shape(rows, 2 * heads_width)]
    attn_flops = 4 * rows * plan.group * heads_width

    saved = []
    x_mid = part = part_far = None
    for layer in range(layers):
        last = layer == layers - 1
        ties = ()
        if layer == 0:
            x, vec, a, q, kv = run(
                plan,
                functools.partial(embed_body, plan),
                "embed",
                meta,
                [tokens, query_bias, value_bias],
                [(first.arrays, 0, n3), (small, 0, LANES)],
                [full, sums, *qkv_outs],
                mm * n3,
                ties=stage_of(plan, second, "got"),
            )
            second.along(kv).across()
            ties = stage_of(plan, second, "stack") + stage_of(plan, third, "stack")
            of_attn = [(first.arrays, 0, n3), (first.arrays, n3, heads_width)]
        else:
            of_attn = [(upper, 0, n3), (upper, n3, heads_width)]
            of_feed = [(upper, n3 + heads_width + i * hidden, hidden) for i in range(2)]
            x, a, q, kv = run(
                plan,
                functools.partial(next_body, plan, layer),
                "project",
                meta,
                [x_mid, part, part_far, vec, query_bias, value_bias],
                of_attn[:1],
                [full, *qkv_outs],
                mm * n3,
            )
        kvs = gather_keys(plan, kv)
        part, o, total, kv_all = run(
            plan,
            functools.partial(attend_body, plan),
            "attend",
            meta,
            [q, *kvs],
            of_attn[1:],
            [low, heads, shape(8, 2 * rows, dtype=F32), shape(plan.group, 2 * heads_width)],
            mm * heads_width + attn_flops,
            ties=ties,
        )
        part_far = swap_tp(part)
        if layer == 0:
            second.cores(part)
            third.across(part).cores(part_far)
            of_feed = [(second.arrays, 0, hidden), (third.arrays, 0, hidden, True)]
        outs = [full, low, wide, shape(rows, hidden, dtype=F32), low]
        if last:
            outs += [wide, low, sums]
        got = run(
            plan,
            functools.partial(feed_body, plan, layer, last),
            "feed",
            meta,
            [x, part, part_far, vec, up_bias] + ([cotangent] if last else []),
            of_feed,
            outs,
            mm * hidden * (4 if last else 2),
        )
        x_mid, b, gelu, slope, part = got[:5]
        part_far = swap_tp(part)
        saved.append((x, a, q, kv_all, o, total, x_mid, b, gelu, slope, of_attn, of_feed))

    gy = dy = cotangent
    dh, db, feed_sum = got[5:]
    final = (x_mid, part, part_far)
    bias_last = vec[2 * layers + 3][None, :]
    small_sums = [None] * layers
    above = None
    for layer in reversed(range(layers)):
        x, a, q, kv_all, o, total, x_mid, b, gelu, slope, of_attn, of_feed = saved[layer]
        if above is not None:
            gy, dy, dh, db, feed_sum = run(
                plan,
                functools.partial(between_body, plan, layer),
                "feed_back",
                meta,
                [da, da_far],
                of_feed,
                [full, low, wide, low, sums],
                2 * mm * hidden,
                kept=[dx_mid, saved[layer + 1][0], vec, slope],
                ties=stage_of(plan, above, "send"),
            )
        db_far = swap_tp(db)
        if above is None:
            ties = ()
        else:
            feeds = [
                Reduction(plan, meta, "up_grad", [(b, dh)]).core(db_far),
                Reduction(plan, meta, "down_grad", [(dy, gelu)], relative=True).core(db_far),
            ]
            ties = stage_of(plan, feeds[0], "send") + stage_of(plan, feeds[1], "send")
        if plan.blocks:
            dkv_outs = [shape(2 * rows, 2 * heads_width)] * 2
        else:
            dkv_outs = [shape(plan.group, 2 * heads_width)]
        dx_mid, dz, dq, attn_sum, *dkv = run(
            plan,
            functools.partial(attend_back_body, plan, layer),
            "attend_back",
            meta,
            [gy, db, db_far],
            of_attn[1:],
            [full, low, heads, sums, *dkv_outs],
            mm * heads_width + 10 * rows * plan.group * heads_width,
            ties=ties,
            kept=[x_mid, vec, q, total, kv_all],
        )
        ties = ()
        if plan.blocks:
            keep, send = dkv
            near = swap_core(send)
            summed = add(keep[rows:], near[rows:]).astype(BF16)
            terms = [keep, near, swap_chip(summed)]
            if above is None:
                x_mid, part, part_far = after_all(final, summed)
                activations = (x_mid + add(part, part_far) + bias_last).astype(BF16)
                ties = (activations,)
        else:
            terms = [lax.psum_scatter(dkv[0], "ctx", scatter_dimension=0, tiled=True)]
            if above is None:
                activations = (x_mid + add(part, part_far) + bias_last).astype(BF16)
        dqkv, da, proj_sum = run(
            plan,
            functools.partial(project_back_body, plan),
            "project_back",
            meta,
            [dq, *terms],
            of_attn[:1],
            [shape(rows, n3), low, shape(8, 2 * heads_width, dtype=F32)],
            mm * n3,
            ties=ties,
        )
        da_far = swap_tp(da)
        if above is None:
            pairs = [(a, dqkv), (dz, o), (b, dh), (dy, gelu)]
            above = Reduction(plan, meta, "layer_grad", pairs, blocks=False)
        else:
            attn = Reduction(plan, meta, "attn_grad", [(a, dqkv), (dz, o)]).core(da_far)
            for feed in feeds:
                feed.pairs(da)
            end_ties = stage_of(plan, attn, "send") + stage_of(plan, feeds[0], "far") + stage_of(plan, feeds[1], "pair")
        small_sums[layer] = [feed_sum, attn_sum, proj_sum]

    grad_tokens, packet = run(
        plan,
        functools.partial(end_body, plan),
        "end",
        meta,
        [da, da_far],
        [],
        [full, shape(32, width)],
        mm * 32,
        ties=end_ties,
        kept=[dx_mid, saved[0][0], vec, *small_sums[0], *small_sums[1]],
    )
    attn.pairs(packet)
    feeds[0].along(packet, *stage_of(plan, attn, "pair"))
    feeds[1].along(packet, *stage_of(plan, feeds[0], "sums"))
    start = (z * contexts + c) * block
    if plan.blocks:
        packet = add(packet, swap_core(packet)).astype(BF16)
        packet = after(packet, attn.pair)
        packet = add(packet, swap_chip(packet)).astype(BF16)
        got = jnp.stack([packet] + [to_shard(plan, packet, k) for k in range(1, shards)])
        other = add(*[got[k] for k in range(0, shards, 2)]) + add(*[got[k] for k in range(1, shards, 2)])
    else:
        packet = lax.psum(packet, "ctx")
        got = lax.all_gather(packet, "shard", axis=0)
        other = jnp.sum(got.astype(F32), axis=0)
        steps_back = jnp.roll(steps_back[::-1], z + 1, axis=0)
    mine = lax.dynamic_slice_in_dim(got[:, :seqs], start, block, axis=2).reshape(-1, block)
    one_hot = (jnp.arange(table.shape[0], dtype=jnp.int32)[:, None] == steps_back.reshape(-1)[None, :]).astype(BF16)
    grad_table = jnp.dot(one_hot, mine, preferred_element_type=F32)

    attn.along(*stage_of(plan, feeds[1], "sums"))
    upper_grad = above.end(packet)
    halves = hidden // width
    per_layer = 5 + halves
    by_layer = other[16 : 16 + layers * per_layer].reshape(layers, per_layer, width)
    local = lax.dynamic_slice_in_dim(by_layer[:, :4], start, block, axis=2)
    grad_norms = jnp.moveaxis(local[:, :2], 1, 2)
    grad_out_biases = jnp.moveaxis(local[:, 2:], 1, 2)
    grad_up_bias = by_layer[:, 4 : 4 + halves].reshape(layers, hidden)
    grad_query_bias = by_layer[:, 4 + halves, :heads_width]
    grad_value_bias = by_layer[:, 4 + halves, heads_width:]
    at = n3 + heads_width
    ups = [feeds[0].end(), upper_grad[:, at : at + hidden]]
    downs = [feeds[1].end(), upper_grad[:, at + hidden :]]
    attns = [attn.end(), upper_grad[:, :at]]
    return (
        activations,
        grad_tokens,
        jnp.stack([g[:, :n3].reshape(block, 3, heads_width) for g in attns]),
        jnp.stack([g[:, n3:at] for g in attns]),
        jnp.stack(ups),
        jnp.stack(downs),
        grad_norms,
        grad_table,
        grad_query_bias,
        grad_value_bias,
        grad_up_bias,
        grad_out_biases,
    )


def solution(mesh):
    placed = (
        P(("shard", "ctx"), None),
        P("shard", None),
        P("shard", None),
        P(None, ("shard", "ctx")),
        P(None, ("shard", "ctx"), None, "tp"),
        P(None, ("shard", "ctx"), "tp"),
        P(None, ("shard", "ctx"), "tp"),
        P(None, ("shard", "ctx"), "tp"),
        P(None, ("shard", "ctx"), None),
        P(None, "tp"),
        P(None, "tp"),
        P(None, "tp"),
        P(None, ("shard", "ctx"), None),
        P(("shard", "ctx"), None),
    )
    return jax.shard_map(
        per_device,
        mesh=mesh,
        in_specs=placed,
        out_specs=(
            P(("shard", "ctx"), None),
            P(("shard", "ctx"), None),
            P(None, ("shard", "ctx"), None, "tp"),
            P(None, ("shard", "ctx"), "tp"),
            P(None, ("shard", "ctx"), "tp"),
            P(None, ("shard", "ctx"), "tp"),
            P(None, ("shard", "ctx"), None),
            P(None, ("shard", "ctx")),
            P(None, "tp"),
            P(None, "tp"),
            P(None, "tp"),
            P(None, ("shard", "ctx"), None),
        ),
        check_vma=False,
    )
```

```python
import functools
import math

import jax
import jax.numpy as jnp
from jax import lax
from jax.experimental import pallas as pl
from jax.experimental.pallas import tpu as pltpu
from jax.sharding import PartitionSpec as P

HEAD_DIM = 64
EPSILON = 1e-05
NEGATIVE = -1e30
F32 = jnp.float32
BF16 = jnp.bfloat16
LANES = 128
CHUNK = 512
SPLIT = 3
VMEM_LIMIT = 46 * 1024 * 1024
LIMIT_FB = 58 * 1024 * 1024
ORDER = (0, 2, 1, 3)


def nn(a, b):
    return lax.dot_general(a, b, (((1,), (0,)), ((), ())), preferred_element_type=F32)


def nt(a, b):
    return lax.dot_general(a, b, (((1,), (1,)), ((), ())), preferred_element_type=F32)


def tn(a, b):
    return lax.dot_general(a, b, (((0,), (0,)), ((), ())), preferred_element_type=F32)


def normed_rows(values):
    centered = values - jnp.mean(values, axis=-1, keepdims=True)
    scale = lax.rsqrt(jnp.mean(centered * centered, axis=-1, keepdims=True) + EPSILON)
    return centered * scale, scale


def norm_back(values, gain, grad):
    hat, scale = normed_rows(values)
    grad_gain = jnp.sum(grad * hat, axis=0, keepdims=True)
    inner = grad * gain
    along = jnp.mean(inner * hat, axis=-1, keepdims=True)
    centre = jnp.mean(inner, axis=-1, keepdims=True)
    return scale * (inner - centre - hat * along), grad_gain


def rows_of(parts, count, width):
    have = len(parts)
    if have < count:
        parts = list(parts) + [jnp.zeros((count - have, width), F32)]
    return jnp.concatenate(parts, axis=0)


class Plan:
    def __init__(self, rows, width, block, heads_width, hidden, shards, contexts, conts):
        self.rows, self.width, self.block = rows, width, block
        self.heads_width, self.hidden = heads_width, hidden
        self.shards, self.contexts, self.conts = shards, contexts, conts
        self.group = rows * contexts
        self.blocks = contexts == 4 and block % 16 == 0


def run(plan, body, name, meta, inputs, weights, outs, flops, scratch=(), direct=(), ties=(), kept=(), limit=VMEM_LIMIT):
    if ties:
        inputs = [after(inputs[0], *ties), *inputs[1:]]
    n_in, n_out = len(inputs), len(outs)
    counts = [len(entry[0]) for entry in weights]
    per_block = plan.shards * len(ORDER) * SPLIT
    copies = sum(1 if n == 1 else per_block for n in counts) + len(kept)

    def kernel(meta_ref, *refs):
        ins = refs[:n_in]
        at = n_in
        sources = []
        for n in counts:
            sources.append(refs[at : at + n])
            at += n
        lying = refs[at : at + len(kept)]
        at += len(kept)
        results = refs[at : at + n_out]
        at += n_out
        held = refs[at : at + len(weights)]
        at += len(weights)
        brought = refs[at : at + len(kept)]
        at += len(kept)
        sems = refs[at] if copies else None
        own = refs[at + 1 :] if copies else refs[at:]
        started, slot = [], 0
        bringing = []
        for ref, into in zip(lying, brought):
            bringing.append(pltpu.make_async_copy(ref, into, sems.at[slot]))
            slot += 1
        for copy in bringing:
            copy.start()
        for (_, column, width, *whole), refs_of, into in zip(weights, sources, held):
            group = []
            columns = pl.ds(column, width)
            split = math.gcd(width // LANES, SPLIT)
            if len(refs_of) == 1:
                group.append(pltpu.make_async_copy(refs_of[0].at[:, columns], into, sems.at[slot]))
                slot += 1
            else:
                for place, offset in enumerate(ORDER):
                    for shift in range(plan.shards):
                        ref = refs_of[place].at[shift]
                        z = shift if whole else lax.rem(meta_ref[0] + (plan.shards - shift), plan.shards)
                        index = z * plan.contexts + jnp.bitwise_xor(meta_ref[1], offset)
                        row = pl.multiple_of(index * plan.block, 16)
                        for part in range(0, width, width // split):
                            group.append(
                                pltpu.make_async_copy(
                                    ref.at[:, pl.ds(column + part, width // split)],
                                    into.at[pl.ds(row, plan.block), pl.ds(part, width // split)],
                                    sems.at[slot],
                                )
                            )
                            slot += 1
            for copy in group:
                copy.start()
            started.append(group)

        def weight(i):
            for copy in started[i]:
                copy.wait()
            return held[i]

        for copy in bringing:
            copy.wait()
        body(meta_ref, (*ins, *brought), weight, results, own)

    vmem = pl.BlockSpec(memory_space=pltpu.VMEM)
    anywhere = pl.BlockSpec(memory_space=pl.ANY)
    outside = pl.BlockSpec(memory_space=pltpu.HBM)
    scratch_shapes = [pltpu.VMEM((plan.width, entry[2]), BF16) for entry in weights]
    scratch_shapes += [pltpu.VMEM(array.shape, array.dtype) for array in kept]
    if copies:
        scratch_shapes.append(pltpu.SemaphoreType.DMA((copies,)))
    moved = sum(x.size * x.dtype.itemsize for x in inputs)
    moved += sum(math.prod(o.shape) * o.dtype.itemsize for o in outs)
    moved += sum(plan.width * entry[2] * 2 for entry in weights)
    call = pl.pallas_call(
        kernel,
        name=name,
        out_shape=tuple(outs),
        in_specs=[pl.BlockSpec(memory_space=pltpu.SMEM)]
        + [vmem] * n_in
        + [outside if n == 1 else anywhere for n in counts for _ in range(n)]
        + [anywhere] * len(kept),
        out_specs=tuple(outside if i in direct else vmem for i in range(n_out)),
        scratch_shapes=scratch_shapes + list(scratch),
        compiler_params=pltpu.CompilerParams(vmem_limit_bytes=limit),
        cost_estimate=pl.CostEstimate(flops=flops, bytes_accessed=moved, transcendentals=0),
    )
    return call(meta, *inputs, *[array for entry in weights for array in entry[0]], *kept)


def shape(*dims, dtype=BF16):
    return jax.ShapeDtypeStruct(dims, dtype)


def segment(plan, meta, position):
    prompt = plan.group // 2
    seg = jnp.ones(position.shape, jnp.int32)
    for j in range(plan.conts):
        seg = seg + (position - prompt >= meta[2 + j]).astype(jnp.int32)
    return jnp.where(position < prompt, 0, seg)


def key_positions(plan, meta):
    if not plan.blocks:
        return lax.broadcasted_iota(jnp.int32, (plan.group, 1), 0)
    inside = lax.broadcasted_iota(jnp.int32, (plan.rows, 1), 0)
    return jnp.concatenate(
        [inside + jnp.bitwise_xor(meta[1], d) * plan.rows for d in ORDER], axis=0
    )


def allowed_keys(plan, meta):
    lane = lax.broadcasted_iota(jnp.int32, (1, 2 * plan.rows), 1)
    query = meta[1] * plan.rows + jnp.where(lane >= plan.rows, lane - plan.rows, lane)
    seg_query = segment(plan, meta, query)
    seg_key = segment(plan, meta, key_positions(plan, meta))
    return (seg_key == 0) | (seg_key == seg_query)


def pair_rows(values):
    first = lax.broadcasted_iota(jnp.int32, values.shape, 1) < HEAD_DIM
    none = jnp.zeros_like(values)
    return jnp.concatenate([jnp.where(first, values, none), jnp.where(first, none, values)], axis=0)


def pair_lanes(values):
    rows = values.shape[0] // 2
    first = lax.broadcasted_iota(jnp.int32, (rows, LANES), 1) < HEAD_DIM
    return jnp.where(first, values[:rows], values[rows:])


def write_qkv(plan, layer, x, gain, weight, q_bias, v_bias, a_ref, q_ref, kv_ref):
    n = plan.heads_width
    hat, _ = normed_rows(x)
    a = (hat * gain).astype(BF16)
    a_ref[...] = a
    bias_q = q_bias[...].astype(F32)[layer : layer + 1]
    bias_v = v_bias[...].astype(F32)[layer : layer + 1]
    kv_ref[:, :n] = nn(a, weight[:, n : 2 * n]).astype(BF16)
    kv_ref[:, n:] = (nn(a, weight[:, 2 * n :]) + bias_v).astype(BF16)
    q_ref[...] = (nn(a, weight[:, :n]) + bias_q).astype(BF16)


def embed_body(plan, meta, ins, weight, outs, own):
    tokens, q_bias, v_bias = ins
    x_ref, vec_ref, a_ref, q_ref, kv_ref = outs
    small = weight(1)[...].astype(F32).T
    vec_ref[...] = small[:8]
    lookup = small[8:24].astype(BF16)
    inside = lax.broadcasted_iota(jnp.int32, (plan.rows, 1), 0)
    seg = segment(plan, meta, meta[1] * plan.rows + inside)
    member = seg == lax.broadcasted_iota(jnp.int32, (plan.rows, 16), 1)
    x = tokens[...].astype(F32) + nn(member.astype(F32).astype(BF16), lookup)
    x_ref[...] = x
    write_qkv(plan, 0, x, small[:1], weight(0), q_bias, v_bias, a_ref, q_ref, kv_ref)


def next_body(plan, layer, meta, ins, weight, outs, own):
    x_mid, part, part_far, vec, q_bias, v_bias = ins
    x_ref, a_ref, q_ref, kv_ref = outs
    x = x_mid[...] + (part[...].astype(F32) + part_far[...].astype(F32))
    x = x + vec[2 * layer + 3 : 2 * layer + 4, :]
    x_ref[...] = x
    gain = vec[2 * layer : 2 * layer + 1, :]
    write_qkv(plan, layer, x, gain, weight(0), q_bias, v_bias, a_ref, q_ref, kv_ref)


def attend_body(plan, meta, ins, weight, outs, own):
    q_ref, kvs = ins[0], ins[1:]
    part_ref, o_ref, total_ref, all_ref = outs
    n = plan.heads_width
    for i, kv in enumerate(kvs):
        all_ref[i * kv.shape[0] : (i + 1) * kv.shape[0], :] = kv[...]
    allowed = allowed_keys(plan, meta)
    totals = []
    for pair in range(n // LANES):
        lanes = slice(pair * LANES, (pair + 1) * LANES)
        late = slice(n + pair * LANES, n + (pair + 1) * LANES)
        q2 = pair_rows(q_ref[:, lanes])
        keys = jnp.concatenate([kv[:, lanes] for kv in kvs], axis=0)
        values = jnp.concatenate([kv[:, late] for kv in kvs], axis=0)
        scores = jnp.where(allowed, nt(keys, q2) * (1.0 / math.sqrt(HEAD_DIM)), NEGATIVE)
        top = jnp.max(scores, axis=0, keepdims=True)
        exps = jnp.exp(scores - top)
        total = jnp.sum(exps, axis=0, keepdims=True)
        prob = (exps * (1.0 / total)).astype(BF16)
        o_ref[:, lanes] = pair_lanes(tn(prob, values)).astype(BF16)
        totals.append(top + jnp.log(total))
    total_ref[...] = rows_of(totals, 8, 2 * plan.rows)
    part_ref[...] = nt(o_ref[...], weight(0)[...]).astype(BF16)


def feed_body(plan, layer, last, meta, ins, weight, outs, own):
    x, part, part_far, vec, bias = ins[:5]
    mid_ref, b_ref, gelu_ref, slope_ref, part_ref = outs[:5]
    x_mid = x[...] + (part[...].astype(F32) + part_far[...].astype(F32))
    x_mid = x_mid + vec[2 * layer + 4 : 2 * layer + 5, :]
    mid_ref[...] = x_mid
    hat, _ = normed_rows(x_mid)
    b = (hat * vec[2 * layer + 1 : 2 * layer + 2, :]).astype(BF16)
    b_ref[...] = b
    bias_f = bias[...].astype(F32)[layer : layer + 1]
    up = weight(0)
    chunks = [slice(i, min(i + CHUNK, plan.hidden)) for i in range(0, plan.hidden, CHUNK)]
    for columns in chunks:
        hidden = nn(b, up[:, columns]) + bias_f[:, columns]
        half = 0.5 * (1.0 + lax.erf(hidden * math.sqrt(0.5)))
        gelu_ref[:, columns] = (hidden * half).astype(BF16)
        bell = jnp.exp(hidden * hidden * -0.5) * (1.0 / math.sqrt(2.0 * math.pi))
        slope_ref[:, columns] = half + hidden * bell
    down = weight(1)
    if last:
        back_feed(plan, ins[5][...], slope_ref, up, down, outs[5], outs[6], outs[7], ins[5][...].astype(F32), None)
    part_ref[...] = nt(gelu_ref[...], down[...]).astype(BF16)


def back_feed(plan, dy, slope, up, down, dh_ref, db_ref, sum_ref, gradient, extra):
    sums = []
    total = None
    for i in range(0, plan.hidden, CHUNK):
        columns = slice(i, min(i + CHUNK, plan.hidden))
        dh = (nn(dy, down[:, columns]) * slope[:, columns]).astype(BF16)
        dh_ref[:, columns] = dh
        sums.append(jnp.sum(dh.astype(F32), axis=0, keepdims=True))
        term = nt(dh, up[:, columns])
        total = term if total is None else total + term
    db_ref[...] = total.astype(BF16)
    bias_sum = jnp.concatenate(sums, axis=1)
    parts = [jnp.sum(gradient, axis=0, keepdims=True)]
    for i in range(plan.hidden // plan.width):
        parts.append(bias_sum[:, i * plan.width : (i + 1) * plan.width])
    if extra is not None:
        parts.append(extra)
    sum_ref[...] = rows_of(parts, 8, plan.width)


def between_body(plan, layer, meta, ins, weight, outs, own):
    da, da_far, dx_mid, x_above, vec, slope = ins
    gy_ref, dy_ref, dh_ref, db_ref, sum_ref = outs
    grad = da[...].astype(F32) + da_far[...].astype(F32)
    back, gain_sum = norm_back(x_above[...], vec[2 * layer + 2 : 2 * layer + 3, :], grad)
    gy = dx_mid[...] + back
    gy_ref[...] = gy
    dy = gy.astype(BF16)
    dy_ref[...] = dy
    back_feed(plan, dy, slope, weight(0), weight(1), dh_ref, db_ref, sum_ref, gy, gain_sum)


def attend_back_body(plan, layer, meta, ins, weight, outs, own):
    gy, db, db_far, x_mid, vec, q_ref, total = ins[:7]
    kvs = ins[7:]
    mid_ref, dz_ref, dq_ref, sum_ref = outs[:4]
    dkv = outs[4:]
    n = plan.heads_width
    scale = 1.0 / math.sqrt(HEAD_DIM)
    grad = db[...].astype(F32) + db_far[...].astype(F32)
    back, gain_sum = norm_back(x_mid[...], vec[2 * layer + 1 : 2 * layer + 2, :], grad)
    dx_mid = gy[...].astype(F32) + back
    mid_ref[...] = dx_mid
    sum_ref[...] = rows_of([gain_sum, jnp.sum(dx_mid, axis=0, keepdims=True)], 8, plan.width)
    dz = dx_mid.astype(BF16)
    dz_ref[...] = dz
    do = nn(dz, weight(0)[...]).astype(BF16)
    allowed = allowed_keys(plan, meta)
    each = plan.group // len(dkv)
    for pair in range(n // LANES):
        lanes = slice(pair * LANES, (pair + 1) * LANES)
        late = slice(n + pair * LANES, n + (pair + 1) * LANES)
        q2 = pair_rows(q_ref[:, lanes])
        do2 = pair_rows(do[:, lanes])
        keys = jnp.concatenate([kv[:, lanes] for kv in kvs], axis=0)
        values = jnp.concatenate([kv[:, late] for kv in kvs], axis=0)
        prob = jnp.exp(nt(keys, q2) * scale - total[pair : pair + 1, :])
        prob = jnp.where(allowed, prob, 0.0)
        dprob = nt(values, do2)
        delta = jnp.sum(prob * dprob, axis=0, keepdims=True)
        dscore = (prob * (dprob - delta)).astype(BF16)
        dq_ref[:, lanes] = (pair_lanes(tn(dscore, keys)) * scale).astype(BF16)
        dk = (nn(dscore, q2) * scale).astype(BF16)
        dv = nn(prob.astype(BF16), do2).astype(BF16)
        for i, ref in enumerate(dkv):
            ref[:, lanes] = dk[i * each : (i + 1) * each]
            ref[:, late] = dv[i * each : (i + 1) * each]


def project_back_body(plan, meta, ins, weight, outs, own):
    dq = ins[0]
    dqkv_ref, da_ref, sum_ref = outs
    n = plan.heads_width
    dkv = ins[1][: plan.rows].astype(F32)
    for term in ins[2:]:
        dkv = dkv + term[: plan.rows].astype(F32)
    dkv = dkv.astype(BF16)
    dqkv_ref[:, :n] = dq[...]
    dqkv_ref[:, n:] = dkv
    da_ref[...] = nt(dqkv_ref[...], weight(0)[...]).astype(BF16)
    sums = [
        jnp.sum(dq[...].astype(F32), axis=0, keepdims=True),
        jnp.sum(dkv[:, n:].astype(F32), axis=0, keepdims=True),
    ]
    sum_ref[...] = rows_of([jnp.concatenate(sums, axis=1)], 8, 2 * n)


def weight_grad_body(plan, widths, relative, meta, ins, weight, outs, own):
    packet, sems = own
    column, copies = 0, []
    for i, width in enumerate(widths):
        left, right = ins[2 * i], ins[2 * i + 1]
        turned = left[...].T
        for j in range(0, width, CHUNK):
            size = min(CHUNK, width - j)
            window = pl.ds(column, size)
            packet[:, column : column + size] = nn(turned, right[:, j : j + size]).astype(BF16)
            column += size
            if len(outs) == 1:
                copy = pltpu.make_async_copy(packet.at[:, window], outs[0].at[:, window], sems.at[len(copies)])
                copy.start()
                copies.append(copy)
                continue
            for place, offset in enumerate(ORDER):
                for k in range(plan.shards):
                    z = lax.rem(meta[0] + k, plan.shards) if relative else k
                    index = z * plan.contexts + jnp.bitwise_xor(meta[1], offset)
                    row = pl.multiple_of(index * plan.block, 16)
                    copy = pltpu.make_async_copy(
                        packet.at[pl.ds(row, plan.block), window],
                        outs[place // 2].at[place % 2, k, :, window],
                        sems.at[len(copies)],
                    )
                    copy.start()
                    copies.append(copy)
    for copy in copies:
        copy.wait()


def end_body(plan, meta, ins, weight, outs, own):
    da, da_far, dx_mid, x, vec = ins[:5]
    feed0, attn0, proj0, feed1, attn1, proj1 = ins[5:]
    gy_ref, small_ref = outs
    grad = da[...].astype(F32) + da_far[...].astype(F32)
    back, gain_sum = norm_back(x[...], vec[:1, :], grad)
    gy = dx_mid[...] + back
    gy_ref[...] = gy
    lane = lax.broadcasted_iota(jnp.int32, (1, plan.rows), 1)
    seg = segment(plan, meta, meta[1] * plan.rows + lane)
    member = (seg == lax.broadcasted_iota(jnp.int32, (16, plan.rows), 0)).astype(F32)
    sums = lax.dot_general(
        member, gy, (((1,), (0,)), ((), ())), precision=lax.Precision.HIGHEST, preferred_element_type=F32
    )
    halves = plan.hidden // plan.width
    parts = [sums]
    for gain_row, feed, attn, proj in (
        (gain_sum, feed0, attn0, proj0),
        (feed0[1 + halves : 2 + halves, :], feed1, attn1, proj1),
    ):
        parts += [gain_row, attn[0:1, :], attn[1:2, :], feed[0:1, :]]
        parts += [feed[1 + i : 2 + i, :] for i in range(halves)]
        parts += [proj[0:1, :]]
    small_ref[...] = rows_of_total(parts, 32, plan.width).astype(BF16)


def rows_of_total(parts, count, width):
    have = sum(part.shape[0] for part in parts)
    return jnp.concatenate(parts + [jnp.zeros((count - have, width), F32)], axis=0)


def swap_core(array):
    return lax.ppermute(array, "ctx", [(i, i ^ 1) for i in range(4)])


def swap_chip(array):
    return lax.ppermute(array, "ctx", [(i, i ^ 2) for i in range(4)])


def swap_tp(array):
    return lax.ppermute(array, "tp", [(0, 1), (1, 0)])


def to_shard(plan, array, shift):
    n = plan.shards
    return lax.ppermute(array, "shard", [(i, (i + shift) % n) for i in range(n)])


def stage_of(plan, thing, *names):
    if not plan.blocks:
        return ()
    found = [getattr(thing, name) for name in names]
    return tuple(array for one in found for array in (one if isinstance(one, tuple) else (one,)))


class Gather:
    def __init__(self, plan, packets, *ties):
        self.plan = plan
        if plan.blocks:
            packets = after_all(packets, *ties) if ties else tuple(packets)
            got = [to_shard(plan, packets[k], k) for k in range(1, plan.shards)]
            self.got = tuple(got)
            self.blocks = (packets[0], *got)
        else:
            self.arrays = (lax.all_gather(packets[0], ("shard", "ctx"), axis=0, tiled=True),)

    @classmethod
    def at_once(cls, plan, packet, *ties):
        self = cls.__new__(cls)
        self.plan = plan
        if plan.blocks:
            copies = jnp.broadcast_to(after(packet, *ties), (plan.shards, *packet.shape))
            self.stack = lax.all_to_all(copies, "shard", 0, 0, tiled=True)
        else:
            self.arrays = (lax.all_gather(packet, ("shard", "ctx"), axis=0, tiled=True),)
        return self

    def along(self, *ties):
        if self.plan.blocks:
            self.stack = jnp.stack(after_all(self.blocks, *ties) if ties else self.blocks)
        return self

    def across(self, *ties):
        if self.plan.blocks:
            self.far = swap_chip(after(self.stack, *ties) if ties else self.stack)
        return self

    def cores(self, *ties):
        if self.plan.blocks:
            halves = (self.stack, self.far)
            sent = after_all(halves, *ties) if ties else halves
            self.arrays = (*halves, *[swap_core(half) for half in sent])
        return self


def gather_keys(plan, kv):
    if plan.blocks:
        far = swap_chip(kv)
        return (kv, far, swap_core(kv), swap_core(far))
    return (lax.all_gather(kv, "ctx", axis=0, tiled=True),)


def after(array, *others):
    return lax.optimization_barrier((array, *others))[0]


def after_all(arrays, *others):
    return lax.optimization_barrier((*arrays, *others))[: len(arrays)]


def add(*terms):
    total = terms[0].astype(F32)
    for term in terms[1:]:
        total = total + term.astype(F32)
    return total


def weight_grads(plan, meta, name, pairs, blocks, relative=False):
    widths = tuple(right.shape[1] for _, right in pairs)
    width = sum(widths)
    copies = sum(pl.cdiv(width, CHUNK) for width in widths)
    if blocks:
        outs = [shape(2, plan.shards, plan.block, width)] * 2
        copies *= plan.shards * 4
    else:
        outs = [shape(plan.width, width)]
    return run(
        plan,
        functools.partial(weight_grad_body, plan, widths, relative),
        name,
        meta,
        [],
        [],
        outs,
        2 * plan.rows * plan.width * width,
        kept=[array for pair in pairs for array in pair],
        scratch=[pltpu.VMEM((plan.width, width), BF16), pltpu.SemaphoreType.DMA((copies,))],
        direct=tuple(range(len(outs))),
    )


class Reduction:
    def __init__(self, plan, meta, name, pairs, blocks=True, relative=False):
        self.blocks = blocks and plan.blocks
        self.plan, self.relative = plan, relative
        parts = weight_grads(plan, meta, name, pairs, self.blocks, relative)
        if self.blocks:
            self.keep, self.send = parts
        else:
            self.send = parts[0]
            total = lax.psum_scatter(parts[0], ("shard", "ctx"), scatter_dimension=0, tiled=True)
            self.total = total

    def core(self, *ties):
        if self.blocks:
            self.near = swap_core(after(self.send, *ties))
        return self

    def pairs(self, *ties):
        if self.blocks:
            self.near = after(self.near, *ties)
            self.pair = add(self.keep[1], self.near[1]).astype(BF16)
            self.far = swap_chip(self.pair)
        return self

    def along(self, *ties):
        if self.blocks:
            far = after(self.far, *ties) if ties else self.far
            if self.relative:
                n = self.plan.shards
                self.sums = tuple(
                    add(self.keep[0, k], self.near[0, k], far[k]).astype(BF16) for k in range(n)
                )
                self.got = (self.sums[0], *[to_shard(self.plan, self.sums[k], k) for k in range(1, n)])
            else:
                self.sums = add(self.keep[0], self.near[0], far).astype(BF16)
                self.got = lax.all_to_all(self.sums, "shard", 0, 0, tiled=True)
        return self

    def end(self, *ties):
        if not self.blocks:
            return (after(self.total, *ties) if self.plan.blocks else self.total).astype(F32)
        if self.relative:
            return add(*after_all(self.got, *ties))
        return jnp.sum(after(self.got, *ties).astype(F32), axis=0)


def per_device(
    tokens,
    timesteps,
    cont_lengths,
    table,
    w_qkv,
    w_out,
    w_up,
    w_down,
    norms,
    query_bias,
    value_bias,
    up_bias,
    out_biases,
    cotangent,
):
    rows, width = tokens.shape
    layers, block = w_qkv.shape[:2]
    heads_width, hidden = w_qkv.shape[3], w_up.shape[2]
    shards, contexts = lax.axis_size("shard"), lax.axis_size("ctx")
    conts = cont_lengths.shape[1]
    plan = Plan(rows, width, block, heads_width, hidden, shards, contexts, conts)
    z, c = lax.axis_index("shard"), lax.axis_index("ctx")
    meta = jnp.concatenate([jnp.stack([z, c]).astype(jnp.int32), jnp.cumsum(cont_lengths[0])])

    n3 = 3 * heads_width

    def everywhere(packet):
        return (lax.all_gather(packet, ("shard", "ctx"), axis=0, tiled=True),)

    upper = jnp.concatenate([w_qkv[1].reshape(block, -1), w_out[1], w_up[1], w_down[1]], axis=1)
    first = jnp.concatenate([w_qkv[0].reshape(block, -1), w_out[0]], axis=1)
    steps = after(timesteps, first)
    first = Gather(plan, [first] * shards)

    vectors = jnp.concatenate(
        [norms[0], norms[1], out_biases[0], out_biases[1]], axis=1
    )
    seqs = conts + 1
    steps_back = jnp.concatenate([steps] + [to_shard(plan, steps, k) for k in range(1, shards)])
    steps_near = jnp.concatenate([steps_back[:1], steps_back[:0:-1]]).reshape(-1)
    one_hot = (steps_near[:, None] == jnp.arange(table.shape[0], dtype=jnp.int32)[None, :]).astype(BF16)
    looked = lax.dot_general(
        table, one_hot, (((0,), (1,)), ((), ())), preferred_element_type=F32
    ).astype(BF16)
    blank = jnp.zeros((block, LANES - vectors.shape[1] - seqs), BF16)
    if plan.blocks:
        small = [
            jnp.concatenate([vectors, looked[:, k * seqs : (k + 1) * seqs], blank], axis=1)
            for k in range(shards)
        ]
        small = Gather(plan, small)
        first.along(*small.got)
        ties = (first.stack,)
        small = small.along().across().cores().arrays
    else:
        looked = jnp.roll(looked.reshape(block, shards, seqs), z, axis=1).reshape(block, -1)
        every = lax.all_gather(jnp.concatenate([vectors, looked], axis=1), ("shard", "ctx"), axis=0, tiled=True)
        mine = lax.dynamic_slice_in_dim(every, 8 + z * seqs, seqs, axis=1)
        blank = jnp.zeros((width, LANES - 8 - seqs), BF16)
        small = [jnp.concatenate([every[:, :8], mine, blank], axis=1)]
        ties = ()
    second = Gather(plan, [w_up[0]] * shards, *ties)
    third = Gather.at_once(plan, w_down[0], *ties)
    first.across().cores(*stage_of(plan, second, "got"))
    upper = everywhere(after(upper, *ties))

    mm = 2 * rows * width
    full = shape(rows, width, dtype=F32)
    low = shape(rows, width)
    heads = shape(rows, heads_width)
    wide = shape(rows, hidden)
    sums = shape(8, width, dtype=F32)
    qkv_outs = [low, heads, shape(rows, 2 * heads_width)]
    attn_flops = 4 * rows * plan.group * heads_width

    saved = []
    x_mid = part = part_far = None
    for layer in range(layers):
        last = layer == layers - 1
        ties = ()
        if layer == 0:
            x, vec, a, q, kv = run(
                plan,
                functools.partial(embed_body, plan),
                "embed",
                meta,
                [tokens, query_bias, value_bias],
                [(first.arrays, 0, n3), (small, 0, LANES)],
                [full, sums, *qkv_outs],
                mm * n3,
                ties=stage_of(plan, second, "got"),
            )
            second.along(kv).across()
            ties = stage_of(plan, second, "stack") + stage_of(plan, third, "stack")
            of_attn = [(first.arrays, 0, n3), (first.arrays, n3, heads_width)]
        else:
            of_attn = [(upper, 0, n3), (upper, n3, heads_width)]
            of_feed = [(upper, n3 + heads_width + i * hidden, hidden) for i in range(2)]
            x, a, q, kv = run(
                plan,
                functools.partial(next_body, plan, layer),
                "project",
                meta,
                [x_mid, part, part_far, vec, query_bias, value_bias],
                of_attn[:1],
                [full, *qkv_outs],
                mm * n3,
            )
        kvs = gather_keys(plan, kv)
        part, o, total, kv_all = run(
            plan,
            functools.partial(attend_body, plan),
            "attend",
            meta,
            [q, *kvs],
            of_attn[1:],
            [low, heads, shape(8, 2 * rows, dtype=F32), shape(plan.group, 2 * heads_width)],
            mm * heads_width + attn_flops,
            ties=ties,
        )
        part_far = swap_tp(part)
        if layer == 0:
            second.cores(part)
            third.across(part).cores(part_far)
            of_feed = [(second.arrays, 0, hidden), (third.arrays, 0, hidden, True)]
        outs = [full, low, wide, shape(rows, hidden, dtype=F32), low]
        if last:
            outs += [wide, low, sums]
        got = run(
            plan,
            functools.partial(feed_body, plan, layer, last),
            "feed",
            meta,
            [x, part, part_far, vec, up_bias] + ([cotangent] if last else []),
            of_feed,
            outs,
            mm * hidden * (4 if last else 2),
        )
        x_mid, b, gelu, slope, part = got[:5]
        part_far = swap_tp(part)
        saved.append((x, a, q, kv_all, o, total, x_mid, b, gelu, slope, of_attn, of_feed))

    gy = dy = cotangent
    dh, db, feed_sum = got[5:]
    final = (x_mid, part, part_far)
    bias_last = vec[2 * layers + 3][None, :]
    small_sums = [None] * layers
    above = None
    for layer in reversed(range(layers)):
        x, a, q, kv_all, o, total, x_mid, b, gelu, slope, of_attn, of_feed = saved[layer]
        if above is not None:
            gy, dy, dh, db, feed_sum = run(
                plan,
                functools.partial(between_body, plan, layer),
                "feed_back",
                meta,
                [da, da_far],
                of_feed,
                [full, low, wide, low, sums],
                2 * mm * hidden,
                kept=[dx_mid, saved[layer + 1][0], vec, slope],
                limit=LIMIT_FB,
                ties=stage_of(plan, above, "send"),
            )
        db_far = swap_tp(db)
        if above is None:
            upper_feed = Reduction(plan, meta, "feed_grad", [(b, dh), (dy, gelu)], blocks=False)
            ties = stage_of(plan, upper_feed, "send")
        else:
            feeds = [
                Reduction(plan, meta, "up_grad", [(b, dh)], relative=True).core(db_far),
                Reduction(plan, meta, "down_grad", [(dy, gelu)]).core(db_far),
            ]
            ties = stage_of(plan, feeds[0], "send") + stage_of(plan, feeds[1], "send")
        if plan.blocks:
            dkv_outs = [shape(2 * rows, 2 * heads_width)] * 2
        else:
            dkv_outs = [shape(plan.group, 2 * heads_width)]
        dx_mid, dz, dq, attn_sum, *dkv = run(
            plan,
            functools.partial(attend_back_body, plan, layer),
            "attend_back",
            meta,
            [gy, db, db_far],
            of_attn[1:],
            [full, low, heads, sums, *dkv_outs],
            mm * heads_width + 10 * rows * plan.group * heads_width,
            ties=ties,
            kept=[x_mid, vec, q, total, kv_all],
        )
        ties = ()
        if plan.blocks:
            keep, send = dkv
            near = swap_core(send)
            summed = add(keep[rows:], near[rows:]).astype(BF16)
            terms = [keep, near, swap_chip(summed)]
        else:
            terms = [lax.psum_scatter(dkv[0], "ctx", scatter_dimension=0, tiled=True)]
            summed = terms[0]
        if above is not None:
            for one in (above, *feeds):
                one.pairs(summed)
                ties += stage_of(plan, one, "pair")
        dqkv, da, proj_sum = run(
            plan,
            functools.partial(project_back_body, plan),
            "project_back",
            meta,
            [dq, *terms],
            of_attn[:1],
            [shape(rows, n3), low, shape(8, 2 * heads_width, dtype=F32)],
            mm * n3,
            ties=ties,
        )
        da_far = swap_tp(da)
        attn = Reduction(plan, meta, "attn_grad", [(a, dqkv), (dz, o)], relative=above is not None).core(da_far)
        if above is not None:
            end_ties = stage_of(plan, attn, "send") + stage_of(plan, above, "far")
            upper_attn = above
        above = attn
        small_sums[layer] = [feed_sum, attn_sum, proj_sum]

    grad_tokens, packet = run(
        plan,
        functools.partial(end_body, plan),
        "end",
        meta,
        [da, da_far],
        [],
        [full, shape(32, width)],
        mm * 32,
        ties=end_ties,
        kept=[dx_mid, saved[0][0], vec, *small_sums[0], *small_sums[1]],
    )
    upper_attn.along(packet)
    attn.pairs(packet, *stage_of(plan, feeds[0], "far"))
    feeds[0].along(packet, *stage_of(plan, upper_attn, "sums"), *stage_of(plan, upper_feed, "total"))
    feeds[1].along(*stage_of(plan, feeds[0], "sums"), *stage_of(plan, attn, "pair"))
    attn.along(*stage_of(plan, feeds[1], "sums"), *stage_of(plan, feeds[0], "got"))
    x_mid, part, part_far = after_all(final, packet)
    activations = (x_mid + add(part, part_far) + bias_last).astype(BF16)
    start = (z * contexts + c) * block
    if plan.blocks:
        packet = add(packet, swap_core(packet)).astype(BF16)
        far = after(swap_chip(packet), *attn.sums)
        packet = add(packet, far).astype(BF16)
        got = jnp.stack([packet] + [to_shard(plan, packet, k) for k in range(1, shards)])
        other = add(*[got[k] for k in range(0, shards, 2)]) + add(*[got[k] for k in range(1, shards, 2)])
    else:
        packet = lax.psum(packet, "ctx")
        got = lax.all_gather(packet, "shard", axis=0)
        other = jnp.sum(got.astype(F32), axis=0)
        steps_back = jnp.roll(steps_back[::-1], z + 1, axis=0)
    mine = lax.dynamic_slice_in_dim(got[:, :seqs], start, block, axis=2).reshape(-1, block)
    one_hot = (jnp.arange(table.shape[0], dtype=jnp.int32)[:, None] == steps_back.reshape(-1)[None, :]).astype(BF16)
    grad_table = jnp.dot(one_hot, mine, preferred_element_type=F32)

    upper_feed, upper_attn = upper_feed.end(packet), upper_attn.end(packet)
    halves = hidden // width
    per_layer = 5 + halves
    by_layer = other[16 : 16 + layers * per_layer].reshape(layers, per_layer, width)
    local = lax.dynamic_slice_in_dim(by_layer[:, :4], start, block, axis=2)
    grad_norms = jnp.moveaxis(local[:, :2], 1, 2)
    grad_out_biases = jnp.moveaxis(local[:, 2:], 1, 2)
    grad_up_bias = by_layer[:, 4 : 4 + halves].reshape(layers, hidden)
    grad_query_bias = by_layer[:, 4 + halves, :heads_width]
    grad_value_bias = by_layer[:, 4 + halves, heads_width:]
    ups = [feeds[0].end(), upper_feed[:, :hidden]]
    downs = [feeds[1].end(), upper_feed[:, hidden:]]
    attns = [attn.end(), upper_attn]
    return (
        activations,
        grad_tokens,
        jnp.stack([g[:, :n3].reshape(block, 3, heads_width) for g in attns]),
        jnp.stack([g[:, n3:] for g in attns]),
        jnp.stack(ups),
        jnp.stack(downs),
        grad_norms,
        grad_table,
        grad_query_bias,
        grad_value_bias,
        grad_up_bias,
        grad_out_biases,
    )


def solution(mesh):
    placed = (
        P(("shard", "ctx"), None),
        P("shard", None),
        P("shard", None),
        P(None, ("shard", "ctx")),
        P(None, ("shard", "ctx"), None, "tp"),
        P(None, ("shard", "ctx"), "tp"),
        P(None, ("shard", "ctx"), "tp"),
        P(None, ("shard", "ctx"), "tp"),
        P(None, ("shard", "ctx"), None),
        P(None, "tp"),
        P(None, "tp"),
        P(None, "tp"),
        P(None, ("shard", "ctx"), None),
        P(("shard", "ctx"), None),
    )
    return jax.shard_map(
        per_device,
        mesh=mesh,
        in_specs=placed,
        out_specs=(
            P(("shard", "ctx"), None),
            P(("shard", "ctx"), None),
            P(None, ("shard", "ctx"), None, "tp"),
            P(None, ("shard", "ctx"), "tp"),
            P(None, ("shard", "ctx"), "tp"),
            P(None, ("shard", "ctx"), "tp"),
            P(None, ("shard", "ctx"), None),
            P(None, ("shard", "ctx")),
            P(None, "tp"),
            P(None, "tp"),
            P(None, "tp"),
            P(None, ("shard", "ctx"), None),
        ),
        check_vma=False,
    )
```

```python
import functools
import math

import jax
import jax.numpy as jnp
from jax import lax
from jax.experimental import pallas as pl
from jax.experimental.pallas import tpu as pltpu
from jax.sharding import PartitionSpec as P

HEAD_DIM = 64
EPSILON = 1e-05
NEGATIVE = -1e30
F32 = jnp.float32
BF16 = jnp.bfloat16
LANES = 128
CHUNK = 512
SPLIT = 3
VMEM_LIMIT = 46 * 1024 * 1024
LIMIT_FB = 58 * 1024 * 1024
ORDER = (0, 2, 1, 3)


def nn(a, b):
    return lax.dot_general(a, b, (((1,), (0,)), ((), ())), preferred_element_type=F32)


def nt(a, b):
    return lax.dot_general(a, b, (((1,), (1,)), ((), ())), preferred_element_type=F32)


def tn(a, b):
    return lax.dot_general(a, b, (((0,), (0,)), ((), ())), preferred_element_type=F32)


def normed_rows(values):
    centered = values - jnp.mean(values, axis=-1, keepdims=True)
    scale = lax.rsqrt(jnp.mean(centered * centered, axis=-1, keepdims=True) + EPSILON)
    return centered * scale, scale


def norm_back(values, gain, grad):
    hat, scale = normed_rows(values)
    grad_gain = jnp.sum(grad * hat, axis=0, keepdims=True)
    inner = grad * gain
    along = jnp.mean(inner * hat, axis=-1, keepdims=True)
    centre = jnp.mean(inner, axis=-1, keepdims=True)
    return scale * (inner - centre - hat * along), grad_gain


def rows_of(parts, count, width):
    have = len(parts)
    if have < count:
        parts = list(parts) + [jnp.zeros((count - have, width), F32)]
    return jnp.concatenate(parts, axis=0)


class Plan:
    def __init__(self, rows, width, block, heads_width, hidden, shards, contexts, conts):
        self.rows, self.width, self.block = rows, width, block
        self.heads_width, self.hidden = heads_width, hidden
        self.shards, self.contexts, self.conts = shards, contexts, conts
        self.group = rows * contexts
        self.blocks = contexts == 4 and block % 16 == 0


def run(plan, body, name, meta, inputs, weights, outs, flops, scratch=(), direct=(), ties=(), kept=(), limit=VMEM_LIMIT):
    if ties:
        inputs = [after(inputs[0], *ties), *inputs[1:]]
    n_in, n_out = len(inputs), len(outs)
    counts = [len(entry[0]) for entry in weights]
    per_block = plan.shards * len(ORDER) * SPLIT
    copies = sum(1 if n == 1 else per_block for n in counts) + len(kept)

    def kernel(meta_ref, *refs):
        ins = refs[:n_in]
        at = n_in
        sources = []
        for n in counts:
            sources.append(refs[at : at + n])
            at += n
        lying = refs[at : at + len(kept)]
        at += len(kept)
        results = refs[at : at + n_out]
        at += n_out
        held = refs[at : at + len(weights)]
        at += len(weights)
        brought = refs[at : at + len(kept)]
        at += len(kept)
        sems = refs[at] if copies else None
        own = refs[at + 1 :] if copies else refs[at:]
        started, slot = [], 0
        bringing = []
        for ref, into in zip(lying, brought):
            bringing.append(pltpu.make_async_copy(ref, into, sems.at[slot]))
            slot += 1
        for copy in bringing:
            copy.start()
        for (_, column, width, *whole), refs_of, into in zip(weights, sources, held):
            group = []
            columns = pl.ds(column, width)
            split = math.gcd(width // LANES, SPLIT)
            if len(refs_of) == 1:
                group.append(pltpu.make_async_copy(refs_of[0].at[:, columns], into, sems.at[slot]))
                slot += 1
            else:
                for place, offset in enumerate(ORDER):
                    for shift in range(plan.shards):
                        ref = refs_of[place].at[shift]
                        z = shift if whole else lax.rem(meta_ref[0] + (plan.shards - shift), plan.shards)
                        index = z * plan.contexts + jnp.bitwise_xor(meta_ref[1], offset)
                        row = pl.multiple_of(index * plan.block, 16)
                        for part in range(0, width, width // split):
                            group.append(
                                pltpu.make_async_copy(
                                    ref.at[:, pl.ds(column + part, width // split)],
                                    into.at[pl.ds(row, plan.block), pl.ds(part, width // split)],
                                    sems.at[slot],
                                )
                            )
                            slot += 1
            for copy in group:
                copy.start()
            started.append(group)

        def weight(i):
            for copy in started[i]:
                copy.wait()
            return held[i]

        for copy in bringing:
            copy.wait()
        body(meta_ref, (*ins, *brought), weight, results, own)

    vmem = pl.BlockSpec(memory_space=pltpu.VMEM)
    anywhere = pl.BlockSpec(memory_space=pl.ANY)
    outside = pl.BlockSpec(memory_space=pltpu.HBM)
    scratch_shapes = [pltpu.VMEM((plan.width, entry[2]), BF16) for entry in weights]
    scratch_shapes += [pltpu.VMEM(array.shape, array.dtype) for array in kept]
    if copies:
        scratch_shapes.append(pltpu.SemaphoreType.DMA((copies,)))
    moved = sum(x.size * x.dtype.itemsize for x in inputs)
    moved += sum(math.prod(o.shape) * o.dtype.itemsize for o in outs)
    moved += sum(plan.width * entry[2] * 2 for entry in weights)
    call = pl.pallas_call(
        kernel,
        name=name,
        out_shape=tuple(outs),
        in_specs=[pl.BlockSpec(memory_space=pltpu.SMEM)]
        + [vmem] * n_in
        + [outside if n == 1 else anywhere for n in counts for _ in range(n)]
        + [anywhere] * len(kept),
        out_specs=tuple(outside if i in direct else vmem for i in range(n_out)),
        scratch_shapes=scratch_shapes + list(scratch),
        compiler_params=pltpu.CompilerParams(vmem_limit_bytes=limit),
        cost_estimate=pl.CostEstimate(flops=flops, bytes_accessed=moved, transcendentals=0),
    )
    return call(meta, *inputs, *[array for entry in weights for array in entry[0]], *kept)


def shape(*dims, dtype=BF16):
    return jax.ShapeDtypeStruct(dims, dtype)


def segment(plan, meta, position):
    prompt = plan.group // 2
    seg = jnp.ones(position.shape, jnp.int32)
    for j in range(plan.conts):
        seg = seg + (position - prompt >= meta[2 + j]).astype(jnp.int32)
    return jnp.where(position < prompt, 0, seg)


def key_positions(plan, meta):
    if not plan.blocks:
        return lax.broadcasted_iota(jnp.int32, (plan.group, 1), 0)
    inside = lax.broadcasted_iota(jnp.int32, (plan.rows, 1), 0)
    return jnp.concatenate(
        [inside + jnp.bitwise_xor(meta[1], d) * plan.rows for d in ORDER], axis=0
    )


def allowed_keys(plan, meta):
    lane = lax.broadcasted_iota(jnp.int32, (1, 2 * plan.rows), 1)
    query = meta[1] * plan.rows + jnp.where(lane >= plan.rows, lane - plan.rows, lane)
    seg_query = segment(plan, meta, query)
    seg_key = segment(plan, meta, key_positions(plan, meta))
    return (seg_key == 0) | (seg_key == seg_query)


def pair_rows(values):
    first = lax.broadcasted_iota(jnp.int32, values.shape, 1) < HEAD_DIM
    none = jnp.zeros_like(values)
    return jnp.concatenate([jnp.where(first, values, none), jnp.where(first, none, values)], axis=0)


def pair_lanes(values):
    rows = values.shape[0] // 2
    first = lax.broadcasted_iota(jnp.int32, (rows, LANES), 1) < HEAD_DIM
    return jnp.where(first, values[:rows], values[rows:])


def write_qkv(plan, layer, x, gain, weight, q_bias, v_bias, a_ref, q_ref, kv_ref):
    n = plan.heads_width
    hat, _ = normed_rows(x)
    a = (hat * gain).astype(BF16)
    a_ref[...] = a
    bias_q = q_bias[...].astype(F32)[layer : layer + 1]
    bias_v = v_bias[...].astype(F32)[layer : layer + 1]
    kv_ref[:, :n] = nn(a, weight[:, n : 2 * n]).astype(BF16)
    kv_ref[:, n:] = (nn(a, weight[:, 2 * n :]) + bias_v).astype(BF16)
    q_ref[...] = (nn(a, weight[:, :n]) + bias_q).astype(BF16)


def embed_body(plan, meta, ins, weight, outs, own):
    tokens, q_bias, v_bias = ins
    x_ref, vec_ref, a_ref, q_ref, kv_ref = outs
    small = weight(1)[...].astype(F32).T
    vec_ref[...] = small[:8]
    lookup = small[8:24].astype(BF16)
    inside = lax.broadcasted_iota(jnp.int32, (plan.rows, 1), 0)
    seg = segment(plan, meta, meta[1] * plan.rows + inside)
    member = seg == lax.broadcasted_iota(jnp.int32, (plan.rows, 16), 1)
    x = tokens[...].astype(F32) + nn(member.astype(F32).astype(BF16), lookup)
    x_ref[...] = x
    write_qkv(plan, 0, x, small[:1], weight(0), q_bias, v_bias, a_ref, q_ref, kv_ref)


def next_body(plan, layer, meta, ins, weight, outs, own):
    x_mid, part, part_far, vec, q_bias, v_bias = ins
    x_ref, a_ref, q_ref, kv_ref = outs
    x = x_mid[...] + (part[...].astype(F32) + part_far[...].astype(F32))
    x = x + vec[2 * layer + 3 : 2 * layer + 4, :]
    x_ref[...] = x
    gain = vec[2 * layer : 2 * layer + 1, :]
    write_qkv(plan, layer, x, gain, weight(0), q_bias, v_bias, a_ref, q_ref, kv_ref)


def attend_body(plan, meta, ins, weight, outs, own):
    q_ref, kvs = ins[0], ins[1:]
    part_ref, o_ref, total_ref, all_ref = outs
    n = plan.heads_width
    for i, kv in enumerate(kvs):
        all_ref[i * kv.shape[0] : (i + 1) * kv.shape[0], :] = kv[...]
    allowed = allowed_keys(plan, meta)
    totals = []
    for pair in range(n // LANES):
        lanes = slice(pair * LANES, (pair + 1) * LANES)
        late = slice(n + pair * LANES, n + (pair + 1) * LANES)
        q2 = pair_rows(q_ref[:, lanes])
        keys = jnp.concatenate([kv[:, lanes] for kv in kvs], axis=0)
        values = jnp.concatenate([kv[:, late] for kv in kvs], axis=0)
        scores = jnp.where(allowed, nt(keys, q2) * (1.0 / math.sqrt(HEAD_DIM)), NEGATIVE)
        top = jnp.max(scores, axis=0, keepdims=True)
        exps = jnp.exp(scores - top)
        total = jnp.sum(exps, axis=0, keepdims=True)
        prob = (exps * (1.0 / total)).astype(BF16)
        o_ref[:, lanes] = pair_lanes(tn(prob, values)).astype(BF16)
        totals.append(top + jnp.log(total))
    total_ref[...] = rows_of(totals, 8, 2 * plan.rows)
    part_ref[...] = nt(o_ref[...], weight(0)[...]).astype(BF16)


def feed_body(plan, layer, last, meta, ins, weight, outs, own):
    x, part, part_far, vec, bias = ins[:5]
    mid_ref, b_ref, gelu_ref, slope_ref, part_ref = outs[:5]
    x_mid = x[...] + (part[...].astype(F32) + part_far[...].astype(F32))
    x_mid = x_mid + vec[2 * layer + 4 : 2 * layer + 5, :]
    mid_ref[...] = x_mid
    hat, _ = normed_rows(x_mid)
    b = (hat * vec[2 * layer + 1 : 2 * layer + 2, :]).astype(BF16)
    b_ref[...] = b
    bias_f = bias[...].astype(F32)[layer : layer + 1]
    up = weight(0)
    chunks = [slice(i, min(i + CHUNK, plan.hidden)) for i in range(0, plan.hidden, CHUNK)]
    for columns in chunks:
        hidden = nn(b, up[:, columns]) + bias_f[:, columns]
        half = 0.5 * (1.0 + lax.erf(hidden * math.sqrt(0.5)))
        gelu_ref[:, columns] = (hidden * half).astype(BF16)
        bell = jnp.exp(hidden * hidden * -0.5) * (1.0 / math.sqrt(2.0 * math.pi))
        slope_ref[:, columns] = half + hidden * bell
    down = weight(1)
    if last:
        back_feed(plan, ins[5][...], slope_ref, up, down, outs[5], outs[6], outs[7], ins[5][...].astype(F32), None)
    part_ref[...] = nt(gelu_ref[...], down[...]).astype(BF16)


def back_feed(plan, dy, slope, up, down, dh_ref, db_ref, sum_ref, gradient, extra):
    sums = []
    total = None
    for i in range(0, plan.hidden, CHUNK):
        columns = slice(i, min(i + CHUNK, plan.hidden))
        dh = (nn(dy, down[:, columns]) * slope[:, columns]).astype(BF16)
        dh_ref[:, columns] = dh
        sums.append(jnp.sum(dh.astype(F32), axis=0, keepdims=True))
        term = nt(dh, up[:, columns])
        total = term if total is None else total + term
    db_ref[...] = total.astype(BF16)
    bias_sum = jnp.concatenate(sums, axis=1)
    parts = [jnp.sum(gradient, axis=0, keepdims=True)]
    for i in range(plan.hidden // plan.width):
        parts.append(bias_sum[:, i * plan.width : (i + 1) * plan.width])
    if extra is not None:
        parts.append(extra)
    sum_ref[...] = rows_of(parts, 8, plan.width)


def between_body(plan, layer, meta, ins, weight, outs, own):
    da, da_far, dx_mid, x_above, vec, slope = ins
    gy_ref, dy_ref, dh_ref, db_ref, sum_ref = outs
    grad = da[...].astype(F32) + da_far[...].astype(F32)
    back, gain_sum = norm_back(x_above[...], vec[2 * layer + 2 : 2 * layer + 3, :], grad)
    gy = dx_mid[...] + back
    gy_ref[...] = gy
    dy = gy.astype(BF16)
    dy_ref[...] = dy
    back_feed(plan, dy, slope, weight(0), weight(1), dh_ref, db_ref, sum_ref, gy, gain_sum)


def attend_back_body(plan, layer, meta, ins, weight, outs, own):
    gy, db, db_far, x_mid, vec, q_ref, total = ins[:7]
    kvs = ins[7:]
    mid_ref, dz_ref, dq_ref, sum_ref = outs[:4]
    dkv = outs[4:]
    n = plan.heads_width
    scale = 1.0 / math.sqrt(HEAD_DIM)
    grad = db[...].astype(F32) + db_far[...].astype(F32)
    back, gain_sum = norm_back(x_mid[...], vec[2 * layer + 1 : 2 * layer + 2, :], grad)
    dx_mid = gy[...].astype(F32) + back
    mid_ref[...] = dx_mid
    sum_ref[...] = rows_of([gain_sum, jnp.sum(dx_mid, axis=0, keepdims=True)], 8, plan.width)
    dz = dx_mid.astype(BF16)
    dz_ref[...] = dz
    do = nn(dz, weight(0)[...]).astype(BF16)
    allowed = allowed_keys(plan, meta)
    each = plan.group // len(dkv)
    for pair in range(n // LANES):
        lanes = slice(pair * LANES, (pair + 1) * LANES)
        late = slice(n + pair * LANES, n + (pair + 1) * LANES)
        q2 = pair_rows(q_ref[:, lanes])
        do2 = pair_rows(do[:, lanes])
        keys = jnp.concatenate([kv[:, lanes] for kv in kvs], axis=0)
        values = jnp.concatenate([kv[:, late] for kv in kvs], axis=0)
        prob = jnp.exp(nt(keys, q2) * scale - total[pair : pair + 1, :])
        prob = jnp.where(allowed, prob, 0.0)
        dprob = nt(values, do2)
        delta = jnp.sum(prob * dprob, axis=0, keepdims=True)
        dscore = (prob * (dprob - delta)).astype(BF16)
        dq_ref[:, lanes] = (pair_lanes(tn(dscore, keys)) * scale).astype(BF16)
        dk = (nn(dscore, q2) * scale).astype(BF16)
        dv = nn(prob.astype(BF16), do2).astype(BF16)
        for i, ref in enumerate(dkv):
            ref[:, lanes] = dk[i * each : (i + 1) * each]
            ref[:, late] = dv[i * each : (i + 1) * each]


def project_back_body(plan, meta, ins, weight, outs, own):
    dq = ins[0]
    dqkv_ref, da_ref, sum_ref = outs
    n = plan.heads_width
    dkv = ins[1][: plan.rows].astype(F32)
    for term in ins[2:]:
        dkv = dkv + term[: plan.rows].astype(F32)
    dkv = dkv.astype(BF16)
    dqkv_ref[:, :n] = dq[...]
    dqkv_ref[:, n:] = dkv
    da_ref[...] = nt(dqkv_ref[...], weight(0)[...]).astype(BF16)
    sums = [
        jnp.sum(dq[...].astype(F32), axis=0, keepdims=True),
        jnp.sum(dkv[:, n:].astype(F32), axis=0, keepdims=True),
    ]
    sum_ref[...] = rows_of([jnp.concatenate(sums, axis=1)], 8, 2 * n)


def weight_grad_body(plan, widths, relative, meta, ins, weight, outs, own):
    packet, sems = own
    column, copies = 0, []
    for i, width in enumerate(widths):
        left, right = ins[2 * i], ins[2 * i + 1]
        turned = left[...].T
        for j in range(0, width, CHUNK):
            size = min(CHUNK, width - j)
            window = pl.ds(column, size)
            packet[:, column : column + size] = nn(turned, right[:, j : j + size]).astype(BF16)
            column += size
            if len(outs) == 1:
                copy = pltpu.make_async_copy(packet.at[:, window], outs[0].at[:, window], sems.at[len(copies)])
                copy.start()
                copies.append(copy)
                continue
            for place, offset in enumerate(ORDER):
                for k in range(plan.shards):
                    z = lax.rem(meta[0] + k, plan.shards) if relative else k
                    index = z * plan.contexts + jnp.bitwise_xor(meta[1], offset)
                    row = pl.multiple_of(index * plan.block, 16)
                    copy = pltpu.make_async_copy(
                        packet.at[pl.ds(row, plan.block), window],
                        outs[place // 2].at[place % 2, k, :, window],
                        sems.at[len(copies)],
                    )
                    copy.start()
                    copies.append(copy)
    for copy in copies:
        copy.wait()


def end_body(plan, meta, ins, weight, outs, own):
    da, da_far, dx_mid, x, vec = ins[:5]
    feed0, attn0, proj0, feed1, attn1, proj1 = ins[5:]
    gy_ref, small_ref = outs
    grad = da[...].astype(F32) + da_far[...].astype(F32)
    back, gain_sum = norm_back(x[...], vec[:1, :], grad)
    gy = dx_mid[...] + back
    gy_ref[...] = gy
    lane = lax.broadcasted_iota(jnp.int32, (1, plan.rows), 1)
    seg = segment(plan, meta, meta[1] * plan.rows + lane)
    member = (seg == lax.broadcasted_iota(jnp.int32, (16, plan.rows), 0)).astype(F32)
    sums = lax.dot_general(
        member, gy, (((1,), (0,)), ((), ())), precision=lax.Precision.HIGHEST, preferred_element_type=F32
    )
    halves = plan.hidden // plan.width
    parts = [sums]
    for gain_row, feed, attn, proj in (
        (gain_sum, feed0, attn0, proj0),
        (feed0[1 + halves : 2 + halves, :], feed1, attn1, proj1),
    ):
        parts += [gain_row, attn[0:1, :], attn[1:2, :], feed[0:1, :]]
        parts += [feed[1 + i : 2 + i, :] for i in range(halves)]
        parts += [proj[0:1, :]]
    small_ref[...] = rows_of_total(parts, 32, plan.width).astype(BF16)


def rows_of_total(parts, count, width):
    have = sum(part.shape[0] for part in parts)
    return jnp.concatenate(parts + [jnp.zeros((count - have, width), F32)], axis=0)


def swap_core(array):
    return lax.ppermute(array, "ctx", [(i, i ^ 1) for i in range(4)])


def swap_chip(array):
    return lax.ppermute(array, "ctx", [(i, i ^ 2) for i in range(4)])


def swap_tp(array):
    return lax.ppermute(array, "tp", [(0, 1), (1, 0)])


def to_shard(plan, array, shift):
    n = plan.shards
    return lax.ppermute(array, "shard", [(i, (i + shift) % n) for i in range(n)])


def stage_of(plan, thing, *names):
    if not plan.blocks:
        return ()
    found = [getattr(thing, name) for name in names]
    return tuple(array for one in found for array in (one if isinstance(one, tuple) else (one,)))


class Gather:
    def __init__(self, plan, packets, *ties):
        self.plan = plan
        if plan.blocks:
            packets = after_all(packets, *ties) if ties else tuple(packets)
            got = [to_shard(plan, packets[k], k) for k in range(1, plan.shards)]
            self.got = tuple(got)
            self.blocks = (packets[0], *got)
        else:
            self.arrays = (lax.all_gather(packets[0], ("shard", "ctx"), axis=0, tiled=True),)

    @classmethod
    def at_once(cls, plan, packet, *ties):
        self = cls.__new__(cls)
        self.plan = plan
        if plan.blocks:
            copies = jnp.broadcast_to(after(packet, *ties), (plan.shards, *packet.shape))
            self.stack = lax.all_to_all(copies, "shard", 0, 0, tiled=True)
        else:
            self.arrays = (lax.all_gather(packet, ("shard", "ctx"), axis=0, tiled=True),)
        return self

    def along(self, *ties):
        if self.plan.blocks:
            self.stack = jnp.stack(after_all(self.blocks, *ties) if ties else self.blocks)
        return self

    def across(self, *ties):
        if self.plan.blocks:
            self.far = swap_chip(after(self.stack, *ties) if ties else self.stack)
        return self

    def cores(self, *ties):
        if self.plan.blocks:
            halves = (self.stack, self.far)
            sent = after_all(halves, *ties) if ties else halves
            self.arrays = (*halves, *[swap_core(half) for half in sent])
        return self


def gather_keys(plan, kv):
    if plan.blocks:
        far = swap_chip(kv)
        return (kv, far, swap_core(kv), swap_core(far))
    return (lax.all_gather(kv, "ctx", axis=0, tiled=True),)


def after(array, *others):
    return lax.optimization_barrier((array, *others))[0]


def after_all(arrays, *others):
    return lax.optimization_barrier((*arrays, *others))[: len(arrays)]


def add(*terms):
    total = terms[0].astype(F32)
    for term in terms[1:]:
        total = total + term.astype(F32)
    return total


def weight_grads(plan, meta, name, pairs, blocks, relative=False):
    widths = tuple(right.shape[1] for _, right in pairs)
    width = sum(widths)
    copies = sum(pl.cdiv(width, CHUNK) for width in widths)
    if blocks:
        outs = [shape(2, plan.shards, plan.block, width)] * 2
        copies *= plan.shards * 4
    else:
        outs = [shape(plan.width, width)]
    return run(
        plan,
        functools.partial(weight_grad_body, plan, widths, relative),
        name,
        meta,
        [],
        [],
        outs,
        2 * plan.rows * plan.width * width,
        kept=[array for pair in pairs for array in pair],
        scratch=[pltpu.VMEM((plan.width, width), BF16), pltpu.SemaphoreType.DMA((copies,))],
        direct=tuple(range(len(outs))),
    )


class Reduction:
    def __init__(self, plan, meta, name, pairs, blocks=True, relative=False):
        self.blocks = blocks and plan.blocks
        self.plan, self.relative = plan, relative
        parts = weight_grads(plan, meta, name, pairs, self.blocks, relative)
        if self.blocks:
            self.keep, self.send = parts
        else:
            self.send = parts[0]
            total = lax.psum_scatter(parts[0], ("shard", "ctx"), scatter_dimension=0, tiled=True)
            self.total = total

    def core(self, *ties):
        if self.blocks:
            self.near = swap_core(after(self.send, *ties))
        return self

    def pairs(self, *ties):
        if self.blocks:
            self.near = after(self.near, *ties)
            self.pair = add(self.keep[1], self.near[1]).astype(BF16)
            self.far = swap_chip(self.pair)
        return self

    def along(self, *ties):
        if self.blocks:
            far = after(self.far, *ties) if ties else self.far
            if self.relative:
                n = self.plan.shards
                self.sums = tuple(
                    add(self.keep[0, k], self.near[0, k], far[k]).astype(BF16) for k in range(n)
                )
                self.got = (self.sums[0], *[to_shard(self.plan, self.sums[k], k) for k in range(1, n)])
            else:
                self.sums = add(self.keep[0], self.near[0], far).astype(BF16)
                self.got = lax.all_to_all(self.sums, "shard", 0, 0, tiled=True)
        return self

    def end(self, *ties):
        if not self.blocks:
            return (after(self.total, *ties) if self.plan.blocks else self.total).astype(F32)
        if self.relative:
            return add(*after_all(self.got, *ties))
        return jnp.sum(after(self.got, *ties).astype(F32), axis=0)


def per_device(
    tokens,
    timesteps,
    cont_lengths,
    table,
    w_qkv,
    w_out,
    w_up,
    w_down,
    norms,
    query_bias,
    value_bias,
    up_bias,
    out_biases,
    cotangent,
):
    rows, width = tokens.shape
    layers, block = w_qkv.shape[:2]
    heads_width, hidden = w_qkv.shape[3], w_up.shape[2]
    shards, contexts = lax.axis_size("shard"), lax.axis_size("ctx")
    conts = cont_lengths.shape[1]
    plan = Plan(rows, width, block, heads_width, hidden, shards, contexts, conts)
    z, c = lax.axis_index("shard"), lax.axis_index("ctx")
    meta = jnp.concatenate([jnp.stack([z, c]).astype(jnp.int32), jnp.cumsum(cont_lengths[0])])

    n3 = 3 * heads_width

    def everywhere(packet):
        return (lax.all_gather(packet, ("shard", "ctx"), axis=0, tiled=True),)

    upper = jnp.concatenate([w_qkv[1].reshape(block, -1), w_out[1], w_up[1], w_down[1]], axis=1)
    first = jnp.concatenate([w_qkv[0].reshape(block, -1), w_out[0]], axis=1)
    steps = after(timesteps, first)
    first = Gather(plan, [first] * shards)

    vectors = jnp.concatenate(
        [norms[0], norms[1], out_biases[0], out_biases[1]], axis=1
    )
    seqs = conts + 1
    steps_back = jnp.concatenate([steps] + [to_shard(plan, steps, k) for k in range(1, shards)])
    steps_near = jnp.concatenate([steps_back[:1], steps_back[:0:-1]]).reshape(-1)
    one_hot = (steps_near[:, None] == jnp.arange(table.shape[0], dtype=jnp.int32)[None, :]).astype(BF16)
    looked = lax.dot_general(
        table, one_hot, (((0,), (1,)), ((), ())), preferred_element_type=F32
    ).astype(BF16)
    blank = jnp.zeros((block, LANES - vectors.shape[1] - seqs), BF16)
    if plan.blocks:
        small = [
            jnp.concatenate([vectors, looked[:, k * seqs : (k + 1) * seqs], blank], axis=1)
            for k in range(shards)
        ]
        small = Gather(plan, small)
        first.along(*small.got)
        ties = (first.stack,)
        small = small.along().across().cores().arrays
    else:
        looked = jnp.roll(looked.reshape(block, shards, seqs), z, axis=1).reshape(block, -1)
        every = lax.all_gather(jnp.concatenate([vectors, looked], axis=1), ("shard", "ctx"), axis=0, tiled=True)
        mine = lax.dynamic_slice_in_dim(every, 8 + z * seqs, seqs, axis=1)
        blank = jnp.zeros((width, LANES - 8 - seqs), BF16)
        small = [jnp.concatenate([every[:, :8], mine, blank], axis=1)]
        ties = ()
    second = Gather(plan, [w_up[0]] * shards, *ties)
    third = Gather.at_once(plan, w_down[0], *ties)
    first.across().cores(*stage_of(plan, second, "got"))
    upper = everywhere(after(upper, *ties))

    mm = 2 * rows * width
    full = shape(rows, width, dtype=F32)
    low = shape(rows, width)
    heads = shape(rows, heads_width)
    wide = shape(rows, hidden)
    sums = shape(8, width, dtype=F32)
    qkv_outs = [low, heads, shape(rows, 2 * heads_width)]
    attn_flops = 4 * rows * plan.group * heads_width

    saved = []
    x_mid = part = part_far = None
    for layer in range(layers):
        last = layer == layers - 1
        ties = ()
        if layer == 0:
            x, vec, a, q, kv = run(
                plan,
                functools.partial(embed_body, plan),
                "embed",
                meta,
                [tokens, query_bias, value_bias],
                [(first.arrays, 0, n3), (small, 0, LANES)],
                [full, sums, *qkv_outs],
                mm * n3,
                ties=stage_of(plan, second, "got"),
            )
            second.along(kv).across()
            ties = stage_of(plan, second, "stack") + stage_of(plan, third, "stack")
            of_attn = [(first.arrays, 0, n3), (first.arrays, n3, heads_width)]
        else:
            of_attn = [(upper, 0, n3), (upper, n3, heads_width)]
            of_feed = [(upper, n3 + heads_width + i * hidden, hidden) for i in range(2)]
            x, a, q, kv = run(
                plan,
                functools.partial(next_body, plan, layer),
                "project",
                meta,
                [x_mid, part, part_far, vec, query_bias, value_bias],
                of_attn[:1],
                [full, *qkv_outs],
                mm * n3,
            )
        kvs = gather_keys(plan, kv)
        part, o, total, kv_all = run(
            plan,
            functools.partial(attend_body, plan),
            "attend",
            meta,
            [q, *kvs],
            of_attn[1:],
            [low, heads, shape(8, 2 * rows, dtype=F32), shape(plan.group, 2 * heads_width)],
            mm * heads_width + attn_flops,
            ties=ties,
        )
        part_far = swap_tp(part)
        if layer == 0:
            second.cores(part)
            third.across(part).cores(part_far)
            of_feed = [(second.arrays, 0, hidden), (third.arrays, 0, hidden, True)]
        outs = [full, low, wide, shape(rows, hidden, dtype=F32), low]
        if last:
            outs += [wide, low, sums]
        got = run(
            plan,
            functools.partial(feed_body, plan, layer, last),
            "feed",
            meta,
            [x, part, part_far, vec, up_bias] + ([cotangent] if last else []),
            of_feed,
            outs,
            mm * hidden * (4 if last else 2),
        )
        x_mid, b, gelu, slope, part = got[:5]
        part_far = swap_tp(part)
        saved.append((x, a, q, kv_all, o, total, x_mid, b, gelu, slope, of_attn, of_feed))

    gy = dy = cotangent
    dh, db, feed_sum = got[5:]
    final = (x_mid, part, part_far)
    bias_last = vec[2 * layers + 3][None, :]
    small_sums = [None] * layers
    above = None
    for layer in reversed(range(layers)):
        x, a, q, kv_all, o, total, x_mid, b, gelu, slope, of_attn, of_feed = saved[layer]
        if above is not None:
            gy, dy, dh, db, feed_sum = run(
                plan,
                functools.partial(between_body, plan, layer),
                "feed_back",
                meta,
                [da, da_far],
                of_feed,
                [full, low, wide, low, sums],
                2 * mm * hidden,
                kept=[dx_mid, saved[layer + 1][0], vec, slope],
                limit=LIMIT_FB,
                ties=stage_of(plan, above, "send"),
            )
        db_far = swap_tp(db)
        if above is None:
            upper_feed = Reduction(plan, meta, "feed_grad", [(b, dh), (dy, gelu)], blocks=False)
            ties = stage_of(plan, upper_feed, "send")
        else:
            feeds = [
                Reduction(plan, meta, "up_grad", [(b, dh)], relative=True).core(db_far),
                Reduction(plan, meta, "down_grad", [(dy, gelu)]).core(db_far),
            ]
            ties = stage_of(plan, feeds[0], "send") + stage_of(plan, feeds[1], "send")
        if plan.blocks:
            dkv_outs = [shape(2 * rows, 2 * heads_width)] * 2
        else:
            dkv_outs = [shape(plan.group, 2 * heads_width)]
        dx_mid, dz, dq, attn_sum, *dkv = run(
            plan,
            functools.partial(attend_back_body, plan, layer),
            "attend_back",
            meta,
            [gy, db, db_far],
            of_attn[1:],
            [full, low, heads, sums, *dkv_outs],
            mm * heads_width + 10 * rows * plan.group * heads_width,
            ties=ties,
            kept=[x_mid, vec, q, total, kv_all],
        )
        ties = ()
        if plan.blocks:
            keep, send = dkv
            near = swap_core(send)
            summed = add(keep[rows:], near[rows:]).astype(BF16)
            terms = [keep, near, swap_chip(summed)]
        else:
            terms = [lax.psum_scatter(dkv[0], "ctx", scatter_dimension=0, tiled=True)]
            summed = terms[0]
        if above is not None:
            for one in (above, *feeds):
                one.pairs(summed)
                ties += stage_of(plan, one, "pair")
        dqkv, da, proj_sum = run(
            plan,
            functools.partial(project_back_body, plan),
            "project_back",
            meta,
            [dq, *terms],
            of_attn[:1],
            [shape(rows, n3), low, shape(8, 2 * heads_width, dtype=F32)],
            mm * n3,
            ties=ties,
        )
        da_far = swap_tp(da)
        attn = Reduction(plan, meta, "attn_grad", [(a, dqkv), (dz, o)], relative=above is not None).core(da_far)
        if above is not None:
            above.along(da)
            end_ties = stage_of(plan, attn, "send") + stage_of(plan, above, "sums") + stage_of(plan, feeds[0], "far")
            upper_attn = above
        above = attn
        small_sums[layer] = [feed_sum, attn_sum, proj_sum]

    grad_tokens, packet = run(
        plan,
        functools.partial(end_body, plan),
        "end",
        meta,
        [da, da_far],
        [],
        [full, shape(32, width)],
        mm * 32,
        ties=end_ties,
        kept=[dx_mid, saved[0][0], vec, *small_sums[0], *small_sums[1]],
    )
    attn.pairs(packet, *stage_of(plan, feeds[0], "far"))
    feeds[0].along(packet, *stage_of(plan, upper_attn, "sums"), *stage_of(plan, upper_feed, "total"))
    feeds[1].along(*stage_of(plan, feeds[0], "sums"), *stage_of(plan, attn, "pair"))
    attn.along(*stage_of(plan, feeds[1], "sums"), *stage_of(plan, feeds[0], "got"))
    x_mid, part, part_far = after_all(final, packet)
    activations = (x_mid + add(part, part_far) + bias_last).astype(BF16)
    start = (z * contexts + c) * block
    if plan.blocks:
        packet = add(packet, swap_core(packet)).astype(BF16)
        far = after(swap_chip(packet), *attn.sums)
        packet = add(packet, far).astype(BF16)
        got = jnp.stack([packet] + [to_shard(plan, packet, k) for k in range(1, shards)])
        other = add(*[got[k] for k in range(0, shards, 2)]) + add(*[got[k] for k in range(1, shards, 2)])
    else:
        packet = lax.psum(packet, "ctx")
        got = lax.all_gather(packet, "shard", axis=0)
        other = jnp.sum(got.astype(F32), axis=0)
        steps_back = jnp.roll(steps_back[::-1], z + 1, axis=0)
    mine = lax.dynamic_slice_in_dim(got[:, :seqs], start, block, axis=2).reshape(-1, block)
    one_hot = (jnp.arange(table.shape[0], dtype=jnp.int32)[:, None] == steps_back.reshape(-1)[None, :]).astype(BF16)
    grad_table = jnp.dot(one_hot, mine, preferred_element_type=F32)

    upper_feed, upper_attn = upper_feed.end(packet), upper_attn.end(packet)
    halves = hidden // width
    per_layer = 5 + halves
    by_layer = other[16 : 16 + layers * per_layer].reshape(layers, per_layer, width)
    local = lax.dynamic_slice_in_dim(by_layer[:, :4], start, block, axis=2)
    grad_norms = jnp.moveaxis(local[:, :2], 1, 2)
    grad_out_biases = jnp.moveaxis(local[:, 2:], 1, 2)
    grad_up_bias = by_layer[:, 4 : 4 + halves].reshape(layers, hidden)
    grad_query_bias = by_layer[:, 4 + halves, :heads_width]
    grad_value_bias = by_layer[:, 4 + halves, heads_width:]
    ups = [feeds[0].end(), upper_feed[:, :hidden]]
    downs = [feeds[1].end(), upper_feed[:, hidden:]]
    attns = [attn.end(), upper_attn]
    return (
        activations,
        grad_tokens,
        jnp.stack([g[:, :n3].reshape(block, 3, heads_width) for g in attns]),
        jnp.stack([g[:, n3:] for g in attns]),
        jnp.stack(ups),
        jnp.stack(downs),
        grad_norms,
        grad_table,
        grad_query_bias,
        grad_value_bias,
        grad_up_bias,
        grad_out_biases,
    )


def solution(mesh):
    placed = (
        P(("shard", "ctx"), None),
        P("shard", None),
        P("shard", None),
        P(None, ("shard", "ctx")),
        P(None, ("shard", "ctx"), None, "tp"),
        P(None, ("shard", "ctx"), "tp"),
        P(None, ("shard", "ctx"), "tp"),
        P(None, ("shard", "ctx"), "tp"),
        P(None, ("shard", "ctx"), None),
        P(None, "tp"),
        P(None, "tp"),
        P(None, "tp"),
        P(None, ("shard", "ctx"), None),
        P(("shard", "ctx"), None),
    )
    return jax.shard_map(
        per_device,
        mesh=mesh,
        in_specs=placed,
        out_specs=(
            P(("shard", "ctx"), None),
            P(("shard", "ctx"), None),
            P(None, ("shard", "ctx"), None, "tp"),
            P(None, ("shard", "ctx"), "tp"),
            P(None, ("shard", "ctx"), "tp"),
            P(None, ("shard", "ctx"), "tp"),
            P(None, ("shard", "ctx"), None),
            P(None, ("shard", "ctx")),
            P(None, "tp"),
            P(None, "tp"),
            P(None, "tp"),
            P(None, ("shard", "ctx"), None),
        ),
        check_vma=False,
    )
```

```python
import functools
import math

import jax
import jax.numpy as jnp
from jax import lax
from jax.experimental import pallas as pl
from jax.experimental.pallas import tpu as pltpu
from jax.sharding import PartitionSpec as P

HEAD_DIM = 64
EPSILON = 1e-05
NEGATIVE = -1e30
F32 = jnp.float32
BF16 = jnp.bfloat16
LANES = 128
CHUNK = 512
SPLIT = 3
VMEM_LIMIT = 46 * 1024 * 1024
LIMIT_FB = 52 * 1024 * 1024
ORDER = (0, 2, 1, 3)


def nn(a, b):
    return lax.dot_general(a, b, (((1,), (0,)), ((), ())), preferred_element_type=F32)


def nt(a, b):
    return lax.dot_general(a, b, (((1,), (1,)), ((), ())), preferred_element_type=F32)


def tn(a, b):
    return lax.dot_general(a, b, (((0,), (0,)), ((), ())), preferred_element_type=F32)


def normed_rows(values):
    centered = values - jnp.mean(values, axis=-1, keepdims=True)
    scale = lax.rsqrt(jnp.mean(centered * centered, axis=-1, keepdims=True) + EPSILON)
    return centered * scale, scale


def norm_back(values, gain, grad):
    hat, scale = normed_rows(values)
    grad_gain = jnp.sum(grad * hat, axis=0, keepdims=True)
    inner = grad * gain
    along = jnp.mean(inner * hat, axis=-1, keepdims=True)
    centre = jnp.mean(inner, axis=-1, keepdims=True)
    return scale * (inner - centre - hat * along), grad_gain


def rows_of(parts, count, width):
    have = len(parts)
    if have < count:
        parts = list(parts) + [jnp.zeros((count - have, width), F32)]
    return jnp.concatenate(parts, axis=0)


class Plan:
    def __init__(self, rows, width, block, heads_width, hidden, shards, contexts, conts):
        self.rows, self.width, self.block = rows, width, block
        self.heads_width, self.hidden = heads_width, hidden
        self.shards, self.contexts, self.conts = shards, contexts, conts
        self.group = rows * contexts
        self.blocks = contexts == 4 and block % 16 == 0


def run(plan, body, name, meta, inputs, weights, outs, flops, scratch=(), direct=(), ties=(), kept=(), limit=VMEM_LIMIT):
    if ties:
        inputs = [after(inputs[0], *ties), *inputs[1:]]
    n_in, n_out = len(inputs), len(outs)
    counts = [len(entry[0]) for entry in weights]
    per_block = plan.shards * len(ORDER) * SPLIT
    copies = sum(1 if n == 1 else per_block for n in counts) + len(kept)

    def kernel(meta_ref, *refs):
        ins = refs[:n_in]
        at = n_in
        sources = []
        for n in counts:
            sources.append(refs[at : at + n])
            at += n
        lying = refs[at : at + len(kept)]
        at += len(kept)
        results = refs[at : at + n_out]
        at += n_out
        held = refs[at : at + len(weights)]
        at += len(weights)
        brought = refs[at : at + len(kept)]
        at += len(kept)
        sems = refs[at] if copies else None
        own = refs[at + 1 :] if copies else refs[at:]
        started, slot = [], 0
        bringing = []
        for ref, into in zip(lying, brought):
            bringing.append(pltpu.make_async_copy(ref, into, sems.at[slot]))
            slot += 1
        for copy in bringing:
            copy.start()
        for (_, column, width, *whole), refs_of, into in zip(weights, sources, held):
            group = []
            columns = pl.ds(column, width)
            split = math.gcd(width // LANES, SPLIT)
            if len(refs_of) == 1:
                group.append(pltpu.make_async_copy(refs_of[0].at[:, columns], into, sems.at[slot]))
                slot += 1
            else:
                for place, offset in enumerate(ORDER):
                    for shift in range(plan.shards):
                        ref = refs_of[place].at[shift]
                        z = shift if whole else lax.rem(meta_ref[0] + (plan.shards - shift), plan.shards)
                        index = z * plan.contexts + jnp.bitwise_xor(meta_ref[1], offset)
                        row = pl.multiple_of(index * plan.block, 16)
                        for part in range(0, width, width // split):
                            group.append(
                                pltpu.make_async_copy(
                                    ref.at[:, pl.ds(column + part, width // split)],
                                    into.at[pl.ds(row, plan.block), pl.ds(part, width // split)],
                                    sems.at[slot],
                                )
                            )
                            slot += 1
            for copy in group:
                copy.start()
            started.append(group)

        def weight(i):
            for copy in started[i]:
                copy.wait()
            return held[i]

        for copy in bringing:
            copy.wait()
        body(meta_ref, (*ins, *brought), weight, results, own)

    vmem = pl.BlockSpec(memory_space=pltpu.VMEM)
    anywhere = pl.BlockSpec(memory_space=pl.ANY)
    outside = pl.BlockSpec(memory_space=pltpu.HBM)
    scratch_shapes = [pltpu.VMEM((plan.width, entry[2]), BF16) for entry in weights]
    scratch_shapes += [pltpu.VMEM(array.shape, array.dtype) for array in kept]
    if copies:
        scratch_shapes.append(pltpu.SemaphoreType.DMA((copies,)))
    moved = sum(x.size * x.dtype.itemsize for x in inputs)
    moved += sum(math.prod(o.shape) * o.dtype.itemsize for o in outs)
    moved += sum(plan.width * entry[2] * 2 for entry in weights)
    call = pl.pallas_call(
        kernel,
        name=name,
        out_shape=tuple(outs),
        in_specs=[pl.BlockSpec(memory_space=pltpu.SMEM)]
        + [vmem] * n_in
        + [outside if n == 1 else anywhere for n in counts for _ in range(n)]
        + [anywhere] * len(kept),
        out_specs=tuple(outside if i in direct else vmem for i in range(n_out)),
        scratch_shapes=scratch_shapes + list(scratch),
        compiler_params=pltpu.CompilerParams(vmem_limit_bytes=limit),
        cost_estimate=pl.CostEstimate(flops=flops, bytes_accessed=moved, transcendentals=0),
    )
    return call(meta, *inputs, *[array for entry in weights for array in entry[0]], *kept)


def shape(*dims, dtype=BF16):
    return jax.ShapeDtypeStruct(dims, dtype)


def segment(plan, meta, position):
    prompt = plan.group // 2
    seg = jnp.ones(position.shape, jnp.int32)
    for j in range(plan.conts):
        seg = seg + (position - prompt >= meta[2 + j]).astype(jnp.int32)
    return jnp.where(position < prompt, 0, seg)


def key_positions(plan, meta):
    if not plan.blocks:
        return lax.broadcasted_iota(jnp.int32, (plan.group, 1), 0)
    inside = lax.broadcasted_iota(jnp.int32, (plan.rows, 1), 0)
    return jnp.concatenate(
        [inside + jnp.bitwise_xor(meta[1], d) * plan.rows for d in ORDER], axis=0
    )


def allowed_keys(plan, meta):
    lane = lax.broadcasted_iota(jnp.int32, (1, 2 * plan.rows), 1)
    query = meta[1] * plan.rows + jnp.where(lane >= plan.rows, lane - plan.rows, lane)
    seg_query = segment(plan, meta, query)
    seg_key = segment(plan, meta, key_positions(plan, meta))
    return (seg_key == 0) | (seg_key == seg_query)


def pair_rows(values):
    first = lax.broadcasted_iota(jnp.int32, values.shape, 1) < HEAD_DIM
    none = jnp.zeros_like(values)
    return jnp.concatenate([jnp.where(first, values, none), jnp.where(first, none, values)], axis=0)


def pair_lanes(values):
    rows = values.shape[0] // 2
    first = lax.broadcasted_iota(jnp.int32, (rows, LANES), 1) < HEAD_DIM
    return jnp.where(first, values[:rows], values[rows:])


def write_qkv(plan, layer, x, gain, weight, q_bias, v_bias, a_ref, q_ref, kv_ref):
    n = plan.heads_width
    hat, _ = normed_rows(x)
    a = (hat * gain).astype(BF16)
    a_ref[...] = a
    bias_q = q_bias[...].astype(F32)[layer : layer + 1]
    bias_v = v_bias[...].astype(F32)[layer : layer + 1]
    kv_ref[:, :n] = nn(a, weight[:, n : 2 * n]).astype(BF16)
    kv_ref[:, n:] = (nn(a, weight[:, 2 * n :]) + bias_v).astype(BF16)
    q_ref[...] = (nn(a, weight[:, :n]) + bias_q).astype(BF16)


def embed_body(plan, meta, ins, weight, outs, own):
    tokens, q_bias, v_bias = ins
    x_ref, vec_ref, a_ref, q_ref, kv_ref = outs
    small = weight(1)[...].astype(F32).T
    vec_ref[...] = small[:8]
    lookup = small[8:24].astype(BF16)
    inside = lax.broadcasted_iota(jnp.int32, (plan.rows, 1), 0)
    seg = segment(plan, meta, meta[1] * plan.rows + inside)
    member = seg == lax.broadcasted_iota(jnp.int32, (plan.rows, 16), 1)
    x = tokens[...].astype(F32) + nn(member.astype(F32).astype(BF16), lookup)
    x_ref[...] = x
    write_qkv(plan, 0, x, small[:1], weight(0), q_bias, v_bias, a_ref, q_ref, kv_ref)


def next_body(plan, layer, meta, ins, weight, outs, own):
    x_mid, part, part_far, vec, q_bias, v_bias = ins
    x_ref, a_ref, q_ref, kv_ref = outs
    x = x_mid[...] + (part[...].astype(F32) + part_far[...].astype(F32))
    x = x + vec[2 * layer + 3 : 2 * layer + 4, :]
    x_ref[...] = x
    gain = vec[2 * layer : 2 * layer + 1, :]
    write_qkv(plan, layer, x, gain, weight(0), q_bias, v_bias, a_ref, q_ref, kv_ref)


def attend_body(plan, meta, ins, weight, outs, own):
    q_ref, kvs = ins[0], ins[1:]
    part_ref, o_ref, total_ref, all_ref = outs
    n = plan.heads_width
    for i, kv in enumerate(kvs):
        all_ref[i * kv.shape[0] : (i + 1) * kv.shape[0], :] = kv[...]
    allowed = allowed_keys(plan, meta)
    totals = []
    for pair in range(n // LANES):
        lanes = slice(pair * LANES, (pair + 1) * LANES)
        late = slice(n + pair * LANES, n + (pair + 1) * LANES)
        q2 = pair_rows(q_ref[:, lanes])
        keys = jnp.concatenate([kv[:, lanes] for kv in kvs], axis=0)
        values = jnp.concatenate([kv[:, late] for kv in kvs], axis=0)
        scores = jnp.where(allowed, nt(keys, q2) * (1.0 / math.sqrt(HEAD_DIM)), NEGATIVE)
        top = jnp.max(scores, axis=0, keepdims=True)
        exps = jnp.exp(scores - top)
        total = jnp.sum(exps, axis=0, keepdims=True)
        prob = (exps * (1.0 / total)).astype(BF16)
        o_ref[:, lanes] = pair_lanes(tn(prob, values)).astype(BF16)
        totals.append(top + jnp.log(total))
    total_ref[...] = rows_of(totals, 8, 2 * plan.rows)
    part_ref[...] = nt(o_ref[...], weight(0)[...]).astype(BF16)


def feed_body(plan, layer, last, meta, ins, weight, outs, own):
    x, part, part_far, vec, bias = ins[:5]
    mid_ref, b_ref, gelu_ref, slope_ref, part_ref = outs[:5]
    x_mid = x[...] + (part[...].astype(F32) + part_far[...].astype(F32))
    x_mid = x_mid + vec[2 * layer + 4 : 2 * layer + 5, :]
    mid_ref[...] = x_mid
    hat, _ = normed_rows(x_mid)
    b = (hat * vec[2 * layer + 1 : 2 * layer + 2, :]).astype(BF16)
    b_ref[...] = b
    bias_f = bias[...].astype(F32)[layer : layer + 1]
    up = weight(0)
    chunks = [slice(i, min(i + CHUNK, plan.hidden)) for i in range(0, plan.hidden, CHUNK)]
    for columns in chunks:
        hidden = nn(b, up[:, columns]) + bias_f[:, columns]
        half = 0.5 * (1.0 + lax.erf(hidden * math.sqrt(0.5)))
        gelu_ref[:, columns] = (hidden * half).astype(BF16)
        bell = jnp.exp(hidden * hidden * -0.5) * (1.0 / math.sqrt(2.0 * math.pi))
        slope_ref[:, columns] = half + hidden * bell
    down = weight(1)
    if last:
        back_feed(plan, ins[5][...], slope_ref, up, down, outs[5], outs[6], outs[7], ins[5][...].astype(F32), None)
    part_ref[...] = nt(gelu_ref[...], down[...]).astype(BF16)


def back_feed(plan, dy, slope, up, down, dh_ref, db_ref, sum_ref, gradient, extra):
    sums = []
    total = None
    for i in range(0, plan.hidden, CHUNK):
        columns = slice(i, min(i + CHUNK, plan.hidden))
        dh = (nn(dy, down[:, columns]) * slope[:, columns]).astype(BF16)
        dh_ref[:, columns] = dh
        sums.append(jnp.sum(dh.astype(F32), axis=0, keepdims=True))
        term = nt(dh, up[:, columns])
        total = term if total is None else total + term
    db_ref[...] = total.astype(BF16)
    bias_sum = jnp.concatenate(sums, axis=1)
    parts = [jnp.sum(gradient, axis=0, keepdims=True)]
    for i in range(plan.hidden // plan.width):
        parts.append(bias_sum[:, i * plan.width : (i + 1) * plan.width])
    if extra is not None:
        parts.append(extra)
    sum_ref[...] = rows_of(parts, 8, plan.width)


def between_body(plan, layer, meta, ins, weight, outs, own):
    da, da_far, dx_mid, x_above, vec, slope = ins
    gy_ref, dy_ref, dh_ref, db_ref, sum_ref = outs
    grad = da[...].astype(F32) + da_far[...].astype(F32)
    back, gain_sum = norm_back(x_above[...], vec[2 * layer + 2 : 2 * layer + 3, :], grad)
    gy = dx_mid[...] + back
    gy_ref[...] = gy
    dy = gy.astype(BF16)
    dy_ref[...] = dy
    back_feed(plan, dy, slope, weight(0), weight(1), dh_ref, db_ref, sum_ref, gy, gain_sum)


def attend_back_body(plan, layer, meta, ins, weight, outs, own):
    gy, db, db_far, x_mid, vec, q_ref, total = ins[:7]
    kvs = ins[7:]
    mid_ref, dz_ref, dq_ref, sum_ref = outs[:4]
    dkv = outs[4:]
    n = plan.heads_width
    scale = 1.0 / math.sqrt(HEAD_DIM)
    grad = db[...].astype(F32) + db_far[...].astype(F32)
    back, gain_sum = norm_back(x_mid[...], vec[2 * layer + 1 : 2 * layer + 2, :], grad)
    dx_mid = gy[...].astype(F32) + back
    mid_ref[...] = dx_mid
    sum_ref[...] = rows_of([gain_sum, jnp.sum(dx_mid, axis=0, keepdims=True)], 8, plan.width)
    dz = dx_mid.astype(BF16)
    dz_ref[...] = dz
    do = nn(dz, weight(0)[...]).astype(BF16)
    allowed = allowed_keys(plan, meta)
    each = plan.group // len(dkv)
    for pair in range(n // LANES):
        lanes = slice(pair * LANES, (pair + 1) * LANES)
        late = slice(n + pair * LANES, n + (pair + 1) * LANES)
        q2 = pair_rows(q_ref[:, lanes])
        do2 = pair_rows(do[:, lanes])
        keys = jnp.concatenate([kv[:, lanes] for kv in kvs], axis=0)
        values = jnp.concatenate([kv[:, late] for kv in kvs], axis=0)
        prob = jnp.exp(nt(keys, q2) * scale - total[pair : pair + 1, :])
        prob = jnp.where(allowed, prob, 0.0)
        dprob = nt(values, do2)
        delta = jnp.sum(prob * dprob, axis=0, keepdims=True)
        dscore = (prob * (dprob - delta)).astype(BF16)
        dq_ref[:, lanes] = (pair_lanes(tn(dscore, keys)) * scale).astype(BF16)
        dk = (nn(dscore, q2) * scale).astype(BF16)
        dv = nn(prob.astype(BF16), do2).astype(BF16)
        for i, ref in enumerate(dkv):
            ref[:, lanes] = dk[i * each : (i + 1) * each]
            ref[:, late] = dv[i * each : (i + 1) * each]


def project_back_body(plan, meta, ins, weight, outs, own):
    dq = ins[0]
    dqkv_ref, da_ref, sum_ref = outs
    n = plan.heads_width
    dkv = ins[1][: plan.rows].astype(F32)
    for term in ins[2:]:
        dkv = dkv + term[: plan.rows].astype(F32)
    dkv = dkv.astype(BF16)
    dqkv_ref[:, :n] = dq[...]
    dqkv_ref[:, n:] = dkv
    da_ref[...] = nt(dqkv_ref[...], weight(0)[...]).astype(BF16)
    sums = [
        jnp.sum(dq[...].astype(F32), axis=0, keepdims=True),
        jnp.sum(dkv[:, n:].astype(F32), axis=0, keepdims=True),
    ]
    sum_ref[...] = rows_of([jnp.concatenate(sums, axis=1)], 8, 2 * n)


def weight_grad_body(plan, widths, relative, meta, ins, weight, outs, own):
    packet, sems = own
    column, copies = 0, []
    for i, width in enumerate(widths):
        left, right = ins[2 * i], ins[2 * i + 1]
        turned = left[...].T
        for j in range(0, width, CHUNK):
            size = min(CHUNK, width - j)
            window = pl.ds(column, size)
            packet[:, column : column + size] = nn(turned, right[:, j : j + size]).astype(BF16)
            column += size
            if len(outs) == 1:
                copy = pltpu.make_async_copy(packet.at[:, window], outs[0].at[:, window], sems.at[len(copies)])
                copy.start()
                copies.append(copy)
                continue
            for place, offset in enumerate(ORDER):
                for k in range(plan.shards):
                    z = lax.rem(meta[0] + k, plan.shards) if relative else k
                    index = z * plan.contexts + jnp.bitwise_xor(meta[1], offset)
                    row = pl.multiple_of(index * plan.block, 16)
                    copy = pltpu.make_async_copy(
                        packet.at[pl.ds(row, plan.block), window],
                        outs[place // 2].at[place % 2, k, :, window],
                        sems.at[len(copies)],
                    )
                    copy.start()
                    copies.append(copy)
    for copy in copies:
        copy.wait()


def end_body(plan, meta, ins, weight, outs, own):
    da, da_far, dx_mid, x, vec = ins[:5]
    feed0, attn0, proj0, feed1, attn1, proj1 = ins[5:]
    gy_ref, small_ref = outs
    grad = da[...].astype(F32) + da_far[...].astype(F32)
    back, gain_sum = norm_back(x[...], vec[:1, :], grad)
    gy = dx_mid[...] + back
    gy_ref[...] = gy
    lane = lax.broadcasted_iota(jnp.int32, (1, plan.rows), 1)
    seg = segment(plan, meta, meta[1] * plan.rows + lane)
    member = (seg == lax.broadcasted_iota(jnp.int32, (16, plan.rows), 0)).astype(F32)
    sums = lax.dot_general(
        member, gy, (((1,), (0,)), ((), ())), precision=lax.Precision.HIGHEST, preferred_element_type=F32
    )
    halves = plan.hidden // plan.width
    parts = [sums]
    for gain_row, feed, attn, proj in (
        (gain_sum, feed0, attn0, proj0),
        (feed0[1 + halves : 2 + halves, :], feed1, attn1, proj1),
    ):
        parts += [gain_row, attn[0:1, :], attn[1:2, :], feed[0:1, :]]
        parts += [feed[1 + i : 2 + i, :] for i in range(halves)]
        parts += [proj[0:1, :]]
    small_ref[...] = rows_of_total(parts, 32, plan.width).astype(BF16)


def rows_of_total(parts, count, width):
    have = sum(part.shape[0] for part in parts)
    return jnp.concatenate(parts + [jnp.zeros((count - have, width), F32)], axis=0)


def swap_core(array):
    return lax.ppermute(array, "ctx", [(i, i ^ 1) for i in range(4)])


def swap_chip(array):
    return lax.ppermute(array, "ctx", [(i, i ^ 2) for i in range(4)])


def swap_tp(array):
    return lax.ppermute(array, "tp", [(0, 1), (1, 0)])


def to_shard(plan, array, shift):
    n = plan.shards
    return lax.ppermute(array, "shard", [(i, (i + shift) % n) for i in range(n)])


def stage_of(plan, thing, *names):
    if not plan.blocks:
        return ()
    found = [getattr(thing, name) for name in names]
    return tuple(array for one in found for array in (one if isinstance(one, tuple) else (one,)))


class Gather:
    def __init__(self, plan, packets, *ties):
        self.plan = plan
        if plan.blocks:
            packets = after_all(packets, *ties) if ties else tuple(packets)
            got = [to_shard(plan, packets[k], k) for k in range(1, plan.shards)]
            self.got = tuple(got)
            self.blocks = (packets[0], *got)
        else:
            self.arrays = (lax.all_gather(packets[0], ("shard", "ctx"), axis=0, tiled=True),)

    @classmethod
    def at_once(cls, plan, packet, *ties):
        self = cls.__new__(cls)
        self.plan = plan
        if plan.blocks:
            copies = jnp.broadcast_to(after(packet, *ties), (plan.shards, *packet.shape))
            self.stack = lax.all_to_all(copies, "shard", 0, 0, tiled=True)
        else:
            self.arrays = (lax.all_gather(packet, ("shard", "ctx"), axis=0, tiled=True),)
        return self

    def along(self, *ties):
        if self.plan.blocks:
            self.stack = jnp.stack(after_all(self.blocks, *ties) if ties else self.blocks)
        return self

    def across(self, *ties):
        if self.plan.blocks:
            self.far = swap_chip(after(self.stack, *ties) if ties else self.stack)
        return self

    def cores(self, *ties):
        if self.plan.blocks:
            halves = (self.stack, self.far)
            sent = after_all(halves, *ties) if ties else halves
            self.arrays = (*halves, *[swap_core(half) for half in sent])
        return self


def gather_keys(plan, kv):
    if plan.blocks:
        far = swap_chip(kv)
        return (kv, far, swap_core(kv), swap_core(far))
    return (lax.all_gather(kv, "ctx", axis=0, tiled=True),)


def after(array, *others):
    return lax.optimization_barrier((array, *others))[0]


def after_all(arrays, *others):
    return lax.optimization_barrier((*arrays, *others))[: len(arrays)]


def add(*terms):
    total = terms[0].astype(F32)
    for term in terms[1:]:
        total = total + term.astype(F32)
    return total


def weight_grads(plan, meta, name, pairs, blocks, relative=False):
    widths = tuple(right.shape[1] for _, right in pairs)
    width = sum(widths)
    copies = sum(pl.cdiv(width, CHUNK) for width in widths)
    if blocks:
        outs = [shape(2, plan.shards, plan.block, width)] * 2
        copies *= plan.shards * 4
    else:
        outs = [shape(plan.width, width)]
    return run(
        plan,
        functools.partial(weight_grad_body, plan, widths, relative),
        name,
        meta,
        [],
        [],
        outs,
        2 * plan.rows * plan.width * width,
        kept=[array for pair in pairs for array in pair],
        scratch=[pltpu.VMEM((plan.width, width), BF16), pltpu.SemaphoreType.DMA((copies,))],
        direct=tuple(range(len(outs))),
    )


class Reduction:
    def __init__(self, plan, meta, name, pairs, blocks=True, relative=False):
        self.blocks = blocks and plan.blocks
        self.plan, self.relative = plan, relative
        parts = weight_grads(plan, meta, name, pairs, self.blocks, relative)
        if self.blocks:
            self.keep, self.send = parts
        else:
            self.send = parts[0]
            total = lax.psum_scatter(parts[0], ("shard", "ctx"), scatter_dimension=0, tiled=True)
            self.total = total

    def core(self, *ties):
        if self.blocks:
            self.near = swap_core(after(self.send, *ties))
        return self

    def pairs(self, *ties):
        if self.blocks:
            self.near = after(self.near, *ties)
            self.pair = add(self.keep[1], self.near[1]).astype(BF16)
            self.far = swap_chip(self.pair)
        return self

    def along(self, *ties):
        if self.blocks:
            far = after(self.far, *ties) if ties else self.far
            if self.relative:
                n = self.plan.shards
                self.sums = tuple(
                    add(self.keep[0, k], self.near[0, k], far[k]).astype(BF16) for k in range(n)
                )
                self.got = (self.sums[0], *[to_shard(self.plan, self.sums[k], k) for k in range(1, n)])
            else:
                self.sums = add(self.keep[0], self.near[0], far).astype(BF16)
                self.got = lax.all_to_all(self.sums, "shard", 0, 0, tiled=True)
        return self

    def end(self, *ties):
        if not self.blocks:
            return (after(self.total, *ties) if self.plan.blocks else self.total).astype(F32)
        if self.relative:
            return add(*after_all(self.got, *ties))
        return jnp.sum(after(self.got, *ties).astype(F32), axis=0)


def per_device(
    tokens,
    timesteps,
    cont_lengths,
    table,
    w_qkv,
    w_out,
    w_up,
    w_down,
    norms,
    query_bias,
    value_bias,
    up_bias,
    out_biases,
    cotangent,
):
    rows, width = tokens.shape
    layers, block = w_qkv.shape[:2]
    heads_width, hidden = w_qkv.shape[3], w_up.shape[2]
    shards, contexts = lax.axis_size("shard"), lax.axis_size("ctx")
    conts = cont_lengths.shape[1]
    plan = Plan(rows, width, block, heads_width, hidden, shards, contexts, conts)
    z, c = lax.axis_index("shard"), lax.axis_index("ctx")
    meta = jnp.concatenate([jnp.stack([z, c]).astype(jnp.int32), jnp.cumsum(cont_lengths[0])])

    n3 = 3 * heads_width

    def everywhere(packet):
        return (lax.all_gather(packet, ("shard", "ctx"), axis=0, tiled=True),)

    upper = jnp.concatenate([w_qkv[1].reshape(block, -1), w_out[1], w_up[1], w_down[1]], axis=1)
    first = jnp.concatenate([w_qkv[0].reshape(block, -1), w_out[0]], axis=1)
    steps = after(timesteps, first)
    first = Gather(plan, [first] * shards)

    vectors = jnp.concatenate(
        [norms[0], norms[1], out_biases[0], out_biases[1]], axis=1
    )
    seqs = conts + 1
    steps_back = jnp.concatenate([steps] + [to_shard(plan, steps, k) for k in range(1, shards)])
    steps_near = jnp.concatenate([steps_back[:1], steps_back[:0:-1]]).reshape(-1)
    one_hot = (steps_near[:, None] == jnp.arange(table.shape[0], dtype=jnp.int32)[None, :]).astype(BF16)
    looked = lax.dot_general(
        table, one_hot, (((0,), (1,)), ((), ())), preferred_element_type=F32
    ).astype(BF16)
    blank = jnp.zeros((block, LANES - vectors.shape[1] - seqs), BF16)
    if plan.blocks:
        small = [
            jnp.concatenate([vectors, looked[:, k * seqs : (k + 1) * seqs], blank], axis=1)
            for k in range(shards)
        ]
        small = Gather(plan, small)
        first.along(*small.got)
        ties = (first.stack,)
        small = small.along().across().cores().arrays
    else:
        looked = jnp.roll(looked.reshape(block, shards, seqs), z, axis=1).reshape(block, -1)
        every = lax.all_gather(jnp.concatenate([vectors, looked], axis=1), ("shard", "ctx"), axis=0, tiled=True)
        mine = lax.dynamic_slice_in_dim(every, 8 + z * seqs, seqs, axis=1)
        blank = jnp.zeros((width, LANES - 8 - seqs), BF16)
        small = [jnp.concatenate([every[:, :8], mine, blank], axis=1)]
        ties = ()
    second = Gather(plan, [w_up[0]] * shards, *ties)
    third = Gather.at_once(plan, w_down[0], *ties)
    first.across().cores(*stage_of(plan, second, "got"))
    upper = everywhere(after(upper, *ties))

    mm = 2 * rows * width
    full = shape(rows, width, dtype=F32)
    low = shape(rows, width)
    heads = shape(rows, heads_width)
    wide = shape(rows, hidden)
    sums = shape(8, width, dtype=F32)
    qkv_outs = [low, heads, shape(rows, 2 * heads_width)]
    attn_flops = 4 * rows * plan.group * heads_width

    saved = []
    x_mid = part = part_far = None
    for layer in range(layers):
        last = layer == layers - 1
        ties = ()
        if layer == 0:
            x, vec, a, q, kv = run(
                plan,
                functools.partial(embed_body, plan),
                "embed",
                meta,
                [tokens, query_bias, value_bias],
                [(first.arrays, 0, n3), (small, 0, LANES)],
                [full, sums, *qkv_outs],
                mm * n3,
                ties=stage_of(plan, second, "got"),
            )
            second.along(kv).across()
            ties = stage_of(plan, second, "stack") + stage_of(plan, third, "stack")
            of_attn = [(first.arrays, 0, n3), (first.arrays, n3, heads_width)]
        else:
            of_attn = [(upper, 0, n3), (upper, n3, heads_width)]
            of_feed = [(upper, n3 + heads_width + i * hidden, hidden) for i in range(2)]
            x, a, q, kv = run(
                plan,
                functools.partial(next_body, plan, layer),
                "project",
                meta,
                [x_mid, part, part_far, vec, query_bias, value_bias],
                of_attn[:1],
                [full, *qkv_outs],
                mm * n3,
            )
        kvs = gather_keys(plan, kv)
        part, o, total, kv_all = run(
            plan,
            functools.partial(attend_body, plan),
            "attend",
            meta,
            [q, *kvs],
            of_attn[1:],
            [low, heads, shape(8, 2 * rows, dtype=F32), shape(plan.group, 2 * heads_width)],
            mm * heads_width + attn_flops,
            ties=ties,
        )
        part_far = swap_tp(part)
        if layer == 0:
            second.cores(part)
            third.across(part).cores(part_far)
            of_feed = [(second.arrays, 0, hidden), (third.arrays, 0, hidden, True)]
        outs = [full, low, wide, shape(rows, hidden, dtype=F32), low]
        if last:
            outs += [wide, low, sums]
        got = run(
            plan,
            functools.partial(feed_body, plan, layer, last),
            "feed",
            meta,
            [x, part, part_far, vec, up_bias] + ([cotangent] if last else []),
            of_feed,
            outs,
            mm * hidden * (4 if last else 2),
        )
        x_mid, b, gelu, slope, part = got[:5]
        part_far = swap_tp(part)
        saved.append((x, a, q, kv_all, o, total, x_mid, b, gelu, slope, of_attn, of_feed))

    gy = dy = cotangent
    dh, db, feed_sum = got[5:]
    final = (x_mid, part, part_far)
    bias_last = vec[2 * layers + 3][None, :]
    small_sums = [None] * layers
    above = None
    for layer in reversed(range(layers)):
        x, a, q, kv_all, o, total, x_mid, b, gelu, slope, of_attn, of_feed = saved[layer]
        if above is not None:
            gy, dy, dh, db, feed_sum = run(
                plan,
                functools.partial(between_body, plan, layer),
                "feed_back",
                meta,
                [da, da_far],
                of_feed,
                [full, low, wide, low, sums],
                2 * mm * hidden,
                kept=[dx_mid, saved[layer + 1][0], vec, slope],
                limit=LIMIT_FB,
                ties=stage_of(plan, above, "send"),
            )
        db_far = swap_tp(db)
        if above is None:
            upper_feed = Reduction(plan, meta, "feed_grad", [(b, dh), (dy, gelu)], blocks=False)
            ties = stage_of(plan, upper_feed, "send")
        else:
            feeds = [
                Reduction(plan, meta, "up_grad", [(b, dh)], relative=True).core(db_far),
                Reduction(plan, meta, "down_grad", [(dy, gelu)]).core(db_far),
            ]
            ties = stage_of(plan, feeds[0], "send") + stage_of(plan, feeds[1], "send")
        if plan.blocks:
            dkv_outs = [shape(2 * rows, 2 * heads_width)] * 2
        else:
            dkv_outs = [shape(plan.group, 2 * heads_width)]
        dx_mid, dz, dq, attn_sum, *dkv = run(
            plan,
            functools.partial(attend_back_body, plan, layer),
            "attend_back",
            meta,
            [gy, db, db_far],
            of_attn[1:],
            [full, low, heads, sums, *dkv_outs],
            mm * heads_width + 10 * rows * plan.group * heads_width,
            ties=ties,
            kept=[x_mid, vec, q, total, kv_all],
        )
        ties = ()
        if plan.blocks:
            keep, send = dkv
            near = swap_core(send)
            summed = add(keep[rows:], near[rows:]).astype(BF16)
            terms = [keep, near, swap_chip(summed)]
        else:
            terms = [lax.psum_scatter(dkv[0], "ctx", scatter_dimension=0, tiled=True)]
            summed = terms[0]
        if above is not None:
            for one in (above, *feeds):
                one.pairs(summed)
                ties += stage_of(plan, one, "pair")
        dqkv, da, proj_sum = run(
            plan,
            functools.partial(project_back_body, plan),
            "project_back",
            meta,
            [dq, *terms],
            of_attn[:1],
            [shape(rows, n3), low, shape(8, 2 * heads_width, dtype=F32)],
            mm * n3,
            ties=ties,
        )
        da_far = swap_tp(da)
        attn = Reduction(plan, meta, "attn_grad", [(a, dqkv), (dz, o)], relative=above is not None).core(da_far)
        if above is not None:
            above.along(da)
            end_ties = stage_of(plan, attn, "send") + stage_of(plan, above, "sums") + stage_of(plan, feeds[0], "far")
            upper_attn = above
        above = attn
        small_sums[layer] = [feed_sum, attn_sum, proj_sum]

    grad_tokens, packet = run(
        plan,
        functools.partial(end_body, plan),
        "end",
        meta,
        [da, da_far],
        [],
        [full, shape(32, width)],
        mm * 32,
        ties=end_ties,
        kept=[dx_mid, saved[0][0], vec, *small_sums[0], *small_sums[1]],
    )
    attn.pairs(packet, *stage_of(plan, feeds[0], "far"))
    feeds[0].along(packet, *stage_of(plan, upper_attn, "sums"), *stage_of(plan, upper_feed, "total"))
    feeds[1].along(*stage_of(plan, feeds[0], "sums"), *stage_of(plan, attn, "pair"))
    attn.along(*stage_of(plan, feeds[1], "sums"), *stage_of(plan, feeds[0], "got"))
    x_mid, part, part_far = after_all(final, packet)
    activations = (x_mid + add(part, part_far) + bias_last).astype(BF16)
    start = (z * contexts + c) * block
    if plan.blocks:
        packet = add(packet, swap_core(packet)).astype(BF16)
        far = after(swap_chip(packet), *attn.sums)
        packet = add(packet, far).astype(BF16)
        got = jnp.stack([packet] + [to_shard(plan, packet, k) for k in range(1, shards)])
        other = add(*[got[k] for k in range(0, shards, 2)]) + add(*[got[k] for k in range(1, shards, 2)])
    else:
        packet = lax.psum(packet, "ctx")
        got = lax.all_gather(packet, "shard", axis=0)
        other = jnp.sum(got.astype(F32), axis=0)
        steps_back = jnp.roll(steps_back[::-1], z + 1, axis=0)
    mine = lax.dynamic_slice_in_dim(got[:, :seqs], start, block, axis=2).reshape(-1, block)
    one_hot = (jnp.arange(table.shape[0], dtype=jnp.int32)[:, None] == steps_back.reshape(-1)[None, :]).astype(BF16)
    grad_table = jnp.dot(one_hot, mine, preferred_element_type=F32)

    upper_feed, upper_attn = upper_feed.end(packet), upper_attn.end(packet)
    halves = hidden // width
    per_layer = 5 + halves
    by_layer = other[16 : 16 + layers * per_layer].reshape(layers, per_layer, width)
    local = lax.dynamic_slice_in_dim(by_layer[:, :4], start, block, axis=2)
    grad_norms = jnp.moveaxis(local[:, :2], 1, 2)
    grad_out_biases = jnp.moveaxis(local[:, 2:], 1, 2)
    grad_up_bias = by_layer[:, 4 : 4 + halves].reshape(layers, hidden)
    grad_query_bias = by_layer[:, 4 + halves, :heads_width]
    grad_value_bias = by_layer[:, 4 + halves, heads_width:]
    ups = [feeds[0].end(), upper_feed[:, :hidden]]
    downs = [feeds[1].end(), upper_feed[:, hidden:]]
    attns = [attn.end(), upper_attn]
    return (
        activations,
        grad_tokens,
        jnp.stack([g[:, :n3].reshape(block, 3, heads_width) for g in attns]),
        jnp.stack([g[:, n3:] for g in attns]),
        jnp.stack(ups),
        jnp.stack(downs),
        grad_norms,
        grad_table,
        grad_query_bias,
        grad_value_bias,
        grad_up_bias,
        grad_out_biases,
    )


def solution(mesh):
    placed = (
        P(("shard", "ctx"), None),
        P("shard", None),
        P("shard", None),
        P(None, ("shard", "ctx")),
        P(None, ("shard", "ctx"), None, "tp"),
        P(None, ("shard", "ctx"), "tp"),
        P(None, ("shard", "ctx"), "tp"),
        P(None, ("shard", "ctx"), "tp"),
        P(None, ("shard", "ctx"), None),
        P(None, "tp"),
        P(None, "tp"),
        P(None, "tp"),
        P(None, ("shard", "ctx"), None),
        P(("shard", "ctx"), None),
    )
    return jax.shard_map(
        per_device,
        mesh=mesh,
        in_specs=placed,
        out_specs=(
            P(("shard", "ctx"), None),
            P(("shard", "ctx"), None),
            P(None, ("shard", "ctx"), None, "tp"),
            P(None, ("shard", "ctx"), "tp"),
            P(None, ("shard", "ctx"), "tp"),
            P(None, ("shard", "ctx"), "tp"),
            P(None, ("shard", "ctx"), None),
            P(None, ("shard", "ctx")),
            P(None, "tp"),
            P(None, "tp"),
            P(None, "tp"),
            P(None, ("shard", "ctx"), None),
        ),
        check_vma=False,
    )
```

```python
import functools
import math

import jax
import jax.numpy as jnp
from jax import lax
from jax.experimental import pallas as pl
from jax.experimental.pallas import tpu as pltpu
from jax.sharding import PartitionSpec as P

HEAD_DIM = 64
EPSILON = 1e-05
NEGATIVE = -1e30
F32 = jnp.float32
BF16 = jnp.bfloat16
LANES = 128
CHUNK = 768
SPLIT = 3
VMEM_LIMIT = 46 * 1024 * 1024
LIMIT_FB = 52 * 1024 * 1024
ORDER = (0, 2, 1, 3)


def nn(a, b):
    return lax.dot_general(a, b, (((1,), (0,)), ((), ())), preferred_element_type=F32)


def nt(a, b):
    return lax.dot_general(a, b, (((1,), (1,)), ((), ())), preferred_element_type=F32)


def tn(a, b):
    return lax.dot_general(a, b, (((0,), (0,)), ((), ())), preferred_element_type=F32)


def normed_rows(values):
    centered = values - jnp.mean(values, axis=-1, keepdims=True)
    scale = lax.rsqrt(jnp.mean(centered * centered, axis=-1, keepdims=True) + EPSILON)
    return centered * scale, scale


def norm_back(values, gain, grad):
    hat, scale = normed_rows(values)
    grad_gain = jnp.sum(grad * hat, axis=0, keepdims=True)
    inner = grad * gain
    along = jnp.mean(inner * hat, axis=-1, keepdims=True)
    centre = jnp.mean(inner, axis=-1, keepdims=True)
    return scale * (inner - centre - hat * along), grad_gain


def rows_of(parts, count, width):
    have = len(parts)
    if have < count:
        parts = list(parts) + [jnp.zeros((count - have, width), F32)]
    return jnp.concatenate(parts, axis=0)


class Plan:
    def __init__(self, rows, width, block, heads_width, hidden, shards, contexts, conts):
        self.rows, self.width, self.block = rows, width, block
        self.heads_width, self.hidden = heads_width, hidden
        self.shards, self.contexts, self.conts = shards, contexts, conts
        self.group = rows * contexts
        self.blocks = contexts == 4 and block % 16 == 0


def run(plan, body, name, meta, inputs, weights, outs, flops, scratch=(), direct=(), ties=(), kept=(), limit=VMEM_LIMIT):
    if ties:
        inputs = [after(inputs[0], *ties), *inputs[1:]]
    n_in, n_out = len(inputs), len(outs)
    counts = [len(entry[0]) for entry in weights]
    per_block = plan.shards * len(ORDER) * SPLIT
    copies = sum(1 if n == 1 else per_block for n in counts) + len(kept)

    def kernel(meta_ref, *refs):
        ins = refs[:n_in]
        at = n_in
        sources = []
        for n in counts:
            sources.append(refs[at : at + n])
            at += n
        lying = refs[at : at + len(kept)]
        at += len(kept)
        results = refs[at : at + n_out]
        at += n_out
        held = refs[at : at + len(weights)]
        at += len(weights)
        brought = refs[at : at + len(kept)]
        at += len(kept)
        sems = refs[at] if copies else None
        own = refs[at + 1 :] if copies else refs[at:]
        started, slot = [], 0
        bringing = []
        for ref, into in zip(lying, brought):
            bringing.append(pltpu.make_async_copy(ref, into, sems.at[slot]))
            slot += 1
        for copy in bringing:
            copy.start()
        for (_, column, width, *whole), refs_of, into in zip(weights, sources, held):
            group = []
            columns = pl.ds(column, width)
            split = math.gcd(width // LANES, SPLIT)
            if len(refs_of) == 1:
                group.append(pltpu.make_async_copy(refs_of[0].at[:, columns], into, sems.at[slot]))
                slot += 1
            else:
                for place, offset in enumerate(ORDER):
                    for shift in range(plan.shards):
                        ref = refs_of[place].at[shift]
                        z = shift if whole else lax.rem(meta_ref[0] + (plan.shards - shift), plan.shards)
                        index = z * plan.contexts + jnp.bitwise_xor(meta_ref[1], offset)
                        row = pl.multiple_of(index * plan.block, 16)
                        for part in range(0, width, width // split):
                            group.append(
                                pltpu.make_async_copy(
                                    ref.at[:, pl.ds(column + part, width // split)],
                                    into.at[pl.ds(row, plan.block), pl.ds(part, width // split)],
                                    sems.at[slot],
                                )
                            )
                            slot += 1
            for copy in group:
                copy.start()
            started.append(group)

        def weight(i):
            for copy in started[i]:
                copy.wait()
            return held[i]

        for copy in bringing:
            copy.wait()
        body(meta_ref, (*ins, *brought), weight, results, own)

    vmem = pl.BlockSpec(memory_space=pltpu.VMEM)
    anywhere = pl.BlockSpec(memory_space=pl.ANY)
    outside = pl.BlockSpec(memory_space=pltpu.HBM)
    scratch_shapes = [pltpu.VMEM((plan.width, entry[2]), BF16) for entry in weights]
    scratch_shapes += [pltpu.VMEM(array.shape, array.dtype) for array in kept]
    if copies:
        scratch_shapes.append(pltpu.SemaphoreType.DMA((copies,)))
    moved = sum(x.size * x.dtype.itemsize for x in inputs)
    moved += sum(math.prod(o.shape) * o.dtype.itemsize for o in outs)
    moved += sum(plan.width * entry[2] * 2 for entry in weights)
    call = pl.pallas_call(
        kernel,
        name=name,
        out_shape=tuple(outs),
        in_specs=[pl.BlockSpec(memory_space=pltpu.SMEM)]
        + [vmem] * n_in
        + [outside if n == 1 else anywhere for n in counts for _ in range(n)]
        + [anywhere] * len(kept),
        out_specs=tuple(outside if i in direct else vmem for i in range(n_out)),
        scratch_shapes=scratch_shapes + list(scratch),
        compiler_params=pltpu.CompilerParams(vmem_limit_bytes=limit),
        cost_estimate=pl.CostEstimate(flops=flops, bytes_accessed=moved, transcendentals=0),
    )
    return call(meta, *inputs, *[array for entry in weights for array in entry[0]], *kept)


def shape(*dims, dtype=BF16):
    return jax.ShapeDtypeStruct(dims, dtype)


def segment(plan, meta, position):
    prompt = plan.group // 2
    seg = jnp.ones(position.shape, jnp.int32)
    for j in range(plan.conts):
        seg = seg + (position - prompt >= meta[2 + j]).astype(jnp.int32)
    return jnp.where(position < prompt, 0, seg)


def key_positions(plan, meta):
    if not plan.blocks:
        return lax.broadcasted_iota(jnp.int32, (plan.group, 1), 0)
    inside = lax.broadcasted_iota(jnp.int32, (plan.rows, 1), 0)
    return jnp.concatenate(
        [inside + jnp.bitwise_xor(meta[1], d) * plan.rows for d in ORDER], axis=0
    )


def allowed_keys(plan, meta):
    lane = lax.broadcasted_iota(jnp.int32, (1, 2 * plan.rows), 1)
    query = meta[1] * plan.rows + jnp.where(lane >= plan.rows, lane - plan.rows, lane)
    seg_query = segment(plan, meta, query)
    seg_key = segment(plan, meta, key_positions(plan, meta))
    return (seg_key == 0) | (seg_key == seg_query)


def pair_rows(values):
    first = lax.broadcasted_iota(jnp.int32, values.shape, 1) < HEAD_DIM
    none = jnp.zeros_like(values)
    return jnp.concatenate([jnp.where(first, values, none), jnp.where(first, none, values)], axis=0)


def pair_lanes(values):
    rows = values.shape[0] // 2
    first = lax.broadcasted_iota(jnp.int32, (rows, LANES), 1) < HEAD_DIM
    return jnp.where(first, values[:rows], values[rows:])


def write_qkv(plan, layer, x, gain, weight, q_bias, v_bias, a_ref, q_ref, kv_ref):
    n = plan.heads_width
    hat, _ = normed_rows(x)
    a = (hat * gain).astype(BF16)
    a_ref[...] = a
    bias_q = q_bias[...].astype(F32)[layer : layer + 1]
    bias_v = v_bias[...].astype(F32)[layer : layer + 1]
    kv_ref[:, :n] = nn(a, weight[:, n : 2 * n]).astype(BF16)
    kv_ref[:, n:] = (nn(a, weight[:, 2 * n :]) + bias_v).astype(BF16)
    q_ref[...] = (nn(a, weight[:, :n]) + bias_q).astype(BF16)


def embed_body(plan, meta, ins, weight, outs, own):
    tokens, q_bias, v_bias = ins
    x_ref, vec_ref, a_ref, q_ref, kv_ref = outs
    small = weight(1)[...].astype(F32).T
    vec_ref[...] = small[:8]
    lookup = small[8:24].astype(BF16)
    inside = lax.broadcasted_iota(jnp.int32, (plan.rows, 1), 0)
    seg = segment(plan, meta, meta[1] * plan.rows + inside)
    member = seg == lax.broadcasted_iota(jnp.int32, (plan.rows, 16), 1)
    x = tokens[...].astype(F32) + nn(member.astype(F32).astype(BF16), lookup)
    x_ref[...] = x
    write_qkv(plan, 0, x, small[:1], weight(0), q_bias, v_bias, a_ref, q_ref, kv_ref)


def next_body(plan, layer, meta, ins, weight, outs, own):
    x_mid, part, part_far, vec, q_bias, v_bias = ins
    x_ref, a_ref, q_ref, kv_ref = outs
    x = x_mid[...] + (part[...].astype(F32) + part_far[...].astype(F32))
    x = x + vec[2 * layer + 3 : 2 * layer + 4, :]
    x_ref[...] = x
    gain = vec[2 * layer : 2 * layer + 1, :]
    write_qkv(plan, layer, x, gain, weight(0), q_bias, v_bias, a_ref, q_ref, kv_ref)


def attend_body(plan, meta, ins, weight, outs, own):
    q_ref, kvs = ins[0], ins[1:]
    part_ref, o_ref, total_ref, all_ref = outs
    n = plan.heads_width
    for i, kv in enumerate(kvs):
        all_ref[i * kv.shape[0] : (i + 1) * kv.shape[0], :] = kv[...]
    allowed = allowed_keys(plan, meta)
    totals = []
    for pair in range(n // LANES):
        lanes = slice(pair * LANES, (pair + 1) * LANES)
        late = slice(n + pair * LANES, n + (pair + 1) * LANES)
        q2 = pair_rows(q_ref[:, lanes])
        keys = jnp.concatenate([kv[:, lanes] for kv in kvs], axis=0)
        values = jnp.concatenate([kv[:, late] for kv in kvs], axis=0)
        scores = jnp.where(allowed, nt(keys, q2) * (1.0 / math.sqrt(HEAD_DIM)), NEGATIVE)
        top = jnp.max(scores, axis=0, keepdims=True)
        exps = jnp.exp(scores - top)
        total = jnp.sum(exps, axis=0, keepdims=True)
        prob = (exps * (1.0 / total)).astype(BF16)
        o_ref[:, lanes] = pair_lanes(tn(prob, values)).astype(BF16)
        totals.append(top + jnp.log(total))
    total_ref[...] = rows_of(totals, 8, 2 * plan.rows)
    part_ref[...] = nt(o_ref[...], weight(0)[...]).astype(BF16)


def feed_body(plan, layer, last, meta, ins, weight, outs, own):
    x, part, part_far, vec, bias = ins[:5]
    mid_ref, b_ref, gelu_ref, slope_ref, part_ref = outs[:5]
    x_mid = x[...] + (part[...].astype(F32) + part_far[...].astype(F32))
    x_mid = x_mid + vec[2 * layer + 4 : 2 * layer + 5, :]
    mid_ref[...] = x_mid
    hat, _ = normed_rows(x_mid)
    b = (hat * vec[2 * layer + 1 : 2 * layer + 2, :]).astype(BF16)
    b_ref[...] = b
    bias_f = bias[...].astype(F32)[layer : layer + 1]
    up = weight(0)
    chunks = [slice(i, min(i + CHUNK, plan.hidden)) for i in range(0, plan.hidden, CHUNK)]
    for columns in chunks:
        hidden = nn(b, up[:, columns]) + bias_f[:, columns]
        half = 0.5 * (1.0 + lax.erf(hidden * math.sqrt(0.5)))
        gelu_ref[:, columns] = (hidden * half).astype(BF16)
        bell = jnp.exp(hidden * hidden * -0.5) * (1.0 / math.sqrt(2.0 * math.pi))
        slope_ref[:, columns] = half + hidden * bell
    down = weight(1)
    if last:
        back_feed(plan, ins[5][...], slope_ref, up, down, outs[5], outs[6], outs[7], ins[5][...].astype(F32), None)
    part_ref[...] = nt(gelu_ref[...], down[...]).astype(BF16)


def back_feed(plan, dy, slope, up, down, dh_ref, db_ref, sum_ref, gradient, extra):
    sums = []
    total = None
    for i in range(0, plan.hidden, CHUNK):
        columns = slice(i, min(i + CHUNK, plan.hidden))
        dh = (nn(dy, down[:, columns]) * slope[:, columns]).astype(BF16)
        dh_ref[:, columns] = dh
        sums.append(jnp.sum(dh.astype(F32), axis=0, keepdims=True))
        term = nt(dh, up[:, columns])
        total = term if total is None else total + term
    db_ref[...] = total.astype(BF16)
    bias_sum = jnp.concatenate(sums, axis=1)
    parts = [jnp.sum(gradient, axis=0, keepdims=True)]
    for i in range(plan.hidden // plan.width):
        parts.append(bias_sum[:, i * plan.width : (i + 1) * plan.width])
    if extra is not None:
        parts.append(extra)
    sum_ref[...] = rows_of(parts, 8, plan.width)


def between_body(plan, layer, meta, ins, weight, outs, own):
    da, da_far, dx_mid, x_above, vec, slope = ins
    gy_ref, dy_ref, dh_ref, db_ref, sum_ref = outs
    grad = da[...].astype(F32) + da_far[...].astype(F32)
    back, gain_sum = norm_back(x_above[...], vec[2 * layer + 2 : 2 * layer + 3, :], grad)
    gy = dx_mid[...] + back
    gy_ref[...] = gy
    dy = gy.astype(BF16)
    dy_ref[...] = dy
    back_feed(plan, dy, slope, weight(0), weight(1), dh_ref, db_ref, sum_ref, gy, gain_sum)


def attend_back_body(plan, layer, meta, ins, weight, outs, own):
    gy, db, db_far, x_mid, vec, q_ref, total = ins[:7]
    kvs = ins[7:]
    mid_ref, dz_ref, dq_ref, sum_ref = outs[:4]
    dkv = outs[4:]
    n = plan.heads_width
    scale = 1.0 / math.sqrt(HEAD_DIM)
    grad = db[...].astype(F32) + db_far[...].astype(F32)
    back, gain_sum = norm_back(x_mid[...], vec[2 * layer + 1 : 2 * layer + 2, :], grad)
    dx_mid = gy[...].astype(F32) + back
    mid_ref[...] = dx_mid
    sum_ref[...] = rows_of([gain_sum, jnp.sum(dx_mid, axis=0, keepdims=True)], 8, plan.width)
    dz = dx_mid.astype(BF16)
    dz_ref[...] = dz
    do = nn(dz, weight(0)[...]).astype(BF16)
    allowed = allowed_keys(plan, meta)
    each = plan.group // len(dkv)
    for pair in range(n // LANES):
        lanes = slice(pair * LANES, (pair + 1) * LANES)
        late = slice(n + pair * LANES, n + (pair + 1) * LANES)
        q2 = pair_rows(q_ref[:, lanes])
        do2 = pair_rows(do[:, lanes])
        keys = jnp.concatenate([kv[:, lanes] for kv in kvs], axis=0)
        values = jnp.concatenate([kv[:, late] for kv in kvs], axis=0)
        prob = jnp.exp(nt(keys, q2) * scale - total[pair : pair + 1, :])
        prob = jnp.where(allowed, prob, 0.0)
        dprob = nt(values, do2)
        delta = jnp.sum(prob * dprob, axis=0, keepdims=True)
        dscore = (prob * (dprob - delta)).astype(BF16)
        dq_ref[:, lanes] = (pair_lanes(tn(dscore, keys)) * scale).astype(BF16)
        dk = (nn(dscore, q2) * scale).astype(BF16)
        dv = nn(prob.astype(BF16), do2).astype(BF16)
        for i, ref in enumerate(dkv):
            ref[:, lanes] = dk[i * each : (i + 1) * each]
            ref[:, late] = dv[i * each : (i + 1) * each]


def project_back_body(plan, meta, ins, weight, outs, own):
    dq = ins[0]
    dqkv_ref, da_ref, sum_ref = outs
    n = plan.heads_width
    dkv = ins[1][: plan.rows].astype(F32)
    for term in ins[2:]:
        dkv = dkv + term[: plan.rows].astype(F32)
    dkv = dkv.astype(BF16)
    dqkv_ref[:, :n] = dq[...]
    dqkv_ref[:, n:] = dkv
    da_ref[...] = nt(dqkv_ref[...], weight(0)[...]).astype(BF16)
    sums = [
        jnp.sum(dq[...].astype(F32), axis=0, keepdims=True),
        jnp.sum(dkv[:, n:].astype(F32), axis=0, keepdims=True),
    ]
    sum_ref[...] = rows_of([jnp.concatenate(sums, axis=1)], 8, 2 * n)


def weight_grad_body(plan, widths, relative, meta, ins, weight, outs, own):
    packet, sems = own
    column, copies = 0, []
    for i, width in enumerate(widths):
        left, right = ins[2 * i], ins[2 * i + 1]
        turned = left[...].T
        for j in range(0, width, CHUNK):
            size = min(CHUNK, width - j)
            window = pl.ds(column, size)
            packet[:, column : column + size] = nn(turned, right[:, j : j + size]).astype(BF16)
            column += size
            if len(outs) == 1:
                copy = pltpu.make_async_copy(packet.at[:, window], outs[0].at[:, window], sems.at[len(copies)])
                copy.start()
                copies.append(copy)
                continue
            for place, offset in enumerate(ORDER):
                for k in range(plan.shards):
                    z = lax.rem(meta[0] + k, plan.shards) if relative else k
                    index = z * plan.contexts + jnp.bitwise_xor(meta[1], offset)
                    row = pl.multiple_of(index * plan.block, 16)
                    copy = pltpu.make_async_copy(
                        packet.at[pl.ds(row, plan.block), window],
                        outs[place // 2].at[place % 2, k, :, window],
                        sems.at[len(copies)],
                    )
                    copy.start()
                    copies.append(copy)
    for copy in copies:
        copy.wait()


def end_body(plan, meta, ins, weight, outs, own):
    da, da_far, dx_mid, x, vec = ins[:5]
    feed0, attn0, proj0, feed1, attn1, proj1 = ins[5:]
    gy_ref, small_ref = outs
    grad = da[...].astype(F32) + da_far[...].astype(F32)
    back, gain_sum = norm_back(x[...], vec[:1, :], grad)
    gy = dx_mid[...] + back
    gy_ref[...] = gy
    lane = lax.broadcasted_iota(jnp.int32, (1, plan.rows), 1)
    seg = segment(plan, meta, meta[1] * plan.rows + lane)
    member = (seg == lax.broadcasted_iota(jnp.int32, (16, plan.rows), 0)).astype(F32)
    sums = lax.dot_general(
        member, gy, (((1,), (0,)), ((), ())), precision=lax.Precision.HIGHEST, preferred_element_type=F32
    )
    halves = plan.hidden // plan.width
    parts = [sums]
    for gain_row, feed, attn, proj in (
        (gain_sum, feed0, attn0, proj0),
        (feed0[1 + halves : 2 + halves, :], feed1, attn1, proj1),
    ):
        parts += [gain_row, attn[0:1, :], attn[1:2, :], feed[0:1, :]]
        parts += [feed[1 + i : 2 + i, :] for i in range(halves)]
        parts += [proj[0:1, :]]
    small_ref[...] = rows_of_total(parts, 32, plan.width).astype(BF16)


def rows_of_total(parts, count, width):
    have = sum(part.shape[0] for part in parts)
    return jnp.concatenate(parts + [jnp.zeros((count - have, width), F32)], axis=0)


def swap_core(array):
    return lax.ppermute(array, "ctx", [(i, i ^ 1) for i in range(4)])


def swap_chip(array):
    return lax.ppermute(array, "ctx", [(i, i ^ 2) for i in range(4)])


def swap_tp(array):
    return lax.ppermute(array, "tp", [(0, 1), (1, 0)])


def to_shard(plan, array, shift):
    n = plan.shards
    return lax.ppermute(array, "shard", [(i, (i + shift) % n) for i in range(n)])


def stage_of(plan, thing, *names):
    if not plan.blocks:
        return ()
    found = [getattr(thing, name) for name in names]
    return tuple(array for one in found for array in (one if isinstance(one, tuple) else (one,)))


class Gather:
    def __init__(self, plan, packets, *ties):
        self.plan = plan
        if plan.blocks:
            packets = after_all(packets, *ties) if ties else tuple(packets)
            got = [to_shard(plan, packets[k], k) for k in range(1, plan.shards)]
            self.got = tuple(got)
            self.blocks = (packets[0], *got)
        else:
            self.arrays = (lax.all_gather(packets[0], ("shard", "ctx"), axis=0, tiled=True),)

    @classmethod
    def at_once(cls, plan, packet, *ties):
        self = cls.__new__(cls)
        self.plan = plan
        if plan.blocks:
            copies = jnp.broadcast_to(after(packet, *ties), (plan.shards, *packet.shape))
            self.stack = lax.all_to_all(copies, "shard", 0, 0, tiled=True)
        else:
            self.arrays = (lax.all_gather(packet, ("shard", "ctx"), axis=0, tiled=True),)
        return self

    def along(self, *ties):
        if self.plan.blocks:
            self.stack = jnp.stack(after_all(self.blocks, *ties) if ties else self.blocks)
        return self

    def across(self, *ties):
        if self.plan.blocks:
            self.far = swap_chip(after(self.stack, *ties) if ties else self.stack)
        return self

    def cores(self, *ties):
        if self.plan.blocks:
            halves = (self.stack, self.far)
            sent = after_all(halves, *ties) if ties else halves
            self.arrays = (*halves, *[swap_core(half) for half in sent])
        return self


def gather_keys(plan, kv):
    if plan.blocks:
        far = swap_chip(kv)
        return (kv, far, swap_core(kv), swap_core(far))
    return (lax.all_gather(kv, "ctx", axis=0, tiled=True),)


def after(array, *others):
    return lax.optimization_barrier((array, *others))[0]


def after_all(arrays, *others):
    return lax.optimization_barrier((*arrays, *others))[: len(arrays)]


def add(*terms):
    total = terms[0].astype(F32)
    for term in terms[1:]:
        total = total + term.astype(F32)
    return total


def weight_grads(plan, meta, name, pairs, blocks, relative=False):
    widths = tuple(right.shape[1] for _, right in pairs)
    width = sum(widths)
    copies = sum(pl.cdiv(width, CHUNK) for width in widths)
    if blocks:
        outs = [shape(2, plan.shards, plan.block, width)] * 2
        copies *= plan.shards * 4
    else:
        outs = [shape(plan.width, width)]
    return run(
        plan,
        functools.partial(weight_grad_body, plan, widths, relative),
        name,
        meta,
        [],
        [],
        outs,
        2 * plan.rows * plan.width * width,
        kept=[array for pair in pairs for array in pair],
        scratch=[pltpu.VMEM((plan.width, width), BF16), pltpu.SemaphoreType.DMA((copies,))],
        direct=tuple(range(len(outs))),
    )


class Reduction:
    def __init__(self, plan, meta, name, pairs, blocks=True, relative=False):
        self.blocks = blocks and plan.blocks
        self.plan, self.relative = plan, relative
        parts = weight_grads(plan, meta, name, pairs, self.blocks, relative)
        if self.blocks:
            self.keep, self.send = parts
        else:
            self.send = parts[0]
            total = lax.psum_scatter(parts[0], ("shard", "ctx"), scatter_dimension=0, tiled=True)
            self.total = total

    def core(self, *ties):
        if self.blocks:
            self.near = swap_core(after(self.send, *ties))
        return self

    def pairs(self, *ties):
        if self.blocks:
            self.near = after(self.near, *ties)
            self.pair = add(self.keep[1], self.near[1]).astype(BF16)
            self.far = swap_chip(self.pair)
        return self

    def along(self, *ties):
        if self.blocks:
            far = after(self.far, *ties) if ties else self.far
            if self.relative:
                n = self.plan.shards
                self.sums = tuple(
                    add(self.keep[0, k], self.near[0, k], far[k]).astype(BF16) for k in range(n)
                )
                self.got = (self.sums[0], *[to_shard(self.plan, self.sums[k], k) for k in range(1, n)])
            else:
                self.sums = add(self.keep[0], self.near[0], far).astype(BF16)
                self.got = lax.all_to_all(self.sums, "shard", 0, 0, tiled=True)
        return self

    def end(self, *ties):
        if not self.blocks:
            return (after(self.total, *ties) if self.plan.blocks else self.total).astype(F32)
        if self.relative:
            return add(*after_all(self.got, *ties))
        return jnp.sum(after(self.got, *ties).astype(F32), axis=0)


def per_device(
    tokens,
    timesteps,
    cont_lengths,
    table,
    w_qkv,
    w_out,
    w_up,
    w_down,
    norms,
    query_bias,
    value_bias,
    up_bias,
    out_biases,
    cotangent,
):
    rows, width = tokens.shape
    layers, block = w_qkv.shape[:2]
    heads_width, hidden = w_qkv.shape[3], w_up.shape[2]
    shards, contexts = lax.axis_size("shard"), lax.axis_size("ctx")
    conts = cont_lengths.shape[1]
    plan = Plan(rows, width, block, heads_width, hidden, shards, contexts, conts)
    z, c = lax.axis_index("shard"), lax.axis_index("ctx")
    meta = jnp.concatenate([jnp.stack([z, c]).astype(jnp.int32), jnp.cumsum(cont_lengths[0])])

    n3 = 3 * heads_width

    def everywhere(packet):
        return (lax.all_gather(packet, ("shard", "ctx"), axis=0, tiled=True),)

    upper = jnp.concatenate([w_qkv[1].reshape(block, -1), w_out[1], w_up[1], w_down[1]], axis=1)
    first = jnp.concatenate([w_qkv[0].reshape(block, -1), w_out[0]], axis=1)
    steps = after(timesteps, first)
    first = Gather(plan, [first] * shards)

    vectors = jnp.concatenate(
        [norms[0], norms[1], out_biases[0], out_biases[1]], axis=1
    )
    seqs = conts + 1
    steps_back = jnp.concatenate([steps] + [to_shard(plan, steps, k) for k in range(1, shards)])
    steps_near = jnp.concatenate([steps_back[:1], steps_back[:0:-1]]).reshape(-1)
    one_hot = (steps_near[:, None] == jnp.arange(table.shape[0], dtype=jnp.int32)[None, :]).astype(BF16)
    looked = lax.dot_general(
        table, one_hot, (((0,), (1,)), ((), ())), preferred_element_type=F32
    ).astype(BF16)
    blank = jnp.zeros((block, LANES - vectors.shape[1] - seqs), BF16)
    if plan.blocks:
        small = [
            jnp.concatenate([vectors, looked[:, k * seqs : (k + 1) * seqs], blank], axis=1)
            for k in range(shards)
        ]
        small = Gather(plan, small)
        first.along(*small.got)
        ties = (first.stack,)
        small = small.along().across().cores().arrays
    else:
        looked = jnp.roll(looked.reshape(block, shards, seqs), z, axis=1).reshape(block, -1)
        every = lax.all_gather(jnp.concatenate([vectors, looked], axis=1), ("shard", "ctx"), axis=0, tiled=True)
        mine = lax.dynamic_slice_in_dim(every, 8 + z * seqs, seqs, axis=1)
        blank = jnp.zeros((width, LANES - 8 - seqs), BF16)
        small = [jnp.concatenate([every[:, :8], mine, blank], axis=1)]
        ties = ()
    second = Gather(plan, [w_up[0]] * shards, *ties)
    third = Gather.at_once(plan, w_down[0], *ties)
    first.across().cores(*stage_of(plan, second, "got"))
    upper = everywhere(after(upper, *ties))

    mm = 2 * rows * width
    full = shape(rows, width, dtype=F32)
    low = shape(rows, width)
    heads = shape(rows, heads_width)
    wide = shape(rows, hidden)
    sums = shape(8, width, dtype=F32)
    qkv_outs = [low, heads, shape(rows, 2 * heads_width)]
    attn_flops = 4 * rows * plan.group * heads_width

    saved = []
    x_mid = part = part_far = None
    for layer in range(layers):
        last = layer == layers - 1
        ties = ()
        if layer == 0:
            x, vec, a, q, kv = run(
                plan,
                functools.partial(embed_body, plan),
                "embed",
                meta,
                [tokens, query_bias, value_bias],
                [(first.arrays, 0, n3), (small, 0, LANES)],
                [full, sums, *qkv_outs],
                mm * n3,
                ties=stage_of(plan, second, "got"),
            )
            second.along(kv).across()
            ties = stage_of(plan, second, "stack") + stage_of(plan, third, "stack")
            of_attn = [(first.arrays, 0, n3), (first.arrays, n3, heads_width)]
        else:
            of_attn = [(upper, 0, n3), (upper, n3, heads_width)]
            of_feed = [(upper, n3 + heads_width + i * hidden, hidden) for i in range(2)]
            x, a, q, kv = run(
                plan,
                functools.partial(next_body, plan, layer),
                "project",
                meta,
                [x_mid, part, part_far, vec, query_bias, value_bias],
                of_attn[:1],
                [full, *qkv_outs],
                mm * n3,
            )
        kvs = gather_keys(plan, kv)
        part, o, total, kv_all = run(
            plan,
            functools.partial(attend_body, plan),
            "attend",
            meta,
            [q, *kvs],
            of_attn[1:],
            [low, heads, shape(8, 2 * rows, dtype=F32), shape(plan.group, 2 * heads_width)],
            mm * heads_width + attn_flops,
            ties=ties,
        )
        part_far = swap_tp(part)
        if layer == 0:
            second.cores(part)
            third.across(part).cores(part_far)
            of_feed = [(second.arrays, 0, hidden), (third.arrays, 0, hidden, True)]
        outs = [full, low, wide, shape(rows, hidden, dtype=F32), low]
        if last:
            outs += [wide, low, sums]
        got = run(
            plan,
            functools.partial(feed_body, plan, layer, last),
            "feed",
            meta,
            [x, part, part_far, vec, up_bias] + ([cotangent] if last else []),
            of_feed,
            outs,
            mm * hidden * (4 if last else 2),
        )
        x_mid, b, gelu, slope, part = got[:5]
        part_far = swap_tp(part)
        saved.append((x, a, q, kv_all, o, total, x_mid, b, gelu, slope, of_attn, of_feed))

    gy = dy = cotangent
    dh, db, feed_sum = got[5:]
    final = (x_mid, part, part_far)
    bias_last = vec[2 * layers + 3][None, :]
    small_sums = [None] * layers
    above = None
    for layer in reversed(range(layers)):
        x, a, q, kv_all, o, total, x_mid, b, gelu, slope, of_attn, of_feed = saved[layer]
        if above is not None:
            gy, dy, dh, db, feed_sum = run(
                plan,
                functools.partial(between_body, plan, layer),
                "feed_back",
                meta,
                [da, da_far],
                of_feed,
                [full, low, wide, low, sums],
                2 * mm * hidden,
                kept=[dx_mid, saved[layer + 1][0], vec, slope],
                limit=LIMIT_FB,
                ties=stage_of(plan, above, "send"),
            )
        db_far = swap_tp(db)
        if above is None:
            upper_feed = Reduction(plan, meta, "feed_grad", [(b, dh), (dy, gelu)], blocks=False)
            ties = stage_of(plan, upper_feed, "send")
        else:
            feeds = [
                Reduction(plan, meta, "up_grad", [(b, dh)], relative=True).core(db_far),
                Reduction(plan, meta, "down_grad", [(dy, gelu)]).core(db_far),
            ]
            ties = stage_of(plan, feeds[0], "send") + stage_of(plan, feeds[1], "send")
        if plan.blocks:
            dkv_outs = [shape(2 * rows, 2 * heads_width)] * 2
        else:
            dkv_outs = [shape(plan.group, 2 * heads_width)]
        dx_mid, dz, dq, attn_sum, *dkv = run(
            plan,
            functools.partial(attend_back_body, plan, layer),
            "attend_back",
            meta,
            [gy, db, db_far],
            of_attn[1:],
            [full, low, heads, sums, *dkv_outs],
            mm * heads_width + 10 * rows * plan.group * heads_width,
            ties=ties,
            kept=[x_mid, vec, q, total, kv_all],
        )
        ties = ()
        if plan.blocks:
            keep, send = dkv
            near = swap_core(send)
            summed = add(keep[rows:], near[rows:]).astype(BF16)
            terms = [keep, near, swap_chip(summed)]
        else:
            terms = [lax.psum_scatter(dkv[0], "ctx", scatter_dimension=0, tiled=True)]
            summed = terms[0]
        if above is not None:
            for one in (above, *feeds):
                one.pairs(summed)
                ties += stage_of(plan, one, "pair")
        dqkv, da, proj_sum = run(
            plan,
            functools.partial(project_back_body, plan),
            "project_back",
            meta,
            [dq, *terms],
            of_attn[:1],
            [shape(rows, n3), low, shape(8, 2 * heads_width, dtype=F32)],
            mm * n3,
            ties=ties,
        )
        da_far = swap_tp(da)
        attn = Reduction(plan, meta, "attn_grad", [(a, dqkv), (dz, o)], relative=above is not None).core(da_far)
        if above is not None:
            above.along(da)
            end_ties = stage_of(plan, attn, "send") + stage_of(plan, above, "sums") + stage_of(plan, feeds[0], "far")
            upper_attn = above
        above = attn
        small_sums[layer] = [feed_sum, attn_sum, proj_sum]

    grad_tokens, packet = run(
        plan,
        functools.partial(end_body, plan),
        "end",
        meta,
        [da, da_far],
        [],
        [full, shape(32, width)],
        mm * 32,
        ties=end_ties,
        kept=[dx_mid, saved[0][0], vec, *small_sums[0], *small_sums[1]],
    )
    attn.pairs(packet, *stage_of(plan, feeds[0], "far"))
    feeds[0].along(packet, *stage_of(plan, upper_attn, "sums"), *stage_of(plan, upper_feed, "total"))
    feeds[1].along(*stage_of(plan, feeds[0], "sums"), *stage_of(plan, attn, "pair"))
    attn.along(*stage_of(plan, feeds[1], "sums"), *stage_of(plan, feeds[0], "got"))
    x_mid, part, part_far = after_all(final, packet)
    activations = (x_mid + add(part, part_far) + bias_last).astype(BF16)
    start = (z * contexts + c) * block
    if plan.blocks:
        packet = add(packet, swap_core(packet)).astype(BF16)
        far = after(swap_chip(packet), *attn.sums)
        packet = add(packet, far).astype(BF16)
        got = jnp.stack([packet] + [to_shard(plan, packet, k) for k in range(1, shards)])
        other = add(*[got[k] for k in range(0, shards, 2)]) + add(*[got[k] for k in range(1, shards, 2)])
    else:
        packet = lax.psum(packet, "ctx")
        got = lax.all_gather(packet, "shard", axis=0)
        other = jnp.sum(got.astype(F32), axis=0)
        steps_back = jnp.roll(steps_back[::-1], z + 1, axis=0)
    mine = lax.dynamic_slice_in_dim(got[:, :seqs], start, block, axis=2).reshape(-1, block)
    one_hot = (jnp.arange(table.shape[0], dtype=jnp.int32)[:, None] == steps_back.reshape(-1)[None, :]).astype(BF16)
    grad_table = jnp.dot(one_hot, mine, preferred_element_type=F32)

    upper_feed, upper_attn = upper_feed.end(packet), upper_attn.end(packet)
    halves = hidden // width
    per_layer = 5 + halves
    by_layer = other[16 : 16 + layers * per_layer].reshape(layers, per_layer, width)
    local = lax.dynamic_slice_in_dim(by_layer[:, :4], start, block, axis=2)
    grad_norms = jnp.moveaxis(local[:, :2], 1, 2)
    grad_out_biases = jnp.moveaxis(local[:, 2:], 1, 2)
    grad_up_bias = by_layer[:, 4 : 4 + halves].reshape(layers, hidden)
    grad_query_bias = by_layer[:, 4 + halves, :heads_width]
    grad_value_bias = by_layer[:, 4 + halves, heads_width:]
    ups = [feeds[0].end(), upper_feed[:, :hidden]]
    downs = [feeds[1].end(), upper_feed[:, hidden:]]
    attns = [attn.end(), upper_attn]
    return (
        activations,
        grad_tokens,
        jnp.stack([g[:, :n3].reshape(block, 3, heads_width) for g in attns]),
        jnp.stack([g[:, n3:] for g in attns]),
        jnp.stack(ups),
        jnp.stack(downs),
        grad_norms,
        grad_table,
        grad_query_bias,
        grad_value_bias,
        grad_up_bias,
        grad_out_biases,
    )


def solution(mesh):
    placed = (
        P(("shard", "ctx"), None),
        P("shard", None),
        P("shard", None),
        P(None, ("shard", "ctx")),
        P(None, ("shard", "ctx"), None, "tp"),
        P(None, ("shard", "ctx"), "tp"),
        P(None, ("shard", "ctx"), "tp"),
        P(None, ("shard", "ctx"), "tp"),
        P(None, ("shard", "ctx"), None),
        P(None, "tp"),
        P(None, "tp"),
        P(None, "tp"),
        P(None, ("shard", "ctx"), None),
        P(("shard", "ctx"), None),
    )
    return jax.shard_map(
        per_device,
        mesh=mesh,
        in_specs=placed,
        out_specs=(
            P(("shard", "ctx"), None),
            P(("shard", "ctx"), None),
            P(None, ("shard", "ctx"), None, "tp"),
            P(None, ("shard", "ctx"), "tp"),
            P(None, ("shard", "ctx"), "tp"),
            P(None, ("shard", "ctx"), "tp"),
            P(None, ("shard", "ctx"), None),
            P(None, ("shard", "ctx")),
            P(None, "tp"),
            P(None, "tp"),
            P(None, "tp"),
            P(None, ("shard", "ctx"), None),
        ),
        check_vma=False,
    )
```
